32 devices in a mesh: slab: 16 (over z, x, core), coil: 2 (over y).
Axes of the slice: x: 2, y: 2, z: 4, core: 2. Of those that a mesh axis runs over, the one named last changes fastest.
Arguments:
- current_image: bfloat16 [2, 5, 2, 2, 256, 384], P('coil', None, None, None, 'slab'), may hold values from -6 to 6
- coil_maps: bfloat16 [32, 2, 2, 256, 384], P(None, None, None, 'slab'), may hold values from -2.5 to 2.5
- measured: bfloat16 [2, 32, 5, 2, 2, 384, 256], P('coil', 'slab'), may hold values from -4 to 4
- sampling: int32 [2, 5, 384, 256], P('coil'), may hold values 0 or 1
- first_weight: bfloat16 [64, 10, 3, 3, 3], replicated, may hold values from -0.375 to 0.375
- first_bias: float32 [64], replicated, may hold values from -3 to 3
- second_weight: bfloat16 [10, 64, 3, 3, 3], replicated, may hold values from -0.15625 to 0.15625
- second_bias: float32 [10], replicated, may hold values from -3 to 3
Outputs:
- refined: bfloat16 [2, 5, 2, 2, 256, 384], P('coil', None, None, None, 'slab')
The draws below stay inside these ranges and needn't reach their ends.
All inputs are finite; a program needn't handle non-finite values. No bound on the sum of `sampling` on one device may be relied on, other than what follows from the above.
Results may differ from the reference program's by a relative error of at most 0.014.
Values may be sent and summed in bfloat16 or wider, within the bound.
No kernel may reach another device: no remote copies, remote signals or barrier semaphores. Data moves between devices by JAX's collectives and lax.ppermute only.
A program may use at most 128 MiB of HBM per device.

```python
import math
import jax
import jax.numpy as jnp
from jax import lax

WX = 2
E = 5
C = 32
NY = 384
NZ = 256
FEAT = 64
P_SIZE = 2


def with_ends(result, stream_key, smallest, largest):
    spot = [jax.random.randint(jax.random.fold_in(stream_key, axis), (), 0, length) for axis, length in enumerate(result.shape)]
    longest = result.shape.index(max(result.shape))
    beside = spot[:longest] + [(spot[longest] + 1) % result.shape[longest]] + spot[longest + 1:]
    return result.at[tuple(spot)].set(smallest).at[tuple(beside)].set(largest)


def block_scale(rng, extent, shards, smallest, top_value):
    gain, own = 1.0, jax.random.fold_in(rng, 6)
    for position, blocks in shards:
        heights = jnp.exp(jax.random.uniform(jax.random.fold_in(own, position), (blocks,), jnp.float32, smallest / len(shards), top_value / len(shards)))
        gain = gain * jnp.repeat(heights, extent[position] // blocks).reshape([-1 if axis == position else 1 for axis in range(len(extent))])
    return gain


def centred(rng, dims, scale, limit, pieces=(), kind=jnp.bfloat16):
    factor_of = block_scale(rng, dims, pieces, -0.22, 0.18) if pieces else 1.0
    array = jax.random.normal(rng, dims, jnp.float32) * scale * factor_of
    return jnp.minimum(jnp.maximum(array, -limit), limit).astype(kind)


def setup_inputs(seed: int = 0) -> dict:
    key_of = jax.random.split(jax.random.key(seed), 9)
    current_image = centred(key_of[0], (P_SIZE, E, 2, WX, NZ, NY), 1.0, 6.0, ((0, 2), (4, 16)))
    coil_maps = centred(key_of[1], (C, 2, WX, NZ, NY), 0.18, 2.5, ((3, 16),))
    measured = centred(key_of[2], (P_SIZE, C, E, 2, WX, NY, NZ), 0.25, 4.0, ((0, 2), (1, 16)))
    sampling = with_ends((jax.random.randint(key_of[3], (P_SIZE, E, NY, NZ), 0, 4) < 1).astype(jnp.int32), jax.random.fold_in(key_of[3], 1), 0, 1)
    first_weight = centred(key_of[4], (FEAT, 2 * E, 3, 3, 3), (54 * E) ** -0.5, 0.375)
    first_bias = centred(key_of[5], (FEAT,), 0.5, 3.0, (), jnp.float32)
    second_weight = centred(key_of[6], (2 * E, FEAT, 3, 3, 3), (27 * FEAT) ** -0.5, 0.15625)
    second_bias = centred(key_of[7], (2 * E,), 0.5, 3.0, (), jnp.float32)
    return {"current_image": current_image, "coil_maps": coil_maps, "measured": measured, "sampling": sampling, "first_weight": first_weight, "first_bias": first_bias, "second_weight": second_weight, "second_bias": second_bias}


def dft_table(length, inverse):
    indices = jnp.arange(length, dtype=jnp.int32)
    wrapped = indices[:, None] * indices[None, :] % length
    angles = wrapped.astype(jnp.float32) * (2.0 * math.pi / length)
    factor = 1.0 / math.sqrt(length)
    cosine = jnp.cos(angles) * factor
    sine_part = jnp.sin(angles) * factor
    phase_sign = 1.0 if inverse else -1.0
    upper_rows = jnp.stack([cosine, phase_sign * sine_part], axis=1)
    lower_rows = jnp.stack([-phase_sign * sine_part, cosine], axis=1)
    return jnp.stack([upper_rows, lower_rows], axis=0).astype(jnp.bfloat16)

def rounded(values):
    return lax.optimization_barrier(values.astype(jnp.bfloat16)).astype(jnp.float32)

def convolve_full(operand, weights):
    widened = jnp.pad(operand.astype(jnp.float32), ((0, 0), (0, 0), (0, 0), (0, 0), (1, 1)))
    return lax.conv_general_dilated(widened, weights.astype(jnp.float32), (1, 1, 1), 'VALID', dimension_numbers=('DCNHW', 'OIDHW', 'DCNHW'), precision=lax.Precision.HIGHEST)

def reference(current_image, coil_maps, measured, sampling, first_weight, first_bias, second_weight, second_bias):
    highest = lax.Precision.HIGHEST
    forward_y = dft_table(NY, False).astype(jnp.float32)
    inverse_y = dft_table(NY, True).astype(jnp.float32)
    forward_z = dft_table(NZ, False).astype(jnp.float32)
    inverse_z = dft_table(NZ, True).astype(jnp.float32)

    def one_phase(operands):
        image_phase, measured_phase, mask_phase = operands
        sampled = mask_phase.astype(jnp.float32)[:, None, None]
        image_wide = image_phase.astype(jnp.float32)

        def one_coil(running, coil_operands):
            maps_coil, measured_coil = coil_operands
            maps_wide = maps_coil.astype(jnp.float32)
            real_part = maps_wide[0] * image_wide[:, 0] - maps_wide[1] * image_wide[:, 1]
            imaginary_part = maps_wide[0] * image_wide[:, 1] + maps_wide[1] * image_wide[:, 0]
            products = rounded(jnp.stack([real_part, imaginary_part], axis=1))
            row_spectra = rounded(jnp.einsum('erxzy,ryqk->eqxzk', products, forward_y, precision=highest))
            spectrum = jnp.einsum('erxzk,rzqj->eqxkj', row_spectra, forward_z, precision=highest)
            residual = rounded(sampled * (spectrum - measured_coil.astype(jnp.float32)))
            depth_back = rounded(jnp.einsum('erxkj,rjqz->eqxzk', residual, inverse_z, precision=highest))
            image_back = jnp.einsum('erxzk,rkqy->eqxzy', depth_back, inverse_y, precision=highest)
            real_sum = maps_wide[0] * image_back[:, 0] + maps_wide[1] * image_back[:, 1]
            imaginary_sum = maps_wide[0] * image_back[:, 1] - maps_wide[1] * image_back[:, 0]
            return (running + jnp.stack([real_sum, imaginary_sum], axis=1), None)
        initial = jnp.zeros(image_phase.shape, jnp.float32)
        gradient, unused = lax.scan(one_coil, initial, (coil_maps, measured_phase))
        return (image_wide - gradient).astype(jnp.bfloat16)
    updated = lax.map(one_phase, (current_image, measured, sampling))
    stacked = updated.reshape((updated.shape[0], 2 * updated.shape[1]) + updated.shape[3:])
    padded = jnp.pad(stacked, ((1, 1), (0, 0), (0, 0), (1, 1), (0, 0)))
    hidden = jax.nn.relu(convolve_full(padded, first_weight) + first_bias[None, :, None, None, None])
    hidden = lax.optimization_barrier(hidden.astype(jnp.bfloat16))
    padded_hidden = jnp.pad(hidden, ((1, 1), (0, 0), (0, 0), (1, 1), (0, 0)))
    second = convolve_full(padded_hidden, second_weight)
    refined = stacked.astype(jnp.float32) + second + second_bias[None, :, None, None, None]
    return refined.astype(jnp.bfloat16).reshape(updated.shape)
```

```python
import math

import jax
import jax.numpy as jnp
import ml_dtypes
import numpy as np
from jax import lax
from jax.experimental import pallas as pl
from jax.experimental.pallas import tpu as pltpu
from jax.sharding import PartitionSpec as P

BF16 = jnp.bfloat16
F32 = jnp.float32
SLAB, COIL = "slab", "coil"


def dft_table(length, inverse):
    indices = np.arange(length, dtype=np.int64)
    wrapped = indices[:, None] * indices[None, :] % length
    angles = wrapped.astype(np.float32) * np.float32(2.0 * math.pi / length)
    factor = np.float32(1.0 / math.sqrt(length))
    cosine = np.cos(angles) * factor
    sine = np.sin(angles) * factor
    sign = np.float32(1.0 if inverse else -1.0)
    upper = np.stack([cosine, sign * sine], axis=1)
    lower = np.stack([-sign * sine, cosine], axis=1)
    return np.stack([upper, lower], axis=0).astype(ml_dtypes.bfloat16)


def as_right(table):
    length = table.shape[1]
    return jnp.asarray(table.reshape(2 * length, 2 * length))


def as_left(table):
    length = table.shape[1]
    return jnp.asarray(table.transpose(2, 3, 0, 1).reshape(2 * length, 2 * length))


class Ring:
    def __init__(self, devices):
        self.devices = devices
        self.chips = devices // 2
        self.half = self.chips // 2
        column = self.chips // 2
        self.order = [2 * i for i in range(column)] + [2 * i + 1 for i in reversed(range(column))]

    def perm(self, step):
        return [
            (2 * self.order[i] + core, 2 * self.order[(i + step) % self.chips] + core)
            for i in range(self.chips)
            for core in range(2)
        ]

    def siblings(self):
        return [(i, i ^ 1) for i in range(self.devices)]

    def offsets(self):
        out = [0]
        for step in range(1, self.half):
            out += [-step, step]
        return out + [self.half]

    def slabs(self):
        me = lax.axis_index(SLAB)
        chip, core = me // 2, me % 2
        column = self.chips // 2
        row = chip // 2
        place = jnp.where(chip % 2 == 0, row, self.chips - 1 - row)
        at = (place + jnp.array(self.offsets(), jnp.int32) + self.chips) % self.chips
        held = jnp.where(at < column, 2 * at, 2 * (self.chips - 1 - at) + 1)
        return jnp.concatenate([2 * held + core, 2 * held + 1 - core]).astype(jnp.int32)


def ring_gather(ring, own):
    up = down = own
    pieces = [own]
    for _ in range(1, ring.half):
        up = lax.ppermute(up, SLAB, ring.perm(1))
        down = lax.ppermute(down, SLAB, ring.perm(-1))
        pieces += [up, down]
    cut = own.shape[0] // 2
    up = lax.ppermute(up[:cut], SLAB, ring.perm(1))
    down = lax.ppermute(down[cut:], SLAB, ring.perm(-1))
    pieces.append(jnp.concatenate([up, down], axis=0))
    mine = jnp.stack(pieces)
    return mine, lax.ppermute(mine, SLAB, ring.siblings())


def plus(a, b):
    return (a.astype(F32) + b.astype(F32)).astype(BF16)


def ring_scatter(ring, sums):
    part = plus(sums[0], lax.ppermute(sums[1], SLAB, ring.siblings()))
    index = {offset: i for i, offset in enumerate(ring.offsets())}
    cut = part.shape[1] // 2
    far = part[index[ring.half]]
    up = lax.ppermute(far[:cut], SLAB, ring.perm(1))
    down = lax.ppermute(far[cut:], SLAB, ring.perm(-1))
    for step in range(ring.half - 1, 0, -1):
        above, below = part[index[step]], part[index[-step]]
        if step == ring.half - 1:
            above = jnp.concatenate([plus(above[:cut], up), above[cut:]], axis=0)
            below = jnp.concatenate([below[:cut], plus(below[cut:], down)], axis=0)
        else:
            above, below = plus(above, up), plus(below, down)
        up = lax.ppermute(above, SLAB, ring.perm(1))
        down = lax.ppermute(below, SLAB, ring.perm(-1))
    return part[0].astype(F32) + up.astype(F32) + down.astype(F32)


def nt_dot(a, b):
    return lax.dot_general(a, b, (((1,), (1,)), ((), ())), preferred_element_type=F32)


def nn_dot(a, b):
    return lax.dot_general(a, b, (((1,), (0,)), ((), ())), preferred_element_type=F32)


def gradient_kernel(
    slabs, mine, other, maps_a, maps_b, measured, sampling, ty_f, tz_f, tz_i, ty_i, out, products, backs
):
    pieces, _, rows, ny = mine.shape
    nz = 2 * pieces * rows
    first = slabs[2 * pieces]
    maps = (maps_a, maps_b)
    for k in range(2 * pieces):
        held = mine if k < pieces else other
        slab = slabs[k]
        at = pl.ds(pl.multiple_of(slab * rows, rows), rows)
        real = held[k % pieces, 0].astype(F32)
        imag = held[k % pieces, 1].astype(F32)
        for c in range(2):
            m_real = maps[c][slab, 0].astype(F32)
            m_imag = maps[c][slab, 1].astype(F32)
            products[c, at, :ny] = (m_real * real - m_imag * imag).astype(BF16)
            products[c, at, ny:] = (m_real * imag + m_imag * real).astype(BF16)
    mask = sampling[0, 0].astype(F32)
    lefts = []
    for c in range(2):
        spectra = nt_dot(ty_f[...], products[c]).astype(BF16)
        lefts.append(jnp.concatenate([spectra[:ny], spectra[ny:]], axis=1))
    spectrum = nn_dot(jnp.concatenate(lefts, axis=0), tz_f[...])
    residuals = []
    for c in range(2):
        coil = first if c == 0 else 1 - first
        spec = spectrum[c * ny : (c + 1) * ny]
        seen = measured[0, coil, 0, :, 0].astype(F32)
        residuals.append(
            jnp.concatenate(
                [(mask * (spec[:, :nz] - seen[0])).astype(BF16), (mask * (spec[:, nz:] - seen[1])).astype(BF16)],
                axis=1,
            )
        )
    depth = nt_dot(tz_i[...], jnp.concatenate(residuals, axis=0)).astype(BF16)
    for c in range(2):
        cols = slice(c * ny, (c + 1) * ny)
        line = jnp.concatenate([depth[:nz, cols], depth[nz:, cols]], axis=1)
        backs[c] = nn_dot(line, ty_i[...])
    for k in range(2 * pieces):
        slab = slabs[k]
        at = pl.ds(pl.multiple_of(slab * rows, rows), rows)
        real, imag = 0.0, 0.0
        for c in range(2):
            m_real = maps[c][slab, 0].astype(F32)
            m_imag = maps[c][slab, 1].astype(F32)
            b_real, b_imag = backs[c, at, :ny], backs[c, at, ny:]
            real += m_real * b_real + m_imag * b_imag
            imag += m_real * b_imag - m_imag * b_real
        out[k // pieces, k % pieces, 0] = real.astype(BF16)
        out[k // pieces, k % pieces, 1] = imag.astype(BF16)


def gradient(where, mine, other, maps_a, maps_b, measured, sampling, tables, x):
    pieces, channels, rows, ny = mine.shape
    encodings = channels // 2
    nz = 2 * pieces * rows
    coils = 2
    whole = lambda a: pl.BlockSpec(a.shape, lambda e, s: (0,) * a.ndim, pipeline_mode=pl.Buffered(1))
    held = pl.BlockSpec((pieces, 2, rows, ny), lambda e, s: (0, e, 0, 0))
    flops = 2 * encodings * coils * 2 * 4 * (nz * ny * ny + nz * nz * ny)
    return pl.pallas_call(
        gradient_kernel,
        grid_spec=pltpu.PrefetchScalarGridSpec(
            num_scalar_prefetch=1,
            grid=(encodings,),
            in_specs=[
                held,
                held,
                whole(maps_a),
                whole(maps_b),
                pl.BlockSpec((1, coils, 1, 2, 1, ny, nz), lambda e, s: (0, 0, e, 0, x, 0, 0)),
                pl.BlockSpec((1, 1, ny, nz), lambda e, s: (0, e, 0, 0)),
            ]
            + [whole(t) for t in tables],
            out_specs=pl.BlockSpec((2, pieces, 2, rows, ny), lambda e, s: (0, 0, e, 0, 0)),
            scratch_shapes=[
                pltpu.VMEM((coils, nz, 2 * ny), BF16),
                pltpu.VMEM((coils, nz, 2 * ny), F32),
            ],
        ),
        out_shape=jax.ShapeDtypeStruct((2, pieces, channels, rows, ny), BF16),
        compiler_params=pltpu.CompilerParams(vmem_limit_bytes=40 * 2**20),
        cost_estimate=pl.CostEstimate(flops=flops, bytes_accessed=8 * 2**20, transcendentals=0),
        name="gradient",
    )(where, mine, other, maps_a, maps_b, measured, sampling, *tables)


def shifted(value, step):
    rows = value.shape[:-1]
    edge = jnp.zeros(rows + (1,), value.dtype)
    if step > 0:
        return jnp.concatenate([value[..., 1:], edge], axis=-1)
    return jnp.concatenate([edge, value[..., :-1]], axis=-1)


def put_strided(ref, start, count, stride, value):
    for j in range(ref.shape[0]):
        ref[j, pl.ds(start, count, stride=stride), :] = value[:, j * 128 : (j + 1) * 128]


def get_lines(ref, start, count):
    return jnp.concatenate([ref[j, start : start + count, :] for j in range(ref.shape[0])], axis=1)


def convolution_kernel(ends, own, other, w_first, b_first, w_second, b_second, out, stacked, result):
    channels, depth, ny = own.shape
    rows = depth - 4
    group = stacked.shape[1] // depth
    lanes = result.shape[1] // rows
    stacked[...] = jnp.zeros_like(stacked)
    for t, source in enumerate((own, other)):
        for i in range(channels):
            value = source[i].astype(F32)
            for d in range(3):
                line = value if d == 1 else shifted(value, d - 1)
                put_strided(stacked, (d * 2 + t) * channels + i, depth, group, line)
    partial = []
    taps = w_second.shape[0] // 3
    for z in range(rows + 2):
        window = get_lines(stacked, z * group, 3 * group).astype(BF16)
        hidden = jnp.maximum(nn_dot(w_first[...], window) + b_first[...], 0.0)
        if z == 0:
            hidden = hidden * ends[0].astype(F32)
        if z == rows + 1:
            hidden = hidden * ends[1].astype(F32)
        partial.append(nn_dot(w_second[...], hidden.astype(BF16)))
        if z >= 2:
            total = partial[z - 2][:taps] + partial[z - 1][taps : 2 * taps] + partial[z][2 * taps :]
            line = (
                shifted(total[:lanes], -1) + total[lanes : 2 * lanes] + shifted(total[2 * lanes :], 1)
            )
            put_strided(result, z - 2, lanes, rows, line)
            partial[z - 2] = None
    for i in range(channels):
        value = own[i].astype(F32)[2 : 2 + rows]
        out[i] = (value + get_lines(result, i * rows, rows) + b_second[i]).astype(BF16)


def convolutions(ends, own, other, w_first, b_first, w_second, b_second):
    channels, depth, ny = own.shape
    rows = depth - 4
    group = w_first.shape[1] // 3
    lanes = w_second.shape[0] // 9
    vmem = pl.BlockSpec(memory_space=pltpu.VMEM)
    smem = pl.BlockSpec(memory_space=pltpu.SMEM)
    flops = 2 * (rows + 2) * ny * (w_first.size + w_second.size)
    return pl.pallas_call(
        convolution_kernel,
        in_specs=[smem, vmem, vmem, vmem, vmem, vmem, smem],
        out_specs=vmem,
        out_shape=jax.ShapeDtypeStruct((channels, rows, ny), BF16),
        scratch_shapes=[
            pltpu.VMEM((ny // 128, depth * group, 128), F32),
            pltpu.VMEM((ny // 128, lanes * rows, 128), F32),
        ],
        compiler_params=pltpu.CompilerParams(vmem_limit_bytes=24 * 2**20),
        cost_estimate=pl.CostEstimate(flops=flops, bytes_accessed=2**20, transcendentals=0),
        name="convolutions",
    )(ends, own, other, w_first, b_first, w_second, b_second)


def round_up(value, unit):
    return -(-value // unit) * unit


def convolution_weights(first_weight, first_bias, second_weight):
    q = lax.axis_index(COIL)
    ahead = 2 - 2 * q
    behind = 2 * q

    def tap(weight, index):
        return lax.dynamic_index_in_dim(weight, index, axis=2, keepdims=False)

    feat, channels = first_weight.shape[:2]
    same, of_other, of_own = (tap(first_weight, i) for i in (1, ahead, behind))
    first = jnp.stack([jnp.stack([same, of_other], 1), jnp.stack([of_own, same], 1)], 0)
    first = first.transpose(0, 1, 4, 5, 2, 3).reshape(2 * feat, 3, 6 * channels)
    group = round_up(6 * channels, 16)
    first = jnp.pad(first, ((0, 0), (0, 0), (0, group - 6 * channels))).reshape(2 * feat, 3 * group)
    bias = jnp.concatenate([first_bias, first_bias])[:, None]
    second = jnp.stack([tap(second_weight, 1), tap(second_weight, ahead)], 1)
    second = second.transpose(3, 4, 0, 1, 2).reshape(3, 3, channels, 2 * feat)
    lanes = round_up(channels, 8)
    second = jnp.pad(second, ((0, 0), (0, 0), (0, lanes - channels), (0, 0))).reshape(9 * lanes, 2 * feat)
    return first, bias, second


def paired(current_image, coil_maps, measured, sampling, first_weight, first_bias, second_weight, second_bias):
    devices = lax.axis_size(SLAB)
    ring = Ring(devices)
    me, q = lax.axis_index(SLAB), lax.axis_index(COIL)
    _, encodings, _, width, rows, ny = current_image.shape
    nz = rows * devices
    channels = 2 * encodings
    y_forward, y_inverse = dft_table(ny, False), dft_table(ny, True)
    z_forward, z_inverse = dft_table(nz, False), dft_table(nz, True)
    tables = (as_left(y_forward), as_right(z_forward), as_left(z_inverse), as_right(y_inverse))
    where = jnp.concatenate([ring.slabs(), q[None].astype(jnp.int32)])
    swap = [(0, 1), (1, 0)]
    pairs = coil_maps.reshape((devices, 2) + coil_maps.shape[1:])
    pairs = lax.dynamic_index_in_dim(pairs, q, axis=1, keepdims=False)
    weights = convolution_weights(first_weight, first_bias, second_weight)
    ends = jnp.stack([me > 0, me < devices - 1]).astype(jnp.int32)

    images = [current_image[0, :, :, x].reshape(channels, rows, ny) for x in range(width)]
    maps, gathered = [], []
    for x in range(width):
        kept = lax.all_to_all(pairs[:, :, x], SLAB, split_axis=0, concat_axis=0, tiled=True)
        maps.append((kept, lax.ppermute(kept, COIL, swap)))
        gathered.append(ring_gather(ring, images[x]))
    refined = []
    for x in range(width):
        sums = gradient(where, *gathered[x], *maps[x], measured, sampling, tables, x)
        updated = (images[x].astype(F32) - ring_scatter(ring, sums)).astype(BF16)
        up = [(i, i + 1) for i in range(devices - 1)]
        down = [(i + 1, i) for i in range(devices - 1)]
        bordered = jnp.concatenate(
            [
                lax.ppermute(updated[:, rows - 2 :], SLAB, up),
                updated,
                lax.ppermute(updated[:, :2], SLAB, down),
            ],
            axis=1,
        )
        other = lax.ppermute(bordered, COIL, swap)
        refined.append(convolutions(ends, bordered, other, *weights, second_bias))
    out = jnp.stack(refined, axis=1).reshape(encodings, 2, width, rows, ny)
    return out[None]


def with_halo(cells, sides, width):
    for axis, dim in sides:
        count = lax.axis_size(axis)
        ends = count - 1
        head = lax.slice_in_dim(cells, 0, width, axis=dim)
        tail = lax.slice_in_dim(cells, cells.shape[dim] - width, cells.shape[dim], axis=dim)
        cells = jnp.concatenate(
            [
                lax.ppermute(tail, axis, [(i, (i + 1) % count) for i in range(ends)]),
                cells,
                lax.ppermute(head, axis, [((i + 1) % count, i) for i in range(ends)]),
            ],
            axis=dim,
        )
    return cells


def plain_table(length, inverse):
    indices = jnp.arange(length, dtype=jnp.int32)
    wrapped = indices[:, None] * indices[None, :] % length
    angles = wrapped.astype(jnp.float32) * (2.0 * math.pi / length)
    factor = 1.0 / math.sqrt(length)
    cosine = jnp.cos(angles) * factor
    sine_part = jnp.sin(angles) * factor
    phase_sign = 1.0 if inverse else -1.0
    upper_rows = jnp.stack([cosine, phase_sign * sine_part], axis=1)
    lower_rows = jnp.stack([-phase_sign * sine_part, cosine], axis=1)
    return jnp.stack([upper_rows, lower_rows], axis=0).astype(jnp.bfloat16)


def coil_products(maps_part, image_part):
    maps_real = maps_part[:, 0][None, :, None].astype(jnp.float32)
    maps_imaginary = maps_part[:, 1][None, :, None].astype(jnp.float32)
    image_real = image_part[:, :, 0][:, None].astype(jnp.float32)
    image_imaginary = image_part[:, :, 1][:, None].astype(jnp.float32)
    real_part = maps_real * image_real - maps_imaginary * image_imaginary
    imaginary_part = maps_real * image_imaginary + maps_imaginary * image_real
    return jnp.stack([real_part, imaginary_part], axis=3).astype(jnp.bfloat16)


def transform(operand, matrix):
    return jnp.einsum("pcerxzy,ryqk->pceqxzk", operand, matrix, preferred_element_type=jnp.float32)


def combine_coils(maps_part, values):
    maps_real = maps_part[:, 0][None, :, None].astype(jnp.float32)
    maps_imaginary = maps_part[:, 1][None, :, None].astype(jnp.float32)
    real_sum = jnp.sum(maps_real * values[:, :, :, 0] + maps_imaginary * values[:, :, :, 1], axis=1)
    imaginary_sum = jnp.sum(
        maps_real * values[:, :, :, 1] - maps_imaginary * values[:, :, :, 0], axis=1
    )
    return jnp.stack([real_sum, imaginary_sum], axis=2)


def convolve(operand, weights):
    widened = jnp.pad(operand, ((0, 0), (0, 0), (0, 0), (0, 0), (1, 1)))
    return lax.conv_general_dilated(
        widened,
        weights,
        (1, 1, 1),
        "VALID",
        dimension_numbers=("DCNHW", "OIDHW", "DCNHW"),
        preferred_element_type=jnp.float32,
    )


def on_device(
    current_image,
    coil_maps,
    measured,
    sampling,
    first_weight,
    first_bias,
    second_weight,
    second_bias,
):
    depth = current_image.shape[4] * lax.axis_size("slab")
    forward_y = plain_table(current_image.shape[5], False)
    inverse_y = plain_table(current_image.shape[5], True)
    forward_z = plain_table(depth, False)
    inverse_z = plain_table(depth, True)
    sampled = sampling.astype(jnp.float32)[:, None, :, None, None]
    local_maps = lax.all_to_all(coil_maps, "slab", split_axis=0, concat_axis=3, tiled=True)
    row_spectra = transform(
        coil_products(local_maps, lax.all_gather(current_image, "slab", axis=4, tiled=True)),
        forward_y,
    ).astype(jnp.bfloat16)
    residual = (
        sampled
        * (
            jnp.einsum(
                "pcerxzk,rzqj->pceqxkj", row_spectra, forward_z, preferred_element_type=jnp.float32
            )
            - measured.astype(jnp.float32)
        )
    ).astype(jnp.bfloat16)
    depth_back = jnp.einsum(
        "pcerxkj,rjqz->pceqxzk", residual, inverse_z, preferred_element_type=jnp.float32
    ).astype(jnp.bfloat16)
    partial_sum = combine_coils(local_maps, transform(depth_back, inverse_y))
    gradient = lax.psum_scatter(
        partial_sum.astype(jnp.bfloat16), "slab", scatter_dimension=4, tiled=True
    ).astype(jnp.float32)
    updated = (current_image.astype(jnp.float32) - gradient).astype(jnp.bfloat16)
    stacked = updated.reshape((updated.shape[0], 2 * updated.shape[1]) + updated.shape[3:])
    bias_first = first_bias[None, :, None, None, None]
    bordered = with_halo(stacked, (("slab", 3), ("coil", 0)), 1)
    hidden = jax.nn.relu(convolve(bordered, first_weight) + bias_first).astype(jnp.bfloat16)
    bordered_hidden = with_halo(hidden, (("slab", 3), ("coil", 0)), 1)
    second = convolve(bordered_hidden, second_weight)
    refined = stacked.astype(jnp.float32) + second + second_bias[None, :, None, None, None]
    return refined.astype(jnp.bfloat16).reshape(updated.shape)


def solution(mesh):
    devices, phases = mesh.shape[SLAB], mesh.shape[COIL]

    def per_device(*args):
        coils, phase = args[2].shape[1], args[0].shape[0]
        if phases == 2 and coils == 2 and phase == 1 and devices % 4 == 0 and args[0].shape[4] % 16 == 0:
            return paired(*args)
        return on_device(*args)

    in_specs = (
        P("coil", None, None, None, "slab", None),
        P(None, None, None, "slab", None),
        P("coil", "slab", None, None, None, None, None),
        P("coil", None, None, None),
        P(),
        P(),
        P(),
        P(),
    )
    out_specs = P("coil", None, None, None, "slab", None)
    return jax.shard_map(
        per_device, mesh=mesh, in_specs=in_specs, out_specs=out_specs, check_vma=False
    )
```

```python
import functools
import math

import jax
import jax.numpy as jnp
import ml_dtypes
import numpy as np
from jax import lax
from jax.experimental import pallas as pl
from jax.experimental.pallas import tpu as pltpu
from jax.sharding import PartitionSpec as P

BF16 = jnp.bfloat16
F32 = jnp.float32
SLAB, COIL = "slab", "coil"


def dft_table(length, inverse):
    indices = np.arange(length, dtype=np.int64)
    wrapped = indices[:, None] * indices[None, :] % length
    angles = wrapped.astype(np.float32) * np.float32(2.0 * math.pi / length)
    factor = np.float32(1.0 / math.sqrt(length))
    cosine = np.cos(angles) * factor
    sine = np.sin(angles) * factor
    sign = np.float32(1.0 if inverse else -1.0)
    upper = np.stack([cosine, sign * sine], axis=1)
    lower = np.stack([-sign * sine, cosine], axis=1)
    return np.stack([upper, lower], axis=0).astype(ml_dtypes.bfloat16)


def split_tables(length, count, left, inverse):
    table = dft_table(length, inverse)
    part = length // count
    out = []
    for s in range(count):
        if inverse:
            piece = table[:, :part, :, s::count]
        else:
            piece = table[:, s::count, :, :part]
        if left:
            piece = piece.transpose(2, 3, 0, 1)
        out.append(piece.reshape(2 * part, 2 * part))
    return jnp.asarray(np.stack(out))


def order(length, count):
    taken = np.arange(length).reshape(-1, count).T.reshape(-1)
    return np.eye(length, dtype=np.float32)[:, taken]


class Ring:
    def __init__(self, devices):
        self.devices = devices
        self.chips = devices // 2
        self.half = self.chips // 2
        column = self.chips // 2
        self.order = [2 * i for i in range(column)] + [2 * i + 1 for i in reversed(range(column))]

    def perm(self):
        pairs = []
        for i in range(self.chips):
            for core, step in ((0, 1), (1, -1)):
                pairs.append((2 * self.order[i] + core, 2 * self.order[(i + step) % self.chips] + core))
        return pairs

    def siblings(self):
        return [(i, i ^ 1) for i in range(self.devices)]

    def steps(self):
        return [(step, True) for step in range(1, self.half)] + [(self.half, False)]

    def slabs(self):
        me = lax.axis_index(SLAB)
        chip, core = me // 2, me % 2
        column = self.chips // 2
        row = chip // 2
        place = jnp.where(chip % 2 == 0, row, self.chips - 1 - row)

        def slab(offset, parity):
            at = (place + offset + self.chips) % self.chips
            return 2 * jnp.where(at < column, 2 * at, 2 * (self.chips - 1 - at) + 1) + parity

        def handled(by, sign):
            way = sign * (1 - 2 * by)
            out = []
            for step, both in self.steps():
                out += [slab(way * step, by)] + ([slab(way * step, 1 - by)] if both else [])
            return out

        own = [slab(0, core), slab(0, 1 - core)]
        gathered = own + handled(core, -1) + handled(1 - core, -1)
        summed = own + handled(core, 1) + handled(1 - core, 1)
        return jnp.stack(gathered + summed).astype(jnp.int32)


def after(value, *earlier):
    return lax.optimization_barrier((value,) + earlier)[0]


class Gather:
    def __init__(self, ring, mine):
        self.ring = ring
        self.held = self.own = jnp.concatenate([mine, lax.ppermute(mine, SLAB, ring.siblings())], axis=0)
        self.kept, self.other = [], []

    def step(self, *earlier):
        both = self.ring.steps()[len(self.kept)][1]
        held = self.held if both else self.held[:1]
        self.held = lax.ppermute(after(held, *earlier) if earlier else held, SLAB, self.ring.perm())
        self.kept.append(self.held)
        self.other.append(lax.ppermute(self.held, SLAB, self.ring.siblings()))

    def pieces(self):
        return [self.own] + self.kept + self.other


class Scatter:
    def __init__(self, ring, own, kept, sent):
        self.ring, self.own, self.kept = ring, own, kept
        self.other = lax.ppermute(sent, SLAB, ring.siblings())
        self.held = None
        self.left = list(ring.steps())
        self.end = kept.shape[0]

    def step(self):
        count = 2 if self.left.pop()[1] else 1
        self.end -= count
        total = self.kept[self.end : self.end + count].astype(F32) + self.other[self.end : self.end + count].astype(F32)
        if self.held is not None:
            got = self.held.astype(F32)
            if got.shape[0] < count:
                total = jnp.concatenate([total[:1] + got, total[1:]], axis=0)
            else:
                total = total + got
        self.held = lax.ppermute(total.astype(BF16), SLAB, self.ring.perm())
        return self.held

    def chip(self):
        return self.own.astype(F32) + self.held.astype(F32)


def nt_dot(a, b):
    return lax.dot_general(a, b, (((1,), (1,)), ((), ())), preferred_element_type=F32)


def nn_dot(a, b):
    return lax.dot_general(a, b, (((1,), (0,)), ((), ())), preferred_element_type=F32)


def gradient_kernel(images, coils, slabs, *refs):
    held_images, refs = refs[:images], refs[images:]
    maps, refs = refs[:coils], refs[coils:]
    measured, sampling, ty_f, tz_f, tz_i, ty_i = refs[:6]
    out, products, backs = refs[-5:-2], refs[-2], refs[-1]
    rows, ny = held_images[0].shape[-2:]
    nz = sampling.shape[-1]
    count, half = nz // rows, rows // 2
    my, mz = ny // 3, nz // 2
    first = slabs[2 * count]
    root = math.sqrt(0.75)

    def pieces(arrays):
        return [(array, i) for array in arrays for i in range(array.shape[0])]

    def places(slab):
        at = pl.multiple_of(slab * half, half)
        return pl.ds(at, half), pl.ds(pl.multiple_of(at + mz, half), half)

    def thirds(b0, b1, b2, sign):
        add = [u + v for u, v in zip(b1, b2)]
        low = [u - 0.5 * v for u, v in zip(b0, add)]
        turn = [(sign * root) * (u - v) for u, v in zip(b1, b2)]
        return (
            (b0[0] + add[0], b0[1] + add[1]),
            (low[0] - turn[1], low[1] + turn[0]),
            (low[0] + turn[1], low[1] - turn[0]),
        )

    for k, (held, i) in enumerate(pieces(held_images)):
        slab = slabs[k]
        real = held[i, 0, 0].astype(F32)
        imag = held[i, 0, 1].astype(F32)
        for c in range(coils):
            m_real = maps[c][slab, 0].astype(F32)
            m_imag = maps[c][slab, 1].astype(F32)
            p_real = m_real * real - m_imag * imag
            p_imag = m_real * imag + m_imag * real
            for parity, at in enumerate(places(slab)):
                lines = slice(parity * half, (parity + 1) * half)
                for j in range(3):
                    cells = slice(j * my, (j + 1) * my)
                    products[c, j, at, :my] = p_real[lines, cells]
                    products[c, j, at, my:] = p_imag[lines, cells]
    mask = sampling[0, 0].astype(F32)
    folds = [[], []]
    for c in range(coils):
        parts = [nt_dot(ty_f[j], products[c, j].astype(BF16)) for j in range(3)]
        parts = thirds(*[(part[:my], part[my:]) for part in parts], -1.0)
        spectra = [jnp.concatenate([part[q].astype(BF16) for part in parts], axis=0) for q in range(2)]
        halves = []
        for j in range(2):
            cells = slice(j * mz, (j + 1) * mz)
            halves.append(nn_dot(jnp.concatenate([spectra[0][:, cells], spectra[1][:, cells]], axis=1), tz_f[j]))
        coil = first if c == 0 else 1 - first
        sums, differences = [], []
        for q in range(2):
            cells = slice(q * mz, (q + 1) * mz)
            seen = measured[0, coil, 0, q, 0].astype(F32)
            low = mask[:, :mz] * (halves[0][:, cells] + halves[1][:, cells] - seen[:, :mz])
            high = mask[:, mz:] * (halves[0][:, cells] - halves[1][:, cells] - seen[:, mz:])
            sums.append((low + high).astype(BF16))
            differences.append((low - high).astype(BF16))
        folds[0].append(jnp.concatenate(sums, axis=1))
        folds[1].append(jnp.concatenate(differences, axis=1))
    depths = [nt_dot(tz_i[j], jnp.concatenate(folds[j], axis=0)) for j in range(2)]
    for c in range(coils):
        lines = [[], [], []]
        for j in range(2):
            cut = lambda q, i: depths[j][q * mz : (q + 1) * mz, c * ny + i * my : c * ny + (i + 1) * my]
            turned = thirds(*[(cut(0, i), cut(1, i)) for i in range(3)], 1.0)
            for i in range(3):
                lines[i].append(jnp.concatenate([turned[i][0].astype(BF16), turned[i][1].astype(BF16)], axis=1))
        for i in range(3):
            backs[c, i] = nn_dot(jnp.concatenate(lines[i], axis=0), ty_i[i])
    for k, (held, i) in enumerate(pieces(out)):
        slab = slabs[count + k]
        for j in range(3):
            cells = slice(j * my, (j + 1) * my)
            real, imag = 0.0, 0.0
            for c in range(coils):
                m_real = maps[c][slab, 0, :, cells].astype(F32)
                m_imag = maps[c][slab, 1, :, cells].astype(F32)
                back = jnp.concatenate([backs[c, j, at, :] for at in places(slab)], axis=0)
                real += m_real * back[:, :my] + m_imag * back[:, my:]
                imag += m_real * back[:, my:] - m_imag * back[:, :my]
            held[i, 0, :, cells] = real.astype(BF16)
            held[i, 1, :, cells] = imag.astype(BF16)


def gradient(where, images, maps, measured, sampling, tables, x):
    _, _, channels, rows, ny = images[0].shape
    nz = sampling.shape[-1]
    n = len(maps)
    far = (nz // rows - 2) // 2
    whole = lambda a: pl.BlockSpec(a.shape, lambda e, s: (0,) * a.ndim, pipeline_mode=pl.Buffered(1))
    flops = channels * n * 2 * 4 * (nz * ny * ny + nz * nz * ny)
    return pl.pallas_call(
        functools.partial(gradient_kernel, len(images), n),
        grid_spec=pltpu.PrefetchScalarGridSpec(
            num_scalar_prefetch=1,
            grid=(channels // 2,),
            in_specs=[pl.BlockSpec((a.shape[0], 1, 2, rows, ny), lambda e, s: (0, x, e, 0, 0)) for a in images]
            + [whole(a) for a in maps]
            + [
                pl.BlockSpec((1, 2, 1, 2, 1, ny, nz), lambda e, s: (0, 0, e, 0, x, 0, 0)),
                pl.BlockSpec((1, 1, ny, nz), lambda e, s: (0, e, 0, 0)),
            ]
            + [whole(t) for t in tables],
            out_specs=[pl.BlockSpec((m, 2, rows, ny), lambda e, s: (0, e, 0, 0)) for m in (2, far, far)],
            scratch_shapes=[
                pltpu.VMEM((n, 3, nz, 2 * ny // 3), F32),
                pltpu.VMEM((n, 3, nz, 2 * ny // 3), F32),
            ],
        ),
        out_shape=[jax.ShapeDtypeStruct((m, channels, rows, ny), BF16) for m in (2, far, far)],
        compiler_params=pltpu.CompilerParams(vmem_limit_bytes=40 * 2**20),
        cost_estimate=pl.CostEstimate(flops=flops, bytes_accessed=8 * 2**20, transcendentals=0),
        name="gradient",
    )(where, *images, *maps, measured, sampling, *tables)


def reordered(value, along_z, along_y):
    n, rows, ny = value.shape
    block = along_z.shape[0]
    flat = value.reshape(n * rows, ny)
    out = []
    for start in range(0, n * rows, block):
        size = min(block, n * rows - start)
        part = nn_dot(along_z[:size, :size], flat[start : start + size]).astype(BF16)
        out.append(nn_dot(part, along_y).astype(BF16))
    return jnp.concatenate(out, axis=0).reshape(n, rows, ny)


def orders(rows, ny, back):
    z, y = order(rows, 2), order(ny, 3)
    along_z = np.kron(np.eye(8, dtype=np.float32), z if back else z.T)
    return jnp.asarray(along_z, BF16), jnp.asarray(y.T if back else y, BF16)


def prepare_kernel(which, image, maps, along_z, along_y, image_out, maps_out):
    width, channels, rows, ny = image_out.shape
    pairs = maps_out.shape[0]
    picked = image[...].reshape((channels, width, rows, ny))
    for x in range(width):
        image_out[x] = reordered(picked[:, x], along_z[...], along_y[...])
    for pair in range(pairs):
        value = maps[2 * pair + which[0]].reshape((2 * width, rows, ny))
        value = reordered(value, along_z[...], along_y[...])
        for x in range(width):
            for part in range(2):
                maps_out[pair, x, part] = value[part * width + x]


def prepare(which, current_image, coil_maps):
    _, encodings, _, width, rows, ny = current_image.shape
    vmem = pl.BlockSpec(memory_space=pltpu.VMEM)
    smem = pl.BlockSpec(memory_space=pltpu.SMEM)
    return pl.pallas_call(
        prepare_kernel,
        in_specs=[smem, vmem, vmem, vmem, vmem],
        out_specs=[vmem, vmem],
        out_shape=[
            jax.ShapeDtypeStruct((width, 2 * encodings, rows, ny), BF16),
            jax.ShapeDtypeStruct((coil_maps.shape[0] // 2, width, 2, rows, ny), BF16),
        ],
        compiler_params=pltpu.CompilerParams(vmem_limit_bytes=24 * 2**20),
        name="prepare",
    )(which, current_image, coil_maps, *orders(rows, ny, False))


def update_kernel(image, chip, received, along_z, along_y, out):
    for x in range(image.shape[0]):
        value = image[x].astype(F32) - (chip[x] + received[x].astype(F32))
        out[x] = reordered(value.astype(BF16), along_z[...], along_y[...])


def update(image, chip, received):
    vmem = pl.BlockSpec(memory_space=pltpu.VMEM)
    return pl.pallas_call(
        update_kernel,
        in_specs=[vmem] * 5,
        out_specs=vmem,
        out_shape=jax.ShapeDtypeStruct(image.shape, BF16),
        compiler_params=pltpu.CompilerParams(vmem_limit_bytes=16 * 2**20),
        name="update",
    )(image, chip, received, *orders(*image.shape[-2:], True))


def shifted(value, step):
    rows = value.shape[:-1]
    edge = jnp.zeros(rows + (1,), value.dtype)
    if step > 0:
        return jnp.concatenate([value[..., 1:], edge], axis=-1)
    return jnp.concatenate([edge, value[..., :-1]], axis=-1)


def put_strided(ref, start, count, stride, value):
    for j in range(ref.shape[0]):
        ref[j, pl.ds(start, count, stride=stride), :] = value[:, j * 128 : (j + 1) * 128]


def get_lines(ref, start, count):
    return jnp.concatenate([ref[j, start : start + count, :] for j in range(ref.shape[0])], axis=1)


def convolution_kernel(ends, own, other, w_first, b_first, w_second, b_second, out, stacked, result):
    channels, depth, ny = own.shape
    rows = depth - 4
    group = stacked.shape[1] // depth
    lanes = result.shape[1] // rows
    stacked[...] = jnp.zeros_like(stacked)
    for t, source in enumerate((own, other)):
        for i in range(channels):
            value = source[i].astype(F32)
            for d in range(3):
                line = value if d == 1 else shifted(value, d - 1)
                put_strided(stacked, (d * 2 + t) * channels + i, depth, group, line)
    partial = []
    taps = w_second.shape[0] // 3
    for z in range(rows + 2):
        window = get_lines(stacked, z * group, 3 * group).astype(BF16)
        hidden = jnp.maximum(nn_dot(w_first[...], window) + b_first[...], 0.0)
        if z == 0:
            hidden = hidden * ends[0].astype(F32)
        if z == rows + 1:
            hidden = hidden * ends[1].astype(F32)
        partial.append(nn_dot(w_second[...], hidden.astype(BF16)))
        if z >= 2:
            total = partial[z - 2][:taps] + partial[z - 1][taps : 2 * taps] + partial[z][2 * taps :]
            line = (
                shifted(total[:lanes], -1) + total[lanes : 2 * lanes] + shifted(total[2 * lanes :], 1)
            )
            put_strided(result, z - 2, lanes, rows, line)
            partial[z - 2] = None
    for i in range(channels):
        value = own[i].astype(F32)[2 : 2 + rows]
        out[i] = (value + get_lines(result, i * rows, rows) + b_second[i]).astype(BF16)


def convolutions(ends, own, other, w_first, b_first, w_second, b_second):
    channels, depth, ny = own.shape
    rows = depth - 4
    group = w_first.shape[1] // 3
    lanes = w_second.shape[0] // 9
    vmem = pl.BlockSpec(memory_space=pltpu.VMEM)
    smem = pl.BlockSpec(memory_space=pltpu.SMEM)
    flops = 2 * (rows + 2) * ny * (w_first.size + w_second.size)
    return pl.pallas_call(
        convolution_kernel,
        in_specs=[smem, vmem, vmem, vmem, vmem, vmem, smem],
        out_specs=vmem,
        out_shape=jax.ShapeDtypeStruct((channels, rows, ny), BF16),
        scratch_shapes=[
            pltpu.VMEM((ny // 128, depth * group, 128), F32),
            pltpu.VMEM((ny // 128, lanes * rows, 128), F32),
        ],
        compiler_params=pltpu.CompilerParams(vmem_limit_bytes=24 * 2**20),
        cost_estimate=pl.CostEstimate(flops=flops, bytes_accessed=2**20, transcendentals=0),
        name="convolutions",
    )(ends, own, other, w_first, b_first, w_second, b_second)


def round_up(value, unit):
    return -(-value // unit) * unit


def convolution_weights(first_weight, first_bias, second_weight):
    q = lax.axis_index(COIL)
    ahead = 2 - 2 * q
    behind = 2 * q

    def tap(weight, index):
        return lax.dynamic_index_in_dim(weight, index, axis=2, keepdims=False)

    feat, channels = first_weight.shape[:2]
    same, of_other, of_own = (tap(first_weight, i) for i in (1, ahead, behind))
    first = jnp.stack([jnp.stack([same, of_other], 1), jnp.stack([of_own, same], 1)], 0)
    first = first.transpose(0, 1, 4, 5, 2, 3).reshape(2 * feat, 3, 6 * channels)
    group = round_up(6 * channels, 16)
    first = jnp.pad(first, ((0, 0), (0, 0), (0, group - 6 * channels))).reshape(2 * feat, 3 * group)
    bias = jnp.concatenate([first_bias, first_bias])[:, None]
    second = jnp.stack([tap(second_weight, 1), tap(second_weight, ahead)], 1)
    second = second.transpose(3, 4, 0, 1, 2).reshape(3, 3, channels, 2 * feat)
    lanes = round_up(channels, 8)
    second = jnp.pad(second, ((0, 0), (0, 0), (0, lanes - channels), (0, 0))).reshape(9 * lanes, 2 * feat)
    return first, bias, second


def paired(current_image, coil_maps, measured, sampling, first_weight, first_bias, second_weight, second_bias):
    devices = lax.axis_size(SLAB)
    ring = Ring(devices)
    me, q = lax.axis_index(SLAB), lax.axis_index(COIL)
    _, encodings, _, width, rows, ny = current_image.shape
    nz = rows * devices
    channels = 2 * encodings
    tables = (
        split_tables(ny, 3, True, False),
        split_tables(nz, 2, False, False),
        split_tables(nz, 2, True, True),
        split_tables(ny, 3, False, True),
    )
    where = jnp.concatenate([ring.slabs(), q[None].astype(jnp.int32)])
    swap = [(0, 1), (1, 0)]
    weights = convolution_weights(first_weight, first_bias, second_weight)
    ends = jnp.stack([me > 0, me < devices - 1]).astype(jnp.int32)

    images, pairs = prepare(q[None].astype(jnp.int32), current_image, coil_maps)
    gather = Gather(ring, images[None])
    kept = lax.all_to_all(pairs, SLAB, split_axis=0, concat_axis=0, tiled=True)
    for step in range(len(ring.steps())):
        gather.step(*((kept,) if step == 2 else ()))
    scatters = []
    for x in range(width):
        maps = (kept[:, x], lax.ppermute(kept[:, x], COIL, swap))
        scatters.append(Scatter(ring, *gradient(where, gather.pieces(), maps, measured, sampling, tables, x)))
    for _ in ring.steps():
        for scatter in scatters:
            scatter.step()
    chip = jnp.stack([scatter.chip() for scatter in scatters])
    updated = update(images, chip[:, 0], lax.ppermute(chip[:, 1].astype(BF16), SLAB, ring.siblings()))
    up = [(i, i + 1) for i in range(devices - 1)]
    down = [(i + 1, i) for i in range(devices - 1)]
    before = lax.ppermute(updated[:, :, rows - 2 :], SLAB, up)
    behind = lax.ppermute(updated[:, :, :2], SLAB, down)
    refined = []
    for x in range(width):
        bordered = jnp.concatenate([before[x], updated[x], behind[x]], axis=1)
        other = lax.ppermute(bordered, COIL, swap)
        refined.append(convolutions(ends, bordered, other, *weights, second_bias))
    out = jnp.stack(refined, axis=1).reshape(encodings, 2, width, rows, ny)
    return out[None]


def with_halo(cells, sides, width):
    for axis, dim in sides:
        count = lax.axis_size(axis)
        ends = count - 1
        head = lax.slice_in_dim(cells, 0, width, axis=dim)
        tail = lax.slice_in_dim(cells, cells.shape[dim] - width, cells.shape[dim], axis=dim)
        cells = jnp.concatenate(
            [
                lax.ppermute(tail, axis, [(i, (i + 1) % count) for i in range(ends)]),
                cells,
                lax.ppermute(head, axis, [((i + 1) % count, i) for i in range(ends)]),
            ],
            axis=dim,
        )
    return cells


def plain_table(length, inverse):
    indices = jnp.arange(length, dtype=jnp.int32)
    wrapped = indices[:, None] * indices[None, :] % length
    angles = wrapped.astype(jnp.float32) * (2.0 * math.pi / length)
    factor = 1.0 / math.sqrt(length)
    cosine = jnp.cos(angles) * factor
    sine_part = jnp.sin(angles) * factor
    phase_sign = 1.0 if inverse else -1.0
    upper_rows = jnp.stack([cosine, phase_sign * sine_part], axis=1)
    lower_rows = jnp.stack([-phase_sign * sine_part, cosine], axis=1)
    return jnp.stack([upper_rows, lower_rows], axis=0).astype(jnp.bfloat16)


def coil_products(maps_part, image_part):
    maps_real = maps_part[:, 0][None, :, None].astype(jnp.float32)
    maps_imaginary = maps_part[:, 1][None, :, None].astype(jnp.float32)
    image_real = image_part[:, :, 0][:, None].astype(jnp.float32)
    image_imaginary = image_part[:, :, 1][:, None].astype(jnp.float32)
    real_part = maps_real * image_real - maps_imaginary * image_imaginary
    imaginary_part = maps_real * image_imaginary + maps_imaginary * image_real
    return jnp.stack([real_part, imaginary_part], axis=3).astype(jnp.bfloat16)


def transform(operand, matrix):
    return jnp.einsum("pcerxzy,ryqk->pceqxzk", operand, matrix, preferred_element_type=jnp.float32)


def combine_coils(maps_part, values):
    maps_real = maps_part[:, 0][None, :, None].astype(jnp.float32)
    maps_imaginary = maps_part[:, 1][None, :, None].astype(jnp.float32)
    real_sum = jnp.sum(maps_real * values[:, :, :, 0] + maps_imaginary * values[:, :, :, 1], axis=1)
    imaginary_sum = jnp.sum(
        maps_real * values[:, :, :, 1] - maps_imaginary * values[:, :, :, 0], axis=1
    )
    return jnp.stack([real_sum, imaginary_sum], axis=2)


def convolve(operand, weights):
    widened = jnp.pad(operand, ((0, 0), (0, 0), (0, 0), (0, 0), (1, 1)))
    return lax.conv_general_dilated(
        widened,
        weights,
        (1, 1, 1),
        "VALID",
        dimension_numbers=("DCNHW", "OIDHW", "DCNHW"),
        preferred_element_type=jnp.float32,
    )


def on_device(
    current_image,
    coil_maps,
    measured,
    sampling,
    first_weight,
    first_bias,
    second_weight,
    second_bias,
):
    depth = current_image.shape[4] * lax.axis_size("slab")
    forward_y = plain_table(current_image.shape[5], False)
    inverse_y = plain_table(current_image.shape[5], True)
    forward_z = plain_table(depth, False)
    inverse_z = plain_table(depth, True)
    sampled = sampling.astype(jnp.float32)[:, None, :, None, None]
    local_maps = lax.all_to_all(coil_maps, "slab", split_axis=0, concat_axis=3, tiled=True)
    row_spectra = transform(
        coil_products(local_maps, lax.all_gather(current_image, "slab", axis=4, tiled=True)),
        forward_y,
    ).astype(jnp.bfloat16)
    residual = (
        sampled
        * (
            jnp.einsum(
                "pcerxzk,rzqj->pceqxkj", row_spectra, forward_z, preferred_element_type=jnp.float32
            )
            - measured.astype(jnp.float32)
        )
    ).astype(jnp.bfloat16)
    depth_back = jnp.einsum(
        "pcerxkj,rjqz->pceqxzk", residual, inverse_z, preferred_element_type=jnp.float32
    ).astype(jnp.bfloat16)
    partial_sum = combine_coils(local_maps, transform(depth_back, inverse_y))
    gradient = lax.psum_scatter(
        partial_sum.astype(jnp.bfloat16), "slab", scatter_dimension=4, tiled=True
    ).astype(jnp.float32)
    updated = (current_image.astype(jnp.float32) - gradient).astype(jnp.bfloat16)
    stacked = updated.reshape((updated.shape[0], 2 * updated.shape[1]) + updated.shape[3:])
    bias_first = first_bias[None, :, None, None, None]
    bordered = with_halo(stacked, (("slab", 3), ("coil", 0)), 1)
    hidden = jax.nn.relu(convolve(bordered, first_weight) + bias_first).astype(jnp.bfloat16)
    bordered_hidden = with_halo(hidden, (("slab", 3), ("coil", 0)), 1)
    second = convolve(bordered_hidden, second_weight)
    refined = stacked.astype(jnp.float32) + second + second_bias[None, :, None, None, None]
    return refined.astype(jnp.bfloat16).reshape(updated.shape)


def solution(mesh):
    devices, phases = mesh.shape[SLAB], mesh.shape[COIL]

    def per_device(*args):
        coils, phase = args[2].shape[1], args[0].shape[0]
        if phases == 2 and coils == 2 and phase == 1 and devices % 4 == 0 and args[0].shape[4] % 16 == 0 and args[0].shape[5] % 384 == 0:
            return paired(*args)
        return on_device(*args)

    in_specs = (
        P("coil", None, None, None, "slab", None),
        P(None, None, None, "slab", None),
        P("coil", "slab", None, None, None, None, None),
        P("coil", None, None, None),
        P(),
        P(),
        P(),
        P(),
    )
    out_specs = P("coil", None, None, None, "slab", None)
    return jax.shard_map(
        per_device, mesh=mesh, in_specs=in_specs, out_specs=out_specs, check_vma=False
    )
```

```python
import functools
import math

import jax
import jax.numpy as jnp
import ml_dtypes
import numpy as np
from jax import lax
from jax.experimental import pallas as pl
from jax.experimental.pallas import tpu as pltpu
from jax.sharding import PartitionSpec as P

BF16 = jnp.bfloat16
F32 = jnp.float32
SLAB, COIL = "slab", "coil"


def dft_table(length, inverse):
    indices = np.arange(length, dtype=np.int64)
    wrapped = indices[:, None] * indices[None, :] % length
    angles = wrapped.astype(np.float32) * np.float32(2.0 * math.pi / length)
    factor = np.float32(1.0 / math.sqrt(length))
    cosine = np.cos(angles) * factor
    sine = np.sin(angles) * factor
    sign = np.float32(1.0 if inverse else -1.0)
    upper = np.stack([cosine, sign * sine], axis=1)
    lower = np.stack([-sign * sine, cosine], axis=1)
    return np.stack([upper, lower], axis=0).astype(ml_dtypes.bfloat16)


def split_tables(length, count, left, inverse):
    table = dft_table(length, inverse)
    part = length // count
    out = []
    for s in range(count):
        if inverse:
            piece = table[:, :part, :, s::count]
        else:
            piece = table[:, s::count, :, :part]
        if left:
            piece = piece.transpose(2, 3, 0, 1)
        out.append(piece.reshape(2 * part, 2 * part))
    return jnp.asarray(np.stack(out))


def order(length, count):
    taken = np.arange(length).reshape(-1, count).T.reshape(-1)
    return np.eye(length, dtype=np.float32)[:, taken]


class Ring:
    def __init__(self, devices):
        self.devices = devices
        self.chips = devices // 2
        self.half = self.chips // 2
        column = self.chips // 2
        self.order = [2 * i for i in range(column)] + [2 * i + 1 for i in reversed(range(column))]

    def perm(self):
        pairs = []
        for i in range(self.chips):
            for core, step in ((0, 1), (1, -1)):
                pairs.append((2 * self.order[i] + core, 2 * self.order[(i + step) % self.chips] + core))
        return pairs

    def siblings(self):
        return [(i, i ^ 1) for i in range(self.devices)]

    def steps(self):
        return [(step, True) for step in range(1, self.half)] + [(self.half, False)]

    def slabs(self):
        me = lax.axis_index(SLAB)
        chip, core = me // 2, me % 2
        column = self.chips // 2
        row = chip // 2
        place = jnp.where(chip % 2 == 0, row, self.chips - 1 - row)

        def slab(offset, parity):
            at = (place + offset + self.chips) % self.chips
            return 2 * jnp.where(at < column, 2 * at, 2 * (self.chips - 1 - at) + 1) + parity

        def handled(by, sign):
            way = sign * (1 - 2 * by)
            out = []
            for step, both in self.steps():
                out += [slab(way * step, by)] + ([slab(way * step, 1 - by)] if both else [])
            return out

        own = [slab(0, core), slab(0, 1 - core)]
        gathered = own + handled(core, -1) + handled(1 - core, -1)
        summed = own + handled(core, 1) + handled(1 - core, 1)
        return jnp.stack(gathered + summed).astype(jnp.int32)


def after(value, *earlier):
    return lax.optimization_barrier((value,) + earlier)[0]


class Gather:
    def __init__(self, ring, mine):
        self.ring = ring
        self.first = lax.ppermute(mine, SLAB, ring.perm())
        self.own = [mine, lax.ppermute(mine, SLAB, ring.siblings())]
        self.held = None
        self.kept, self.other = [], []

    def step(self, *earlier):
        both = self.ring.steps()[len(self.kept)][1]
        if self.held is None:
            self.held = jnp.concatenate([self.first, lax.ppermute(self.own[1], SLAB, self.ring.perm())], axis=0)
        else:
            held = self.held if both else self.held[:1]
            self.held = lax.ppermute(after(held, *earlier) if earlier else held, SLAB, self.ring.perm())
        self.kept.append(self.held)
        self.other.append(lax.ppermute(self.held, SLAB, self.ring.siblings()))

    def pieces(self):
        return self.own + self.kept + self.other


class Scatter:
    def __init__(self, ring, own, kept, sent):
        self.ring, self.own, self.kept = ring, own, kept
        self.other = lax.ppermute(sent, SLAB, ring.siblings())
        self.held = None
        self.left = list(ring.steps())
        self.end = kept.shape[0]

    def step(self):
        count = 2 if self.left.pop()[1] else 1
        self.end -= count
        total = self.kept[self.end : self.end + count].astype(F32) + self.other[self.end : self.end + count].astype(F32)
        if self.held is not None:
            got = self.held.astype(F32)
            if got.shape[0] < count:
                total = jnp.concatenate([total[:1] + got, total[1:]], axis=0)
            else:
                total = total + got
        self.held = lax.ppermute(total.astype(BF16), SLAB, self.ring.perm())
        return self.held

    def chip(self):
        return self.own.astype(F32) + self.held.astype(F32)


def nt_dot(a, b):
    return lax.dot_general(a, b, (((1,), (1,)), ((), ())), preferred_element_type=F32)


def nn_dot(a, b):
    return lax.dot_general(a, b, (((1,), (0,)), ((), ())), preferred_element_type=F32)


def gradient_kernel(images, coils, slabs, *refs):
    held_images, refs = refs[:images], refs[images:]
    maps, refs = refs[:coils], refs[coils:]
    measured, sampling, ty_f, tz_f, tz_i, ty_i = refs[:6]
    out, products, backs = refs[6:9], refs[9], refs[10]
    rows, ny = held_images[0].shape[-2:]
    nz = sampling.shape[-1]
    count, half = nz // rows, rows // 2
    my, mz = ny // 3, nz // 2
    first = slabs[2 * count]
    root = math.sqrt(0.75)

    def pieces(arrays):
        return [(array, i) for array in arrays for i in range(array.shape[0])]

    def places(slab):
        at = pl.multiple_of(slab * half, half)
        return pl.ds(at, half), pl.ds(pl.multiple_of(at + mz, half), half)

    def thirds(b0, b1, b2, sign):
        add = [u + v for u, v in zip(b1, b2)]
        low = [u - 0.5 * v for u, v in zip(b0, add)]
        turn = [(sign * root) * (u - v) for u, v in zip(b1, b2)]
        return (
            (b0[0] + add[0], b0[1] + add[1]),
            (low[0] - turn[1], low[1] + turn[0]),
            (low[0] + turn[1], low[1] - turn[0]),
        )

    for k, (held, i) in enumerate(pieces(held_images)):
        slab = slabs[k]
        real = held[i, 0].astype(F32)
        imag = held[i, 1].astype(F32)
        for c in range(coils):
            m_real = maps[c][slab, 0, 0].astype(F32)
            m_imag = maps[c][slab, 0, 1].astype(F32)
            p_real = m_real * real - m_imag * imag
            p_imag = m_real * imag + m_imag * real
            for parity, at in enumerate(places(slab)):
                lines = slice(parity * half, (parity + 1) * half)
                for j in range(3):
                    cells = slice(j * my, (j + 1) * my)
                    products[c, j, at, :my] = p_real[lines, cells]
                    products[c, j, at, my:] = p_imag[lines, cells]
    mask = sampling[0, 0].astype(F32)
    folds = [[], []]
    for c in range(coils):
        parts = [nt_dot(ty_f[j], products[c, j].astype(BF16)) for j in range(3)]
        parts = thirds(*[(part[:my], part[my:]) for part in parts], -1.0)
        spectra = [jnp.concatenate([part[q].astype(BF16) for part in parts], axis=0) for q in range(2)]
        halves = []
        for j in range(2):
            cells = slice(j * mz, (j + 1) * mz)
            halves.append(nn_dot(jnp.concatenate([spectra[0][:, cells], spectra[1][:, cells]], axis=1), tz_f[j]))
        coil = first if c == 0 else 1 - first
        sums, differences = [], []
        for q in range(2):
            cells = slice(q * mz, (q + 1) * mz)
            seen = measured[0, coil, 0, q, 0].astype(F32)
            low = mask[:, :mz] * (halves[0][:, cells] + halves[1][:, cells] - seen[:, :mz])
            high = mask[:, mz:] * (halves[0][:, cells] - halves[1][:, cells] - seen[:, mz:])
            sums.append((low + high).astype(BF16))
            differences.append((low - high).astype(BF16))
        folds[0].append(jnp.concatenate(sums, axis=1))
        folds[1].append(jnp.concatenate(differences, axis=1))
    depths = [nt_dot(tz_i[j], jnp.concatenate(folds[j], axis=0)) for j in range(2)]
    for c in range(coils):
        lines = [[], [], []]
        for j in range(2):
            cut = lambda q, i: depths[j][q * mz : (q + 1) * mz, c * ny + i * my : c * ny + (i + 1) * my]
            turned = thirds(*[(cut(0, i), cut(1, i)) for i in range(3)], 1.0)
            for i in range(3):
                lines[i].append(jnp.concatenate([turned[i][0].astype(BF16), turned[i][1].astype(BF16)], axis=1))
        for i in range(3):
            backs[c, i] = nn_dot(jnp.concatenate(lines[i], axis=0), ty_i[i])
    for k, (held, i) in enumerate(pieces(out)):
        slab = slabs[count + k]
        for j in range(3):
            cells = slice(j * my, (j + 1) * my)
            real, imag = 0.0, 0.0
            for c in range(coils):
                m_real = maps[c][slab, 0, 0, :, cells].astype(F32)
                m_imag = maps[c][slab, 0, 1, :, cells].astype(F32)
                back = jnp.concatenate([backs[c, j, at, :] for at in places(slab)], axis=0)
                real += m_real * back[:, :my] + m_imag * back[:, my:]
                imag += m_real * back[:, my:] - m_imag * back[:, :my]
            held[i, 0, :, cells] = real.astype(BF16)
            held[i, 1, :, cells] = imag.astype(BF16)


def gradient(where, images, maps, measured, sampling, tables, x):
    _, channels, rows, ny = images[0].shape
    nz = sampling.shape[-1]
    n = len(maps)
    far = (nz // rows - 2) // 2
    whole = lambda a: pl.BlockSpec(a.shape, lambda e, s: (0,) * a.ndim, pipeline_mode=pl.Buffered(1))
    flops = channels * n * 2 * 4 * (nz * ny * ny + nz * nz * ny)
    return pl.pallas_call(
        functools.partial(gradient_kernel, len(images), n),
        grid_spec=pltpu.PrefetchScalarGridSpec(
            num_scalar_prefetch=1,
            grid=(channels // 2,),
            in_specs=[pl.BlockSpec((a.shape[0], 2, rows, ny), lambda e, s: (0, e, 0, 0)) for a in images]
            + [
                pl.BlockSpec((a.shape[0], 1, 2, rows, ny), functools.partial(lambda at, e, s: (0, at, 0, 0, 0), at),
                             pipeline_mode=pl.Buffered(1))
                for a, at in maps
            ]
            + [
                pl.BlockSpec((1, 2, 1, 2, 1, ny, nz), lambda e, s: (0, 0, e, 0, x, 0, 0)),
                pl.BlockSpec((1, 1, ny, nz), lambda e, s: (0, e, 0, 0)),
            ]
            + [whole(t) for t in tables],
            out_specs=[pl.BlockSpec((m, 2, rows, ny), lambda e, s: (0, e, 0, 0)) for m in (2, far, far)],
            scratch_shapes=[
                pltpu.VMEM((n, 3, nz, 2 * ny // 3), F32),
                pltpu.VMEM((n, 3, nz, 2 * ny // 3), F32),
            ],
        ),
        out_shape=[jax.ShapeDtypeStruct((m, channels, rows, ny), BF16) for m in (2, far, far)],
        compiler_params=pltpu.CompilerParams(vmem_limit_bytes=40 * 2**20),
        cost_estimate=pl.CostEstimate(flops=flops, bytes_accessed=8 * 2**20, transcendentals=0),
        name="gradient",
    )(where, *images, *[a for a, _ in maps], measured, sampling, *tables)


def reordered(value, along_z, along_y):
    n, rows, ny = value.shape
    block = along_z.shape[0]
    flat = nn_dot(value.reshape(n * rows, ny), along_y).astype(BF16)
    out = []
    for start in range(0, n * rows, block):
        size = min(block, n * rows - start)
        out.append(nn_dot(along_z[:size, :size], flat[start : start + size]).astype(BF16))
    return jnp.concatenate(out, axis=0).reshape(n, rows, ny)


def orders(rows, ny, back):
    z, y = order(rows, 2), order(ny, 3)
    along_z = np.kron(np.eye(8, dtype=np.float32), z if back else z.T)
    return jnp.asarray(along_z, BF16), jnp.asarray(y.T if back else y, BF16)


def prepare_kernel(which, image, maps, along_z, along_y, image_out, maps_out):
    width, channels, rows, ny = image_out.shape

    @pl.when(pl.program_id(0) == 0)
    def _():
        picked = image[...].reshape((channels, width, rows, ny))
        for x in range(width):
            image_out[x] = reordered(picked[:, x], along_z[...], along_y[...])

    count = maps_out.shape[0]
    value = reordered(maps[:, 0].reshape((count * 2 * width, rows, ny)), along_z[...], along_y[...])
    for pair in range(count):
        for x in range(width):
            for part in range(2):
                maps_out[pair, x, part] = value[(pair * 2 + part) * width + x]


def prepare(which, current_image, coil_maps):
    _, encodings, _, width, rows, ny = current_image.shape
    devices = coil_maps.shape[0] // 2
    pairs = coil_maps.reshape((devices, 2) + coil_maps.shape[1:])
    whole = lambda shape: pl.BlockSpec(shape, lambda i, t: (0,) * len(shape))
    matrices = orders(rows, ny, False)
    image_shape = (width, 2 * encodings, rows, ny)
    steps = 4
    group = (devices // steps, width, 2, rows, ny)
    return pl.pallas_call(
        prepare_kernel,
        grid_spec=pltpu.PrefetchScalarGridSpec(
            num_scalar_prefetch=1,
            grid=(steps,),
            in_specs=[
                whole(current_image.shape),
                pl.BlockSpec((devices // steps, 1) + coil_maps.shape[1:], lambda i, t: (i, t[0], 0, 0, 0, 0)),
            ]
            + [whole(m.shape) for m in matrices],
            out_specs=[whole(image_shape), pl.BlockSpec(group, lambda i, t: (i, 0, 0, 0, 0))],
        ),
        out_shape=[
            jax.ShapeDtypeStruct(image_shape, BF16),
            jax.ShapeDtypeStruct((devices, width, 2, rows, ny), BF16),
        ],
        compiler_params=pltpu.CompilerParams(vmem_limit_bytes=58 * 2**20),
        name="prepare",
    )(which, current_image, pairs, *matrices)


def update_kernel(image, chip, received, along_z, along_y, out):
    for x in range(image.shape[0]):
        value = image[x].astype(F32) - (chip[x] + received[x].astype(F32))
        out[x] = reordered(value.astype(BF16), along_z[...], along_y[...])


def update(image, chip, received):
    vmem = pl.BlockSpec(memory_space=pltpu.VMEM)
    return pl.pallas_call(
        update_kernel,
        in_specs=[vmem] * 5,
        out_specs=vmem,
        out_shape=jax.ShapeDtypeStruct(image.shape, BF16),
        compiler_params=pltpu.CompilerParams(vmem_limit_bytes=16 * 2**20),
        name="update",
    )(image, chip, received, *orders(*image.shape[-2:], True))


def shifted(value, step):
    rows = value.shape[:-1]
    edge = jnp.zeros(rows + (1,), value.dtype)
    if step > 0:
        return jnp.concatenate([value[..., 1:], edge], axis=-1)
    return jnp.concatenate([edge, value[..., :-1]], axis=-1)


def put_strided(ref, start, count, stride, value):
    for j in range(ref.shape[0]):
        ref[j, pl.ds(start, count, stride=stride), :] = value[:, j * 128 : (j + 1) * 128]


def get_lines(ref, start, count):
    return jnp.concatenate([ref[j, start : start + count, :] for j in range(ref.shape[0])], axis=1)


def convolution_kernel(ends, *refs):
    sources, refs = (refs[:3], refs[3:6]), refs[6:]
    w_first, b_first, w_second, b_second, out, stacked, result = refs
    _, channels, rows, ny = sources[0][1].shape
    depth = rows + 4
    group = stacked.shape[1] // depth
    lanes = result.shape[1] // rows
    stacked[...] = jnp.zeros_like(stacked)
    for t, source in enumerate(sources):
        for i in range(channels):
            value = jnp.concatenate([part[0, i].astype(F32) for part in source], axis=0)
            for d in range(3):
                line = value if d == 1 else shifted(value, d - 1)
                put_strided(stacked, (d * 2 + t) * channels + i, depth, group, line)
    features = w_first.shape[0] // 2
    taps = w_second.shape[0] // 4
    partial = []
    for pair in range(rows // 2 + 1):
        window = get_lines(stacked, 2 * pair * group, 4 * group).astype(BF16)
        hidden = jnp.maximum(nn_dot(w_first[...], window) + b_first[...], 0.0)
        if pair == 0:
            hidden = jnp.concatenate([hidden[:features] * ends[0].astype(F32), hidden[features:]], axis=0)
        if pair == rows // 2:
            hidden = jnp.concatenate([hidden[:features], hidden[features:] * ends[1].astype(F32)], axis=0)
        partial.append(nn_dot(w_second[...], hidden.astype(BF16)))
        if pair > 0:
            for z in range(2):
                total = partial[0][(2 + z) * taps : (3 + z) * taps] + partial[1][z * taps : (z + 1) * taps]
                line = shifted(total[:lanes], -1) + total[lanes : 2 * lanes] + shifted(total[2 * lanes :], 1)
                put_strided(result, 2 * pair - 2 + z, lanes, rows, line)
            partial = partial[1:]
    for i in range(channels):
        value = sources[0][1][0, i].astype(F32)
        out[0, i // 2, i % 2, 0] = (value + get_lines(result, i * rows, rows) + b_second[i]).astype(BF16)


def convolutions(ends, parts, w_first, b_first, w_second, b_second, encodings):
    width, channels, rows, ny = parts[1].shape
    depth = rows + 4
    group = w_first.shape[1] // 4
    lanes = w_second.shape[0] // 12
    smem = pl.BlockSpec(memory_space=pltpu.SMEM)
    whole = lambda a: pl.BlockSpec(a.shape, lambda x: (0,) * a.ndim)
    flops = width * (rows + 2) * ny * (w_first.size + w_second.size)
    return pl.pallas_call(
        convolution_kernel,
        grid=(width,),
        in_specs=[smem]
        + [pl.BlockSpec((1,) + a.shape[1:], lambda x: (x, 0, 0, 0)) for a in parts]
        + [whole(w_first), whole(b_first), whole(w_second), smem],
        out_specs=pl.BlockSpec((1, encodings, 2, 1, rows, ny), lambda x: (0, 0, 0, x, 0, 0)),
        out_shape=jax.ShapeDtypeStruct((1, encodings, 2, width, rows, ny), BF16),
        scratch_shapes=[
            pltpu.VMEM((ny // 128, depth * group, 128), F32),
            pltpu.VMEM((ny // 128, lanes * rows, 128), F32),
        ],
        compiler_params=pltpu.CompilerParams(vmem_limit_bytes=24 * 2**20),
        cost_estimate=pl.CostEstimate(flops=flops, bytes_accessed=2**20, transcendentals=0),
        name="convolutions",
    )(ends, *parts, w_first, b_first, w_second, b_second)


def round_up(value, unit):
    return -(-value // unit) * unit


def convolution_weights(first_weight, first_bias, second_weight):
    q = lax.axis_index(COIL)
    ahead = 2 - 2 * q
    behind = 2 * q

    def tap(weight, index):
        return lax.dynamic_index_in_dim(weight, index, axis=2, keepdims=False)

    feat, channels = first_weight.shape[:2]
    same, of_other, of_own = (tap(first_weight, i) for i in (1, ahead, behind))
    first = jnp.stack([jnp.stack([same, of_other], 1), jnp.stack([of_own, same], 1)], 0)
    first = first.transpose(0, 1, 4, 5, 2, 3).reshape(2 * feat, 3, 6 * channels)
    group = round_up(6 * channels, 16)
    first = jnp.pad(first, ((0, 0), (0, 0), (0, group - 6 * channels))).reshape(2 * feat, 3 * group)
    first = jnp.concatenate([jnp.pad(first, ((0, 0), (0, group))), jnp.pad(first, ((0, 0), (group, 0)))], axis=0)
    bias = jnp.concatenate([first_bias] * 4)[:, None]
    second = jnp.stack([tap(second_weight, 1), tap(second_weight, ahead)], 1)
    second = second.transpose(3, 4, 0, 1, 2).reshape(3, 3, channels, 2 * feat)
    lanes = round_up(channels, 8)
    second = jnp.pad(second, ((0, 0), (0, 0), (0, lanes - channels), (0, 0))).reshape(3, 3 * lanes, 2 * feat)
    none = jnp.zeros_like(second[0])
    line = lambda u: jnp.concatenate([second[u + 2 - r] if 0 <= u + 2 - r <= 2 else none for r in range(4)], axis=0)
    return first, bias, jnp.concatenate([line(0), line(1)], axis=1)


def paired(current_image, coil_maps, measured, sampling, first_weight, first_bias, second_weight, second_bias):
    devices = lax.axis_size(SLAB)
    ring = Ring(devices)
    me, q = lax.axis_index(SLAB), lax.axis_index(COIL)
    _, encodings, _, width, rows, ny = current_image.shape
    nz = rows * devices
    channels = 2 * encodings
    tables = (
        split_tables(ny, 3, True, False),
        split_tables(nz, 2, False, False),
        split_tables(nz, 2, True, True),
        split_tables(ny, 3, False, True),
    )
    which = q[None].astype(jnp.int32)
    where = jnp.concatenate([ring.slabs(), which])
    swap = [(0, 1), (1, 0)]
    weights = convolution_weights(first_weight, first_bias, second_weight)
    ends = jnp.stack([me > 0, me < devices - 1]).astype(jnp.int32)

    images, pairs = prepare(which, current_image, coil_maps)
    gathers = [Gather(ring, images[x : x + 1]) for x in range(width)]
    kept = lax.all_to_all(after(pairs, *[gather.own[1] for gather in gathers]), SLAB, split_axis=0, concat_axis=0, tiled=True)
    halves = [kept[:, x : x + 1] for x in range(width)]
    for step in range(len(ring.steps())):
        for gather in gathers:
            gather.step(*((halves[step - 2],) if 2 <= step < 2 + width else ()))
    swapped = [lax.ppermute(half, COIL, swap) for half in halves]
    scatters = []
    for x in range(width):
        scatters.append(Scatter(ring, *gradient(where, gathers[x].pieces(), [(kept, x), (swapped[x], 0)], measured, sampling, tables, x)))
    for _ in ring.steps():
        for scatter in scatters:
            scatter.step()
    chip = jnp.stack([scatter.chip() for scatter in scatters])
    updated = update(images, chip[:, 0], lax.ppermute(chip[:, 1].astype(BF16), SLAB, ring.siblings()))
    both = (SLAB, COIL)
    cross = lambda shift, flip: [
        ((i * 2 + q), ((i + shift) * 2 + (q ^ flip)))
        for i in range(devices)
        for q in range(2)
        if 0 <= i + shift < devices
    ]
    head, tail = updated[:, :, :2], updated[:, :, rows - 2 :]
    phases = []
    for flip in range(2):
        phases.append(
            [
                lax.ppermute(tail, both, cross(1, flip)),
                lax.ppermute(updated, both, cross(0, 1)) if flip else updated,
                lax.ppermute(head, both, cross(-1, flip)),
            ]
        )
    return convolutions(ends, phases[0] + phases[1], *weights, second_bias, encodings)


def with_halo(cells, sides, width):
    for axis, dim in sides:
        count = lax.axis_size(axis)
        ends = count - 1
        head = lax.slice_in_dim(cells, 0, width, axis=dim)
        tail = lax.slice_in_dim(cells, cells.shape[dim] - width, cells.shape[dim], axis=dim)
        cells = jnp.concatenate(
            [
                lax.ppermute(tail, axis, [(i, (i + 1) % count) for i in range(ends)]),
                cells,
                lax.ppermute(head, axis, [((i + 1) % count, i) for i in range(ends)]),
            ],
            axis=dim,
        )
    return cells


def plain_table(length, inverse):
    indices = jnp.arange(length, dtype=jnp.int32)
    wrapped = indices[:, None] * indices[None, :] % length
    angles = wrapped.astype(jnp.float32) * (2.0 * math.pi / length)
    factor = 1.0 / math.sqrt(length)
    cosine = jnp.cos(angles) * factor
    sine_part = jnp.sin(angles) * factor
    phase_sign = 1.0 if inverse else -1.0
    upper_rows = jnp.stack([cosine, phase_sign * sine_part], axis=1)
    lower_rows = jnp.stack([-phase_sign * sine_part, cosine], axis=1)
    return jnp.stack([upper_rows, lower_rows], axis=0).astype(jnp.bfloat16)


def coil_products(maps_part, image_part):
    maps_real = maps_part[:, 0][None, :, None].astype(jnp.float32)
    maps_imaginary = maps_part[:, 1][None, :, None].astype(jnp.float32)
    image_real = image_part[:, :, 0][:, None].astype(jnp.float32)
    image_imaginary = image_part[:, :, 1][:, None].astype(jnp.float32)
    real_part = maps_real * image_real - maps_imaginary * image_imaginary
    imaginary_part = maps_real * image_imaginary + maps_imaginary * image_real
    return jnp.stack([real_part, imaginary_part], axis=3).astype(jnp.bfloat16)


def transform(operand, matrix):
    return jnp.einsum("pcerxzy,ryqk->pceqxzk", operand, matrix, preferred_element_type=jnp.float32)


def combine_coils(maps_part, values):
    maps_real = maps_part[:, 0][None, :, None].astype(jnp.float32)
    maps_imaginary = maps_part[:, 1][None, :, None].astype(jnp.float32)
    real_sum = jnp.sum(maps_real * values[:, :, :, 0] + maps_imaginary * values[:, :, :, 1], axis=1)
    imaginary_sum = jnp.sum(
        maps_real * values[:, :, :, 1] - maps_imaginary * values[:, :, :, 0], axis=1
    )
    return jnp.stack([real_sum, imaginary_sum], axis=2)


def convolve(operand, weights):
    widened = jnp.pad(operand, ((0, 0), (0, 0), (0, 0), (0, 0), (1, 1)))
    return lax.conv_general_dilated(
        widened,
        weights,
        (1, 1, 1),
        "VALID",
        dimension_numbers=("DCNHW", "OIDHW", "DCNHW"),
        preferred_element_type=jnp.float32,
    )


def on_device(
    current_image,
    coil_maps,
    measured,
    sampling,
    first_weight,
    first_bias,
    second_weight,
    second_bias,
):
    depth = current_image.shape[4] * lax.axis_size("slab")
    forward_y = plain_table(current_image.shape[5], False)
    inverse_y = plain_table(current_image.shape[5], True)
    forward_z = plain_table(depth, False)
    inverse_z = plain_table(depth, True)
    sampled = sampling.astype(jnp.float32)[:, None, :, None, None]
    local_maps = lax.all_to_all(coil_maps, "slab", split_axis=0, concat_axis=3, tiled=True)
    row_spectra = transform(
        coil_products(local_maps, lax.all_gather(current_image, "slab", axis=4, tiled=True)),
        forward_y,
    ).astype(jnp.bfloat16)
    residual = (
        sampled
        * (
            jnp.einsum(
                "pcerxzk,rzqj->pceqxkj", row_spectra, forward_z, preferred_element_type=jnp.float32
            )
            - measured.astype(jnp.float32)
        )
    ).astype(jnp.bfloat16)
    depth_back = jnp.einsum(
        "pcerxkj,rjqz->pceqxzk", residual, inverse_z, preferred_element_type=jnp.float32
    ).astype(jnp.bfloat16)
    partial_sum = combine_coils(local_maps, transform(depth_back, inverse_y))
    gradient = lax.psum_scatter(
        partial_sum.astype(jnp.bfloat16), "slab", scatter_dimension=4, tiled=True
    ).astype(jnp.float32)
    updated = (current_image.astype(jnp.float32) - gradient).astype(jnp.bfloat16)
    stacked = updated.reshape((updated.shape[0], 2 * updated.shape[1]) + updated.shape[3:])
    bias_first = first_bias[None, :, None, None, None]
    bordered = with_halo(stacked, (("slab", 3), ("coil", 0)), 1)
    hidden = jax.nn.relu(convolve(bordered, first_weight) + bias_first).astype(jnp.bfloat16)
    bordered_hidden = with_halo(hidden, (("slab", 3), ("coil", 0)), 1)
    second = convolve(bordered_hidden, second_weight)
    refined = stacked.astype(jnp.float32) + second + second_bias[None, :, None, None, None]
    return refined.astype(jnp.bfloat16).reshape(updated.shape)


def solution(mesh):
    devices, phases = mesh.shape[SLAB], mesh.shape[COIL]

    def per_device(*args):
        coils, phase = args[2].shape[1], args[0].shape[0]
        if phases == 2 and coils == 2 and phase == 1 and devices % 4 == 0 and args[0].shape[4] % 16 == 0 and args[0].shape[5] % 384 == 0:
            return paired(*args)
        return on_device(*args)

    in_specs = (
        P("coil", None, None, None, "slab", None),
        P(None, None, None, "slab", None),
        P("coil", "slab", None, None, None, None, None),
        P("coil", None, None, None),
        P(),
        P(),
        P(),
        P(),
    )
    out_specs = P("coil", None, None, None, "slab", None)
    return jax.shard_map(
        per_device, mesh=mesh, in_specs=in_specs, out_specs=out_specs, check_vma=False
    )
```

```python
import functools
import math

import jax
import jax.numpy as jnp
import ml_dtypes
import numpy as np
from jax import lax
from jax.experimental import pallas as pl
from jax.experimental.pallas import tpu as pltpu
from jax.sharding import PartitionSpec as P

BF16 = jnp.bfloat16
F32 = jnp.float32
SLAB, COIL = "slab", "coil"


def dft_table(length, inverse):
    indices = np.arange(length, dtype=np.int64)
    wrapped = indices[:, None] * indices[None, :] % length
    angles = wrapped.astype(np.float32) * np.float32(2.0 * math.pi / length)
    factor = np.float32(1.0 / math.sqrt(length))
    cosine = np.cos(angles) * factor
    sine = np.sin(angles) * factor
    sign = np.float32(1.0 if inverse else -1.0)
    upper = np.stack([cosine, sign * sine], axis=1)
    lower = np.stack([-sign * sine, cosine], axis=1)
    return np.stack([upper, lower], axis=0).astype(ml_dtypes.bfloat16)


def split_tables(length, count, left, inverse):
    table = dft_table(length, inverse)
    part = length // count
    out = []
    for s in range(count):
        if inverse:
            piece = table[:, :part, :, s::count]
        else:
            piece = table[:, s::count, :, :part]
        if left:
            piece = piece.transpose(2, 3, 0, 1)
        out.append(piece.reshape(2 * part, 2 * part))
    return np.stack(out)


def order(length, count):
    taken = np.arange(length).reshape(-1, count).T.reshape(-1)
    return np.eye(length, dtype=np.float32)[:, taken]


class Ring:
    def __init__(self, devices):
        self.devices = devices
        self.chips = devices // 2
        self.half = self.chips // 2
        column = self.chips // 2
        self.order = [2 * i for i in range(column)] + [2 * i + 1 for i in reversed(range(column))]

    def perm(self):
        pairs = []
        for i in range(self.chips):
            for core, step in ((0, 1), (1, -1)):
                pairs.append((2 * self.order[i] + core, 2 * self.order[(i + step) % self.chips] + core))
        return pairs

    def siblings(self):
        return [(i, i ^ 1) for i in range(self.devices)]

    def steps(self):
        return [(step, True) for step in range(1, self.half)] + [(self.half, False)]

    def slabs(self):
        me = lax.axis_index(SLAB)
        chip, core = me // 2, me % 2
        column = self.chips // 2
        row = chip // 2
        place = jnp.where(chip % 2 == 0, row, self.chips - 1 - row)

        def slab(offset, parity):
            at = (place + offset + self.chips) % self.chips
            return 2 * jnp.where(at < column, 2 * at, 2 * (self.chips - 1 - at) + 1) + parity

        def handled(by, sign):
            way = sign * (1 - 2 * by)
            out = []
            for step, both in self.steps():
                out += [slab(way * step, by)] + ([slab(way * step, 1 - by)] if both else [])
            return out

        own = [slab(0, core), slab(0, 1 - core)]
        gathered = own + handled(core, -1) + handled(1 - core, -1)
        summed = own + handled(core, 1) + handled(1 - core, 1)
        return jnp.stack(gathered + summed).astype(jnp.int32)


def after(value, *earlier):
    return lax.optimization_barrier((value,) + earlier)[0]


class Gather:
    def __init__(self, ring, mine):
        self.ring = ring
        self.first = lax.ppermute(mine, SLAB, ring.perm())
        self.own = [mine, lax.ppermute(mine, SLAB, ring.siblings())]
        self.held = None
        self.kept, self.other = [], []

    def step(self, *earlier):
        both = self.ring.steps()[len(self.kept)][1]
        if self.held is None:
            self.held = jnp.concatenate([self.first, lax.ppermute(self.own[1], SLAB, self.ring.perm())], axis=0)
        else:
            held = self.held if both else self.held[:1]
            self.held = lax.ppermute(after(held, *earlier) if earlier else held, SLAB, self.ring.perm())
        self.kept.append(self.held)
        self.other.append(lax.ppermute(self.held, SLAB, self.ring.siblings()))

    def pieces(self):
        return self.own + self.kept + self.other


class Scatter:
    def __init__(self, ring, own, kept, sent):
        self.ring, self.own, self.kept = ring, own, kept
        self.other = lax.ppermute(sent, SLAB, ring.siblings())
        self.held = None
        self.left = list(ring.steps())
        self.end = kept.shape[0]

    def step(self):
        count = 2 if self.left.pop()[1] else 1
        self.end -= count
        total = self.kept[self.end : self.end + count].astype(F32) + self.other[self.end : self.end + count].astype(F32)
        if self.held is not None:
            got = self.held.astype(F32)
            if got.shape[0] < count:
                total = jnp.concatenate([total[:1] + got, total[1:]], axis=0)
            else:
                total = total + got
        self.held = lax.ppermute(total.astype(BF16), SLAB, self.ring.perm())
        return self.held

    def chip(self):
        return self.own.astype(F32) + self.held.astype(F32)


def nt_dot(a, b):
    return lax.dot_general(a, b, (((1,), (1,)), ((), ())), preferred_element_type=F32)


def nn_dot(a, b):
    return lax.dot_general(a, b, (((1,), (0,)), ((), ())), preferred_element_type=F32)


def gradient_kernel(images, coils, slabs, *refs):
    held_images, refs = refs[:images], refs[images:]
    maps, refs = refs[:coils], refs[coils:]
    measured, sampling, tables = refs[:3]
    out, products, backs = refs[3:6], refs[6], refs[7]
    ty_f, tz_f, tz_i, ty_i = [0, 1, 2], [3, 4], [5, 6], [7, 8, 9]
    rows, ny = held_images[0].shape[-2:]
    nz = sampling.shape[-1]
    count, half = nz // rows, rows // 2
    my, mz = ny // 3, nz // 2
    first = slabs[2 * count]
    root = math.sqrt(0.75)

    def pieces(arrays):
        return [(array, i) for array in arrays for i in range(array.shape[0])]

    def places(slab):
        at = pl.multiple_of(slab * half, half)
        return pl.ds(at, half), pl.ds(pl.multiple_of(at + mz, half), half)

    def thirds(b0, b1, b2, sign):
        add = [u + v for u, v in zip(b1, b2)]
        low = [u - 0.5 * v for u, v in zip(b0, add)]
        turn = [(sign * root) * (u - v) for u, v in zip(b1, b2)]
        return (
            (b0[0] + add[0], b0[1] + add[1]),
            (low[0] - turn[1], low[1] + turn[0]),
            (low[0] + turn[1], low[1] - turn[0]),
        )

    def product(c):
        for k, (held, i) in enumerate(pieces(held_images)):
            slab = slabs[k]
            real = held[i, 0].astype(F32)
            imag = held[i, 1].astype(F32)
            m_real = maps[c][slab, 0, 0].astype(F32)
            m_imag = maps[c][slab, 0, 1].astype(F32)
            p_real = m_real * real - m_imag * imag
            p_imag = m_real * imag + m_imag * real
            for parity, at in enumerate(places(slab)):
                lines = slice(parity * half, (parity + 1) * half)
                for j in range(3):
                    cells = slice(j * my, (j + 1) * my)
                    products[c, j, at, :my] = p_real[lines, cells]
                    products[c, j, at, my:] = p_imag[lines, cells]

    def to_frequency_y(c):
        return [nt_dot(tables[ty_f[j]], products[c, j].astype(BF16)) for j in range(3)]

    def spectra_of(parts):
        parts = thirds(*[(part[:my], part[my:]) for part in parts], -1.0)
        return [jnp.concatenate([part[q].astype(BF16) for part in parts], axis=0) for q in range(2)]

    def to_frequency_z(spectra):
        halves = []
        for j in range(2):
            cells = slice(j * mz, (j + 1) * mz)
            halves.append(nn_dot(jnp.concatenate([spectra[0][:, cells], spectra[1][:, cells]], axis=1), tables[tz_f[j]]))
        return halves

    def residual_of(c, halves):
        coil = first if c == 0 else 1 - first
        mask = sampling[0, 0].astype(F32)
        sums, differences = [], []
        for q in range(2):
            cells = slice(q * mz, (q + 1) * mz)
            seen = measured[0, coil, 0, q, 0].astype(F32)
            low = mask[:, :mz] * (halves[0][:, cells] + halves[1][:, cells] - seen[:, :mz])
            high = mask[:, mz:] * (halves[0][:, cells] - halves[1][:, cells] - seen[:, mz:])
            sums.append((low + high).astype(BF16))
            differences.append((low - high).astype(BF16))
        return jnp.concatenate(sums, axis=1), jnp.concatenate(differences, axis=1)

    def to_depth(folds):
        return [nt_dot(tables[tz_i[j]], folds[j]) for j in range(2)]

    def lines_of(depths):
        lines = [[], [], []]
        for j in range(2):
            cut = lambda q, i: depths[j][q * mz : (q + 1) * mz, i * my : (i + 1) * my]
            turned = thirds(*[(cut(0, i), cut(1, i)) for i in range(3)], 1.0)
            for i in range(3):
                lines[i].append(jnp.concatenate([turned[i][0].astype(BF16), turned[i][1].astype(BF16)], axis=1))
        return [jnp.concatenate(line, axis=0) for line in lines]

    def to_image(c, lines):
        for i in range(3):
            backs[c, i] = nn_dot(lines[i], tables[ty_i[i]])

    stages = [
        lambda c, _: product(c),
        lambda c, _: to_frequency_y(c),
        lambda c, value: spectra_of(value),
        lambda c, value: to_frequency_z(value),
        lambda c, value: residual_of(c, value),
        lambda c, value: to_depth(value),
        lambda c, value: lines_of(value),
        lambda c, value: to_image(c, value),
    ]
    held_values = [None] * coils
    for step in range(len(stages) + coils - 1):
        for c in range(coils):
            if 0 <= step - c < len(stages):
                held_values[c] = stages[step - c](c, held_values[c])
    for k, (held, i) in enumerate(pieces(out)):
        slab = slabs[count + k]
        for j in range(3):
            cells = slice(j * my, (j + 1) * my)
            real, imag = 0.0, 0.0
            for c in range(coils):
                m_real = maps[c][slab, 0, 0, :, cells].astype(F32)
                m_imag = maps[c][slab, 0, 1, :, cells].astype(F32)
                back = jnp.concatenate([backs[c, j, at, :] for at in places(slab)], axis=0)
                real += m_real * back[:, :my] + m_imag * back[:, my:]
                imag += m_real * back[:, my:] - m_imag * back[:, :my]
            held[i, 0, :, cells] = real.astype(BF16)
            held[i, 1, :, cells] = imag.astype(BF16)


def gradient(where, images, maps, measured, sampling, tables, x):
    _, channels, rows, ny = images[0].shape
    nz = sampling.shape[-1]
    n = len(maps)
    far = (nz // rows - 2) // 2
    whole = lambda a: pl.BlockSpec(a.shape, lambda e, s: (0,) * a.ndim, pipeline_mode=pl.Buffered(1))
    flops = channels * n * 2 * 4 * (nz * ny * ny + nz * nz * ny)
    return pl.pallas_call(
        functools.partial(gradient_kernel, len(images), n),
        grid_spec=pltpu.PrefetchScalarGridSpec(
            num_scalar_prefetch=1,
            grid=(channels // 2,),
            in_specs=[pl.BlockSpec((a.shape[0], 2, rows, ny), lambda e, s: (0, e, 0, 0)) for a in images]
            + [
                pl.BlockSpec((a.shape[0], 1, 2, rows, ny), functools.partial(lambda at, e, s: (0, at, 0, 0, 0), at),
                             pipeline_mode=pl.Buffered(1))
                for a, at in maps
            ]
            + [
                pl.BlockSpec((1, 2, 1, 2, 1, ny, nz), lambda e, s: (0, 0, e, 0, x, 0, 0)),
                pl.BlockSpec((1, 1, ny, nz), lambda e, s: (0, e, 0, 0)),
            ]
            + [whole(tables)],
            out_specs=[pl.BlockSpec((m, 2, rows, ny), lambda e, s: (0, e, 0, 0)) for m in (2, far, far)],
            scratch_shapes=[
                pltpu.VMEM((n, 3, nz, 2 * ny // 3), F32),
                pltpu.VMEM((n, 3, nz, 2 * ny // 3), F32),
            ],
        ),
        out_shape=[jax.ShapeDtypeStruct((m, channels, rows, ny), BF16) for m in (2, far, far)],
        compiler_params=pltpu.CompilerParams(vmem_limit_bytes=40 * 2**20),
        cost_estimate=pl.CostEstimate(flops=flops, bytes_accessed=8 * 2**20, transcendentals=0),
        name="gradient",
    )(where, *images, *[a for a, _ in maps], measured, sampling, tables)


def reordered(value, along_z, along_y):
    n, rows, ny = value.shape
    block = along_z.shape[0]
    flat = nn_dot(value.reshape(n * rows, ny), along_y).astype(BF16)
    out = []
    for start in range(0, n * rows, block):
        size = min(block, n * rows - start)
        out.append(nn_dot(along_z[:size, :size], flat[start : start + size]).astype(BF16))
    return jnp.concatenate(out, axis=0).reshape(n, rows, ny)


def orders(rows, ny, back):
    z, y = order(rows, 2), order(ny, 3)
    along_z = np.kron(np.eye(8, dtype=np.float32), z if back else z.T)
    return jnp.asarray(along_z, BF16), jnp.asarray(y.T if back else y, BF16)


def prepare_image_kernel(image, along_z, along_y, earlier, out):
    width, channels, rows, ny = out.shape
    picked = image[...].reshape((channels, width, rows, ny))
    for x in range(width):
        out[x] = reordered(picked[:, x], along_z[...], along_y[...])


def prepare_image(current_image, earlier):
    _, encodings, _, width, rows, ny = current_image.shape
    vmem = pl.BlockSpec(memory_space=pltpu.VMEM)
    return pl.pallas_call(
        prepare_image_kernel,
        in_specs=[vmem, vmem, vmem, pl.BlockSpec(memory_space=pl.ANY)],
        out_specs=vmem,
        out_shape=jax.ShapeDtypeStruct((width, 2 * encodings, rows, ny), BF16),
        compiler_params=pltpu.CompilerParams(vmem_limit_bytes=16 * 2**20),
        name="prepare_image",
    )(current_image, *orders(rows, ny, False), earlier)


def prepare_maps_kernel(which, maps, along_z, along_y, out):
    count, width, _, rows, ny = out.shape
    value = reordered(maps[:, 0].reshape((count * 2 * width, rows, ny)), along_z[...], along_y[...])
    for pair in range(count):
        for x in range(width):
            for part in range(2):
                out[pair, x, part] = value[(pair * 2 + part) * width + x]


def prepare_maps(which, coil_maps):
    coils, _, width, rows, ny = coil_maps.shape
    devices = coils // 2
    pairs = coil_maps.reshape((devices, 2) + coil_maps.shape[1:])
    matrices = orders(rows, ny, False)
    steps = 2
    return pl.pallas_call(
        prepare_maps_kernel,
        grid_spec=pltpu.PrefetchScalarGridSpec(
            num_scalar_prefetch=1,
            grid=(steps,),
            in_specs=[pl.BlockSpec((devices // steps, 1) + coil_maps.shape[1:], lambda i, t: (i, t[0], 0, 0, 0, 0))]
            + [pl.BlockSpec(m.shape, lambda i, t: (0, 0)) for m in matrices],
            out_specs=pl.BlockSpec((devices // steps, width, 2, rows, ny), lambda i, t: (i, 0, 0, 0, 0)),
        ),
        out_shape=jax.ShapeDtypeStruct((devices, width, 2, rows, ny), BF16),
        compiler_params=pltpu.CompilerParams(vmem_limit_bytes=58 * 2**20),
        name="prepare_maps",
    )(which, pairs, *matrices)


def update_kernel(image, chip, received, along_z, along_y, out):
    for x in range(image.shape[0]):
        value = image[x].astype(F32) - (chip[x] + received[x].astype(F32))
        out[x] = reordered(value.astype(BF16), along_z[...], along_y[...])


def update(image, chip, received):
    vmem = pl.BlockSpec(memory_space=pltpu.VMEM)
    return pl.pallas_call(
        update_kernel,
        in_specs=[vmem] * 5,
        out_specs=vmem,
        out_shape=jax.ShapeDtypeStruct(image.shape, BF16),
        compiler_params=pltpu.CompilerParams(vmem_limit_bytes=16 * 2**20),
        name="update",
    )(image, chip, received, *orders(*image.shape[-2:], True))


def shifted(value, step):
    rows = value.shape[:-1]
    edge = jnp.zeros(rows + (1,), value.dtype)
    if step > 0:
        return jnp.concatenate([value[..., 1:], edge], axis=-1)
    return jnp.concatenate([edge, value[..., :-1]], axis=-1)


def put_strided(ref, start, count, stride, value):
    for j in range(ref.shape[0]):
        ref[j, pl.ds(start, count, stride=stride), :] = value[:, j * 128 : (j + 1) * 128]


def get_lines(ref, start, count):
    return jnp.concatenate([ref[j, start : start + count, :] for j in range(ref.shape[0])], axis=1)


def convolution_kernel(ends, *refs):
    sources, refs = refs[:2], refs[2:]
    w_first, b_first, w_second, b_second, out, stacked, result = refs
    channels, depth, ny = sources[0].shape
    rows = depth - 4
    group = stacked.shape[1] // depth
    lanes = result.shape[1] // rows
    stacked[...] = jnp.zeros_like(stacked)
    for t, source in enumerate(sources):
        for i in range(channels):
            value = source[i].astype(F32)
            for d in range(3):
                line = value if d == 1 else shifted(value, d - 1)
                put_strided(stacked, (d * 2 + t) * channels + i, depth, group, line)
    features = w_first.shape[0] // 2
    taps = w_second.shape[0] // 4
    partial = []
    for pair in range(rows // 2 + 1):
        window = get_lines(stacked, 2 * pair * group, 4 * group).astype(BF16)
        hidden = jnp.maximum(nn_dot(w_first[...], window) + b_first[...], 0.0)
        if pair == 0:
            hidden = jnp.concatenate([hidden[:features] * ends[0].astype(F32), hidden[features:]], axis=0)
        if pair == rows // 2:
            hidden = jnp.concatenate([hidden[:features], hidden[features:] * ends[1].astype(F32)], axis=0)
        partial.append(nn_dot(w_second[...], hidden.astype(BF16)))
        if pair > 0:
            for z in range(2):
                total = partial[0][(2 + z) * taps : (3 + z) * taps] + partial[1][z * taps : (z + 1) * taps]
                line = shifted(total[:lanes], -1) + total[lanes : 2 * lanes] + shifted(total[2 * lanes :], 1)
                put_strided(result, 2 * pair - 2 + z, lanes, rows, line)
            partial = partial[1:]
    for i in range(channels):
        value = sources[0][i].astype(F32)[2 : 2 + rows]
        out[i] = (value + get_lines(result, i * rows, rows) + b_second[i]).astype(BF16)


def convolutions(ends, own, other, w_first, b_first, w_second, b_second):
    channels, depth, ny = own.shape
    rows = depth - 4
    group = w_first.shape[1] // 4
    lanes = w_second.shape[0] // 12
    vmem = pl.BlockSpec(memory_space=pltpu.VMEM)
    smem = pl.BlockSpec(memory_space=pltpu.SMEM)
    flops = (rows + 2) * ny * (w_first.size + w_second.size)
    return pl.pallas_call(
        convolution_kernel,
        in_specs=[smem, vmem, vmem, vmem, vmem, vmem, smem],
        out_specs=vmem,
        out_shape=jax.ShapeDtypeStruct((channels, rows, ny), BF16),
        scratch_shapes=[
            pltpu.VMEM((ny // 128, depth * group, 128), F32),
            pltpu.VMEM((ny // 128, lanes * rows, 128), F32),
        ],
        compiler_params=pltpu.CompilerParams(vmem_limit_bytes=24 * 2**20),
        cost_estimate=pl.CostEstimate(flops=flops, bytes_accessed=2**20, transcendentals=0),
        name="convolutions",
    )(ends, own, other, w_first, b_first, w_second, b_second)


def round_up(value, unit):
    return -(-value // unit) * unit


def convolution_weights(first_weight, first_bias, second_weight):
    q = lax.axis_index(COIL)
    ahead = 2 - 2 * q
    behind = 2 * q

    def tap(weight, index):
        return lax.dynamic_index_in_dim(weight, index, axis=2, keepdims=False)

    feat, channels = first_weight.shape[:2]
    same, of_other, of_own = (tap(first_weight, i) for i in (1, ahead, behind))
    first = jnp.stack([jnp.stack([same, of_other], 1), jnp.stack([of_own, same], 1)], 0)
    first = first.transpose(0, 1, 4, 5, 2, 3).reshape(2 * feat, 3, 6 * channels)
    group = round_up(6 * channels, 16)
    first = jnp.pad(first, ((0, 0), (0, 0), (0, group - 6 * channels))).reshape(2 * feat, 3 * group)
    first = jnp.concatenate([jnp.pad(first, ((0, 0), (0, group))), jnp.pad(first, ((0, 0), (group, 0)))], axis=0)
    bias = jnp.concatenate([first_bias] * 4)[:, None]
    second = jnp.stack([tap(second_weight, 1), tap(second_weight, ahead)], 1)
    second = second.transpose(3, 4, 0, 1, 2).reshape(3, 3, channels, 2 * feat)
    lanes = round_up(channels, 8)
    second = jnp.pad(second, ((0, 0), (0, 0), (0, lanes - channels), (0, 0))).reshape(3, 3 * lanes, 2 * feat)
    none = jnp.zeros_like(second[0])
    line = lambda u: jnp.concatenate([second[u + 2 - r] if 0 <= u + 2 - r <= 2 else none for r in range(4)], axis=0)
    return first, bias, jnp.concatenate([line(0), line(1)], axis=1)


def paired(current_image, coil_maps, measured, sampling, first_weight, first_bias, second_weight, second_bias):
    devices = lax.axis_size(SLAB)
    ring = Ring(devices)
    me, q = lax.axis_index(SLAB), lax.axis_index(COIL)
    _, encodings, _, width, rows, ny = current_image.shape
    nz = rows * devices
    channels = 2 * encodings
    tables = jnp.asarray(
        np.concatenate(
            [
                split_tables(ny, 3, True, False),
                split_tables(nz, 2, False, False),
                split_tables(nz, 2, True, True),
                split_tables(ny, 3, False, True),
            ]
        )
    )
    which = q[None].astype(jnp.int32)
    where = jnp.concatenate([ring.slabs(), which])
    swap = [(0, 1), (1, 0)]
    mask = sampling.astype(BF16)
    weights = convolution_weights(first_weight, first_bias, second_weight)
    ends = jnp.stack([me > 0, me < devices - 1]).astype(jnp.int32)

    pairs = prepare_maps(which, coil_maps)
    images = prepare_image(current_image, pairs)
    gathers = [Gather(ring, images[x : x + 1]) for x in range(width)]
    kept = lax.all_to_all(pairs, SLAB, split_axis=0, concat_axis=0, tiled=True)
    halves = [kept[:, x : x + 1] for x in range(width)]
    for step in range(len(ring.steps())):
        for gather in gathers:
            gather.step(*(weights + (mask,) if step == 1 else (halves[step - 2],) if 2 <= step < 2 + width else ()))
    swapped = [lax.ppermute(half, COIL, swap) for half in halves]
    scatters = []
    for x in range(width):
        scatters.append(Scatter(ring, *gradient(where, gathers[x].pieces(), [(kept, x), (swapped[x], 0)], measured, mask, tables, x)))
    for _ in ring.steps():
        for scatter in scatters:
            scatter.step()
    chip = jnp.stack([scatter.chip() for scatter in scatters])
    updated = update(images, chip[:, 0], lax.ppermute(chip[:, 1].astype(BF16), SLAB, ring.siblings()))
    up = [(i, i + 1) for i in range(devices - 1)]
    down = [(i + 1, i) for i in range(devices - 1)]
    before = lax.ppermute(updated[:, :, rows - 2 :], SLAB, up)
    behind = lax.ppermute(updated[:, :, :2], SLAB, down)
    refined = []
    for x in range(width):
        bordered = jnp.concatenate([before[x], updated[x], behind[x]], axis=1)
        refined.append(convolutions(ends, bordered, lax.ppermute(bordered, COIL, swap), *weights, second_bias))
    return jnp.stack(refined, axis=1).reshape(current_image.shape)


def with_halo(cells, sides, width):
    for axis, dim in sides:
        count = lax.axis_size(axis)
        ends = count - 1
        head = lax.slice_in_dim(cells, 0, width, axis=dim)
        tail = lax.slice_in_dim(cells, cells.shape[dim] - width, cells.shape[dim], axis=dim)
        cells = jnp.concatenate(
            [
                lax.ppermute(tail, axis, [(i, (i + 1) % count) for i in range(ends)]),
                cells,
                lax.ppermute(head, axis, [((i + 1) % count, i) for i in range(ends)]),
            ],
            axis=dim,
        )
    return cells


def plain_table(length, inverse):
    indices = jnp.arange(length, dtype=jnp.int32)
    wrapped = indices[:, None] * indices[None, :] % length
    angles = wrapped.astype(jnp.float32) * (2.0 * math.pi / length)
    factor = 1.0 / math.sqrt(length)
    cosine = jnp.cos(angles) * factor
    sine_part = jnp.sin(angles) * factor
    phase_sign = 1.0 if inverse else -1.0
    upper_rows = jnp.stack([cosine, phase_sign * sine_part], axis=1)
    lower_rows = jnp.stack([-phase_sign * sine_part, cosine], axis=1)
    return jnp.stack([upper_rows, lower_rows], axis=0).astype(jnp.bfloat16)


def coil_products(maps_part, image_part):
    maps_real = maps_part[:, 0][None, :, None].astype(jnp.float32)
    maps_imaginary = maps_part[:, 1][None, :, None].astype(jnp.float32)
    image_real = image_part[:, :, 0][:, None].astype(jnp.float32)
    image_imaginary = image_part[:, :, 1][:, None].astype(jnp.float32)
    real_part = maps_real * image_real - maps_imaginary * image_imaginary
    imaginary_part = maps_real * image_imaginary + maps_imaginary * image_real
    return jnp.stack([real_part, imaginary_part], axis=3).astype(jnp.bfloat16)


def transform(operand, matrix):
    return jnp.einsum("pcerxzy,ryqk->pceqxzk", operand, matrix, preferred_element_type=jnp.float32)


def combine_coils(maps_part, values):
    maps_real = maps_part[:, 0][None, :, None].astype(jnp.float32)
    maps_imaginary = maps_part[:, 1][None, :, None].astype(jnp.float32)
    real_sum = jnp.sum(maps_real * values[:, :, :, 0] + maps_imaginary * values[:, :, :, 1], axis=1)
    imaginary_sum = jnp.sum(
        maps_real * values[:, :, :, 1] - maps_imaginary * values[:, :, :, 0], axis=1
    )
    return jnp.stack([real_sum, imaginary_sum], axis=2)


def convolve(operand, weights):
    widened = jnp.pad(operand, ((0, 0), (0, 0), (0, 0), (0, 0), (1, 1)))
    return lax.conv_general_dilated(
        widened,
        weights,
        (1, 1, 1),
        "VALID",
        dimension_numbers=("DCNHW", "OIDHW", "DCNHW"),
        preferred_element_type=jnp.float32,
    )


def on_device(
    current_image,
    coil_maps,
    measured,
    sampling,
    first_weight,
    first_bias,
    second_weight,
    second_bias,
):
    depth = current_image.shape[4] * lax.axis_size("slab")
    forward_y = plain_table(current_image.shape[5], False)
    inverse_y = plain_table(current_image.shape[5], True)
    forward_z = plain_table(depth, False)
    inverse_z = plain_table(depth, True)
    sampled = sampling.astype(jnp.float32)[:, None, :, None, None]
    local_maps = lax.all_to_all(coil_maps, "slab", split_axis=0, concat_axis=3, tiled=True)
    row_spectra = transform(
        coil_products(local_maps, lax.all_gather(current_image, "slab", axis=4, tiled=True)),
        forward_y,
    ).astype(jnp.bfloat16)
    residual = (
        sampled
        * (
            jnp.einsum(
                "pcerxzk,rzqj->pceqxkj", row_spectra, forward_z, preferred_element_type=jnp.float32
            )
            - measured.astype(jnp.float32)
        )
    ).astype(jnp.bfloat16)
    depth_back = jnp.einsum(
        "pcerxkj,rjqz->pceqxzk", residual, inverse_z, preferred_element_type=jnp.float32
    ).astype(jnp.bfloat16)
    partial_sum = combine_coils(local_maps, transform(depth_back, inverse_y))
    gradient = lax.psum_scatter(
        partial_sum.astype(jnp.bfloat16), "slab", scatter_dimension=4, tiled=True
    ).astype(jnp.float32)
    updated = (current_image.astype(jnp.float32) - gradient).astype(jnp.bfloat16)
    stacked = updated.reshape((updated.shape[0], 2 * updated.shape[1]) + updated.shape[3:])
    bias_first = first_bias[None, :, None, None, None]
    bordered = with_halo(stacked, (("slab", 3), ("coil", 0)), 1)
    hidden = jax.nn.relu(convolve(bordered, first_weight) + bias_first).astype(jnp.bfloat16)
    bordered_hidden = with_halo(hidden, (("slab", 3), ("coil", 0)), 1)
    second = convolve(bordered_hidden, second_weight)
    refined = stacked.astype(jnp.float32) + second + second_bias[None, :, None, None, None]
    return refined.astype(jnp.bfloat16).reshape(updated.shape)


def fits(shape, devices):
    rows, ny = shape[4:]
    return rows % 16 == 0 and ny % 384 == 0 and 2 * ny == 3 * rows * devices


def solution(mesh):
    devices, phases = mesh.shape[SLAB], mesh.shape[COIL]

    def per_device(*args):
        coils, phase = args[2].shape[1], args[0].shape[0]
        if phases == 2 and coils == 2 and phase == 1 and devices % 4 == 0 and fits(args[0].shape, devices):
            return paired(*args)
        return on_device(*args)

    in_specs = (
        P("coil", None, None, None, "slab", None),
        P(None, None, None, "slab", None),
        P("coil", "slab", None, None, None, None, None),
        P("coil", None, None, None),
        P(),
        P(),
        P(),
        P(),
    )
    out_specs = P("coil", None, None, None, "slab", None)
    return jax.shard_map(
        per_device, mesh=mesh, in_specs=in_specs, out_specs=out_specs, check_vma=False
    )
```

```python
import functools
import math

import jax
import jax.numpy as jnp
import ml_dtypes
import numpy as np
from jax import lax
from jax.experimental import pallas as pl
from jax.experimental.pallas import tpu as pltpu
from jax.sharding import PartitionSpec as P

BF16 = jnp.bfloat16
F32 = jnp.float32
SLAB, COIL = "slab", "coil"


def dft_table(length, inverse):
    indices = np.arange(length, dtype=np.int64)
    wrapped = indices[:, None] * indices[None, :] % length
    angles = wrapped.astype(np.float32) * np.float32(2.0 * math.pi / length)
    factor = np.float32(1.0 / math.sqrt(length))
    cosine = np.cos(angles) * factor
    sine = np.sin(angles) * factor
    sign = np.float32(1.0 if inverse else -1.0)
    upper = np.stack([cosine, sign * sine], axis=1)
    lower = np.stack([-sign * sine, cosine], axis=1)
    return np.stack([upper, lower], axis=0).astype(ml_dtypes.bfloat16)


def split_tables(length, count, left, inverse):
    table = dft_table(length, inverse)
    part = length // count
    out = []
    for s in range(count):
        if inverse:
            piece = table[:, :part, :, s::count]
        else:
            piece = table[:, s::count, :, :part]
        if left:
            piece = piece.transpose(2, 3, 0, 1)
        out.append(piece.reshape(2 * part, 2 * part))
    return np.stack(out)


def order(length, count):
    taken = np.arange(length).reshape(-1, count).T.reshape(-1)
    return np.eye(length, dtype=np.float32)[:, taken]


class Ring:
    def __init__(self, devices):
        self.devices = devices
        self.chips = devices // 2
        self.half = self.chips // 2
        column = self.chips // 2
        self.order = [2 * i for i in range(column)] + [2 * i + 1 for i in reversed(range(column))]

    def perm(self):
        pairs = []
        for i in range(self.chips):
            for core, step in ((0, 1), (1, -1)):
                pairs.append((2 * self.order[i] + core, 2 * self.order[(i + step) % self.chips] + core))
        return pairs

    def siblings(self):
        return [(i, i ^ 1) for i in range(self.devices)]

    def steps(self):
        return [(step, True) for step in range(1, self.half)] + [(self.half, False)]

    def slabs(self):
        me = lax.axis_index(SLAB)
        chip, core = me // 2, me % 2
        column = self.chips // 2
        row = chip // 2
        place = jnp.where(chip % 2 == 0, row, self.chips - 1 - row)

        def slab(offset, parity):
            at = (place + offset + self.chips) % self.chips
            return 2 * jnp.where(at < column, 2 * at, 2 * (self.chips - 1 - at) + 1) + parity

        def handled(by, sign):
            way = sign * (1 - 2 * by)
            out = []
            for step, both in self.steps():
                out += [slab(way * step, by)] + ([slab(way * step, 1 - by)] if both else [])
            return out

        own = [slab(0, core), slab(0, 1 - core)]
        gathered = own + handled(core, -1) + handled(1 - core, -1)
        summed = own + handled(core, 1) + handled(1 - core, 1)
        return jnp.stack(gathered + summed).astype(jnp.int32)


def after(value, *earlier):
    return lax.optimization_barrier((value,) + earlier)[0]


class Gather:
    def __init__(self, ring, mine):
        self.ring = ring
        self.first = lax.ppermute(mine, SLAB, ring.perm())
        self.own = [mine, lax.ppermute(mine, SLAB, ring.siblings())]
        self.held = None
        self.kept, self.other = [], []

    def step(self, *earlier):
        both = self.ring.steps()[len(self.kept)][1]
        if self.held is None:
            self.held = jnp.concatenate([self.first, lax.ppermute(self.own[1], SLAB, self.ring.perm())], axis=0)
        else:
            held = self.held if both else self.held[:1]
            self.held = lax.ppermute(after(held, *earlier) if earlier else held, SLAB, self.ring.perm())
        self.kept.append(self.held)
        self.other.append(lax.ppermute(self.held, SLAB, self.ring.siblings()))

    def pieces(self):
        return self.own + self.kept + self.other


class Scatter:
    def __init__(self, ring, own, kept, sent):
        self.ring, self.own, self.kept = ring, own, kept
        self.other = lax.ppermute(sent, SLAB, ring.siblings())
        self.held = None
        self.left = list(ring.steps())
        self.end = kept.shape[0]

    def step(self):
        count = 2 if self.left.pop()[1] else 1
        self.end -= count
        total = self.kept[self.end : self.end + count].astype(F32) + self.other[self.end : self.end + count].astype(F32)
        if self.held is not None:
            got = self.held.astype(F32)
            if got.shape[0] < count:
                total = jnp.concatenate([total[:1] + got, total[1:]], axis=0)
            else:
                total = total + got
        self.held = lax.ppermute(total.astype(BF16), SLAB, self.ring.perm())
        return self.held

    def chip(self):
        return self.own.astype(F32) + self.held.astype(F32)


def nt_dot(a, b):
    return lax.dot_general(a, b, (((1,), (1,)), ((), ())), preferred_element_type=F32)


def nn_dot(a, b):
    return lax.dot_general(a, b, (((1,), (0,)), ((), ())), preferred_element_type=F32)


def gradient_kernel(images, coils, slabs, *refs):
    held_images, refs = refs[:images], refs[images:]
    maps, refs = refs[:coils], refs[coils:]
    measured, sampling, tables = refs[:3]
    out, products, backs = refs[3:6], refs[6], refs[7]
    ty_f, tz_f, tz_i, ty_i = [0, 1, 2], [3, 4], [5, 6], [7, 8, 9]
    rows, ny = held_images[0].shape[-2:]
    nz = sampling.shape[-1]
    count, half = nz // rows, rows // 2
    my, mz = ny // 3, nz // 2
    first = slabs[2 * count]
    root = math.sqrt(0.75)

    def pieces(arrays):
        return [(array, i) for array in arrays for i in range(array.shape[0])]

    def places(slab):
        at = pl.multiple_of(slab * half, half)
        return pl.ds(at, half), pl.ds(pl.multiple_of(at + mz, half), half)

    def thirds(b0, b1, b2, sign):
        add = [u + v for u, v in zip(b1, b2)]
        low = [u - 0.5 * v for u, v in zip(b0, add)]
        turn = [(sign * root) * (u - v) for u, v in zip(b1, b2)]
        return (
            (b0[0] + add[0], b0[1] + add[1]),
            (low[0] - turn[1], low[1] + turn[0]),
            (low[0] + turn[1], low[1] - turn[0]),
        )

    def product(c):
        for k, (held, i) in enumerate(pieces(held_images)):
            slab = slabs[k]
            real = held[i, 0].astype(F32)
            imag = held[i, 1].astype(F32)
            m_real = maps[c][slab, 0, 0].astype(F32)
            m_imag = maps[c][slab, 0, 1].astype(F32)
            p_real = m_real * real - m_imag * imag
            p_imag = m_real * imag + m_imag * real
            for parity, at in enumerate(places(slab)):
                lines = slice(parity * half, (parity + 1) * half)
                for j in range(3):
                    cells = slice(j * my, (j + 1) * my)
                    products[c, j, at, :my] = p_real[lines, cells]
                    products[c, j, at, my:] = p_imag[lines, cells]

    def to_frequency_y(c):
        return [nt_dot(tables[ty_f[j]], products[c, j].astype(BF16)) for j in range(3)]

    def spectra_of(parts):
        parts = thirds(*[(part[:my], part[my:]) for part in parts], -1.0)
        return [jnp.concatenate([part[q].astype(BF16) for part in parts], axis=0) for q in range(2)]

    def to_frequency_z(spectra):
        halves = []
        for j in range(2):
            cells = slice(j * mz, (j + 1) * mz)
            halves.append(nn_dot(jnp.concatenate([spectra[0][:, cells], spectra[1][:, cells]], axis=1), tables[tz_f[j]]))
        return halves

    def residual_of(c, halves):
        coil = first if c == 0 else 1 - first
        mask = sampling[0, 0].astype(F32)
        sums, differences = [], []
        for q in range(2):
            cells = slice(q * mz, (q + 1) * mz)
            seen = measured[0, coil, 0, q, 0].astype(F32)
            low = mask[:, :mz] * (halves[0][:, cells] + halves[1][:, cells] - seen[:, :mz])
            high = mask[:, mz:] * (halves[0][:, cells] - halves[1][:, cells] - seen[:, mz:])
            sums.append((low + high).astype(BF16))
            differences.append((low - high).astype(BF16))
        return jnp.concatenate(sums, axis=1), jnp.concatenate(differences, axis=1)

    def to_depth(folds):
        return [nt_dot(tables[tz_i[j]], folds[j]) for j in range(2)]

    def lines_of(depths):
        lines = [[], [], []]
        for j in range(2):
            cut = lambda q, i: depths[j][q * mz : (q + 1) * mz, i * my : (i + 1) * my]
            turned = thirds(*[(cut(0, i), cut(1, i)) for i in range(3)], 1.0)
            for i in range(3):
                lines[i].append(jnp.concatenate([turned[i][0].astype(BF16), turned[i][1].astype(BF16)], axis=1))
        return [jnp.concatenate(line, axis=0) for line in lines]

    def to_image(c, lines):
        for i in range(3):
            backs[c, i] = nn_dot(lines[i], tables[ty_i[i]])

    stages = [
        lambda c, _: product(c),
        lambda c, _: to_frequency_y(c),
        lambda c, value: spectra_of(value),
        lambda c, value: to_frequency_z(value),
        lambda c, value: residual_of(c, value),
        lambda c, value: to_depth(value),
        lambda c, value: lines_of(value),
        lambda c, value: to_image(c, value),
    ]
    held_values = [None] * coils
    for step in range(len(stages) + coils - 1):
        for c in range(coils):
            if 0 <= step - c < len(stages):
                held_values[c] = stages[step - c](c, held_values[c])
    for k, (held, i) in enumerate(pieces(out)):
        slab = slabs[count + k]
        for j in range(3):
            cells = slice(j * my, (j + 1) * my)
            real, imag = 0.0, 0.0
            for c in range(coils):
                m_real = maps[c][slab, 0, 0, :, cells].astype(F32)
                m_imag = maps[c][slab, 0, 1, :, cells].astype(F32)
                back = jnp.concatenate([backs[c, j, at, :] for at in places(slab)], axis=0)
                real += m_real * back[:, :my] + m_imag * back[:, my:]
                imag += m_real * back[:, my:] - m_imag * back[:, :my]
            held[i, 0, :, cells] = real.astype(BF16)
            held[i, 1, :, cells] = imag.astype(BF16)


def gradient(where, images, maps, measured, sampling, tables, x):
    _, channels, rows, ny = images[0].shape
    nz = sampling.shape[-1]
    n = len(maps)
    far = (nz // rows - 2) // 2
    whole = lambda a: pl.BlockSpec(a.shape, lambda e, s: (0,) * a.ndim, pipeline_mode=pl.Buffered(1))
    flops = channels * n * 2 * 4 * (nz * ny * ny + nz * nz * ny)
    return pl.pallas_call(
        functools.partial(gradient_kernel, len(images), n),
        grid_spec=pltpu.PrefetchScalarGridSpec(
            num_scalar_prefetch=1,
            grid=(channels // 2,),
            in_specs=[pl.BlockSpec((a.shape[0], 2, rows, ny), lambda e, s: (0, e, 0, 0)) for a in images]
            + [
                pl.BlockSpec((a.shape[0], 1, 2, rows, ny), functools.partial(lambda at, e, s: (0, at, 0, 0, 0), at),
                             pipeline_mode=pl.Buffered(1))
                for a, at in maps
            ]
            + [
                pl.BlockSpec((1, 2, 1, 2, 1, ny, nz), lambda e, s: (0, 0, e, 0, x, 0, 0)),
                pl.BlockSpec((1, 1, ny, nz), lambda e, s: (0, e, 0, 0)),
            ]
            + [whole(tables)],
            out_specs=[pl.BlockSpec((m, 2, rows, ny), lambda e, s: (0, e, 0, 0)) for m in (2, far, far)],
            scratch_shapes=[
                pltpu.VMEM((n, 3, nz, 2 * ny // 3), F32),
                pltpu.VMEM((n, 3, nz, 2 * ny // 3), F32),
            ],
        ),
        out_shape=[jax.ShapeDtypeStruct((m, channels, rows, ny), BF16) for m in (2, far, far)],
        compiler_params=pltpu.CompilerParams(vmem_limit_bytes=40 * 2**20),
        cost_estimate=pl.CostEstimate(flops=flops, bytes_accessed=8 * 2**20, transcendentals=0),
        name="gradient",
    )(where, *images, *[a for a, _ in maps], measured, sampling, tables)


def reordered(value, along_z, along_y):
    n, rows, ny = value.shape
    block = along_z.shape[0]
    flat = nn_dot(value.reshape(n * rows, ny), along_y).astype(BF16)
    out = []
    for start in range(0, n * rows, block):
        size = min(block, n * rows - start)
        out.append(nn_dot(along_z[:size, :size], flat[start : start + size]).astype(BF16))
    return jnp.concatenate(out, axis=0).reshape(n, rows, ny)


def orders(rows, ny, back):
    z, y = order(rows, 2), order(ny, 3)
    along_z = np.kron(np.eye(8, dtype=np.float32), z if back else z.T)
    return jnp.asarray(along_z, BF16), jnp.asarray(y.T if back else y, BF16)


def prepare_image_kernel(image, along_z, along_y, earlier, out):
    width, channels, rows, ny = out.shape
    picked = image[...].reshape((channels, width, rows, ny))
    for x in range(width):
        out[x] = reordered(picked[:, x], along_z[...], along_y[...])


def prepare_image(current_image, earlier):
    _, encodings, _, width, rows, ny = current_image.shape
    vmem = pl.BlockSpec(memory_space=pltpu.VMEM)
    return pl.pallas_call(
        prepare_image_kernel,
        in_specs=[vmem, vmem, vmem, pl.BlockSpec(memory_space=pl.ANY)],
        out_specs=vmem,
        out_shape=jax.ShapeDtypeStruct((width, 2 * encodings, rows, ny), BF16),
        compiler_params=pltpu.CompilerParams(vmem_limit_bytes=16 * 2**20),
        name="prepare_image",
    )(current_image, *orders(rows, ny, False), earlier)


def prepare_maps_kernel(which, maps, along_z, along_y, out):
    count, width, _, rows, ny = out.shape
    value = reordered(maps[:, 0].reshape((count * 2 * width, rows, ny)), along_z[...], along_y[...])
    for pair in range(count):
        for x in range(width):
            for part in range(2):
                out[pair, x, part] = value[(pair * 2 + part) * width + x]


def prepare_maps(which, coil_maps):
    coils, _, width, rows, ny = coil_maps.shape
    devices = coils // 2
    pairs = coil_maps.reshape((devices, 2) + coil_maps.shape[1:])
    matrices = orders(rows, ny, False)
    steps = 2
    return pl.pallas_call(
        prepare_maps_kernel,
        grid_spec=pltpu.PrefetchScalarGridSpec(
            num_scalar_prefetch=1,
            grid=(steps,),
            in_specs=[pl.BlockSpec((devices // steps, 1) + coil_maps.shape[1:], lambda i, t: (i, t[0], 0, 0, 0, 0))]
            + [pl.BlockSpec(m.shape, lambda i, t: (0, 0)) for m in matrices],
            out_specs=pl.BlockSpec((devices // steps, width, 2, rows, ny), lambda i, t: (i, 0, 0, 0, 0)),
        ),
        out_shape=jax.ShapeDtypeStruct((devices, width, 2, rows, ny), BF16),
        compiler_params=pltpu.CompilerParams(vmem_limit_bytes=58 * 2**20),
        name="prepare_maps",
    )(which, pairs, *matrices)


def update_kernel(image, chip, received, along_z, along_y, out):
    for x in range(image.shape[0]):
        value = image[x].astype(F32) - (chip[x] + received[x].astype(F32))
        out[x] = reordered(value.astype(BF16), along_z[...], along_y[...])


def update(image, chip, received):
    vmem = pl.BlockSpec(memory_space=pltpu.VMEM)
    return pl.pallas_call(
        update_kernel,
        in_specs=[vmem] * 5,
        out_specs=vmem,
        out_shape=jax.ShapeDtypeStruct(image.shape, BF16),
        compiler_params=pltpu.CompilerParams(vmem_limit_bytes=16 * 2**20),
        name="update",
    )(image, chip, received, *orders(*image.shape[-2:], True))


def shifted(value, step):
    rows = value.shape[:-1]
    edge = jnp.zeros(rows + (1,), value.dtype)
    if step > 0:
        return jnp.concatenate([value[..., 1:], edge], axis=-1)
    return jnp.concatenate([edge, value[..., :-1]], axis=-1)


def put_strided(ref, start, count, stride, value):
    for j in range(ref.shape[0]):
        ref[j, pl.ds(start, count, stride=stride), :] = value[:, j * 128 : (j + 1) * 128]


def get_lines(ref, start, count):
    return jnp.concatenate([ref[j, start : start + count, :] for j in range(ref.shape[0])], axis=1)


def convolution_kernel(ends, *refs):
    sources, refs = (refs[:2], refs[2:4]), refs[4:]
    w_first, b_first, w_second, b_second, out, stacked, result = refs
    _, channels, rows, ny = sources[0][0].shape
    depth = rows + 4
    group = stacked.shape[1] // depth
    lanes = result.shape[1] // rows
    nothing = jnp.zeros((depth, ny), F32)
    for i in range(6 * channels, group):
        put_strided(stacked, i, depth, group, nothing)
    for t, (cells, edges) in enumerate(sources):
        for i in range(channels):
            edge = edges[0, i].astype(F32)
            value = jnp.concatenate([edge[:2], cells[0, i].astype(F32), edge[2:]], axis=0)
            for d in range(3):
                line = value if d == 1 else shifted(value, d - 1)
                put_strided(stacked, (d * 2 + t) * channels + i, depth, group, line)
    features = w_first.shape[0] // 2
    taps = w_second.shape[0] // 4
    partial = []
    for pair in range(rows // 2 + 1):
        window = get_lines(stacked, 2 * pair * group, 4 * group).astype(BF16)
        hidden = jnp.maximum(nn_dot(w_first[...], window) + b_first[...], 0.0)
        if pair == 0:
            hidden = jnp.concatenate([hidden[:features] * ends[0].astype(F32), hidden[features:]], axis=0)
        if pair == rows // 2:
            hidden = jnp.concatenate([hidden[:features], hidden[features:] * ends[1].astype(F32)], axis=0)
        partial.append(nn_dot(w_second[...], hidden.astype(BF16)))
        if pair > 0:
            for z in range(2):
                total = partial[0][(2 + z) * taps : (3 + z) * taps] + partial[1][z * taps : (z + 1) * taps]
                line = shifted(total[:lanes], -1) + total[lanes : 2 * lanes] + shifted(total[2 * lanes :], 1)
                put_strided(result, 2 * pair - 2 + z, lanes, rows, line)
            partial = partial[1:]
    for i in range(channels):
        value = sources[0][0][0, i].astype(F32)
        out[0, i // 2, i % 2, 0] = (value + get_lines(result, i * rows, rows) + b_second[i]).astype(BF16)


def convolutions(ends, parts, w_first, b_first, w_second, b_second, shape):
    width, _, rows, ny = parts[0].shape
    group = w_first.shape[1] // 4
    lanes = w_second.shape[0] // 12
    smem = pl.BlockSpec(memory_space=pltpu.SMEM)
    whole = lambda a: pl.BlockSpec(a.shape, lambda x: (0,) * a.ndim)
    flops = width * (rows + 2) * ny * (w_first.size + w_second.size)
    return pl.pallas_call(
        convolution_kernel,
        grid=(width,),
        in_specs=[smem]
        + [pl.BlockSpec((1,) + a.shape[1:], lambda x: (x, 0, 0, 0)) for a in parts]
        + [whole(w_first), whole(b_first), whole(w_second), smem],
        out_specs=pl.BlockSpec((1,) + shape[1:3] + (1,) + shape[4:], lambda x: (0, 0, 0, x, 0, 0)),
        out_shape=jax.ShapeDtypeStruct(shape, BF16),
        scratch_shapes=[
            pltpu.VMEM((ny // 128, (rows + 4) * group, 128), F32),
            pltpu.VMEM((ny // 128, lanes * rows, 128), F32),
        ],
        compiler_params=pltpu.CompilerParams(vmem_limit_bytes=24 * 2**20),
        cost_estimate=pl.CostEstimate(flops=flops, bytes_accessed=2**20, transcendentals=0),
        name="convolutions",
    )(ends, *parts, w_first, b_first, w_second, b_second)


def round_up(value, unit):
    return -(-value // unit) * unit


def convolution_weights(first_weight, first_bias, second_weight):
    q = lax.axis_index(COIL)
    ahead = 2 - 2 * q
    behind = 2 * q

    def tap(weight, index):
        return lax.dynamic_index_in_dim(weight, index, axis=2, keepdims=False)

    feat, channels = first_weight.shape[:2]
    same, of_other, of_own = (tap(first_weight, i) for i in (1, ahead, behind))
    first = jnp.stack([jnp.stack([same, of_other], 1), jnp.stack([of_own, same], 1)], 0)
    first = first.transpose(0, 1, 4, 5, 2, 3).reshape(2 * feat, 3, 6 * channels)
    group = round_up(6 * channels, 16)
    first = jnp.pad(first, ((0, 0), (0, 0), (0, group - 6 * channels))).reshape(2 * feat, 3 * group)
    first = jnp.concatenate([jnp.pad(first, ((0, 0), (0, group))), jnp.pad(first, ((0, 0), (group, 0)))], axis=0)
    bias = jnp.concatenate([first_bias] * 4)[:, None]
    second = jnp.stack([tap(second_weight, 1), tap(second_weight, ahead)], 1)
    second = second.transpose(3, 4, 0, 1, 2).reshape(3, 3, channels, 2 * feat)
    lanes = round_up(channels, 8)
    second = jnp.pad(second, ((0, 0), (0, 0), (0, lanes - channels), (0, 0))).reshape(3, 3 * lanes, 2 * feat)
    none = jnp.zeros_like(second[0])
    line = lambda u: jnp.concatenate([second[u + 2 - r] if 0 <= u + 2 - r <= 2 else none for r in range(4)], axis=0)
    return first, bias, jnp.concatenate([line(0), line(1)], axis=1)


def paired(current_image, coil_maps, measured, sampling, first_weight, first_bias, second_weight, second_bias):
    devices = lax.axis_size(SLAB)
    ring = Ring(devices)
    me, q = lax.axis_index(SLAB), lax.axis_index(COIL)
    _, encodings, _, width, rows, ny = current_image.shape
    nz = rows * devices
    channels = 2 * encodings
    tables = jnp.asarray(
        np.concatenate(
            [
                split_tables(ny, 3, True, False),
                split_tables(nz, 2, False, False),
                split_tables(nz, 2, True, True),
                split_tables(ny, 3, False, True),
            ]
        )
    )
    which = q[None].astype(jnp.int32)
    where = jnp.concatenate([ring.slabs(), which])
    swap = [(0, 1), (1, 0)]
    mask = sampling.astype(BF16)
    weights = convolution_weights(first_weight, first_bias, second_weight)
    ends = jnp.stack([me > 0, me < devices - 1]).astype(jnp.int32)

    pairs = prepare_maps(which, coil_maps)
    images = prepare_image(current_image, pairs)
    gathers = [Gather(ring, images[x : x + 1]) for x in range(width)]
    kept = lax.all_to_all(pairs, SLAB, split_axis=0, concat_axis=0, tiled=True)
    for step in range(len(ring.steps())):
        for gather in gathers:
            gather.step(*(weights + (mask,) if step == 1 else (kept,) if step == 2 else ()))
    swapped = lax.ppermute(kept, COIL, swap)
    scatters = []
    for x in range(width):
        scatters.append(Scatter(ring, *gradient(where, gathers[x].pieces(), [(kept, x), (swapped, x)], measured, mask, tables, x)))
    for _ in ring.steps():
        for scatter in scatters:
            scatter.step()
    chip = jnp.stack([scatter.chip() for scatter in scatters])
    updated = update(images, chip[:, 0], lax.ppermute(chip[:, 1].astype(BF16), SLAB, ring.siblings()))
    up = [(i, i + 1) for i in range(devices - 1)]
    down = [(i + 1, i) for i in range(devices - 1)]
    other = lax.ppermute(updated, COIL, swap)
    edges = jnp.concatenate(
        [lax.ppermute(updated[:, :, rows - 2 :], SLAB, up), lax.ppermute(updated[:, :, :2], SLAB, down)], axis=2
    )
    parts = (updated, edges, other, lax.ppermute(edges, COIL, swap))
    return convolutions(ends, parts, *weights, second_bias, current_image.shape)


def with_halo(cells, sides, width):
    for axis, dim in sides:
        count = lax.axis_size(axis)
        ends = count - 1
        head = lax.slice_in_dim(cells, 0, width, axis=dim)
        tail = lax.slice_in_dim(cells, cells.shape[dim] - width, cells.shape[dim], axis=dim)
        cells = jnp.concatenate(
            [
                lax.ppermute(tail, axis, [(i, (i + 1) % count) for i in range(ends)]),
                cells,
                lax.ppermute(head, axis, [((i + 1) % count, i) for i in range(ends)]),
            ],
            axis=dim,
        )
    return cells


def plain_table(length, inverse):
    indices = jnp.arange(length, dtype=jnp.int32)
    wrapped = indices[:, None] * indices[None, :] % length
    angles = wrapped.astype(jnp.float32) * (2.0 * math.pi / length)
    factor = 1.0 / math.sqrt(length)
    cosine = jnp.cos(angles) * factor
    sine_part = jnp.sin(angles) * factor
    phase_sign = 1.0 if inverse else -1.0
    upper_rows = jnp.stack([cosine, phase_sign * sine_part], axis=1)
    lower_rows = jnp.stack([-phase_sign * sine_part, cosine], axis=1)
    return jnp.stack([upper_rows, lower_rows], axis=0).astype(jnp.bfloat16)


def coil_products(maps_part, image_part):
    maps_real = maps_part[:, 0][None, :, None].astype(jnp.float32)
    maps_imaginary = maps_part[:, 1][None, :, None].astype(jnp.float32)
    image_real = image_part[:, :, 0][:, None].astype(jnp.float32)
    image_imaginary = image_part[:, :, 1][:, None].astype(jnp.float32)
    real_part = maps_real * image_real - maps_imaginary * image_imaginary
    imaginary_part = maps_real * image_imaginary + maps_imaginary * image_real
    return jnp.stack([real_part, imaginary_part], axis=3).astype(jnp.bfloat16)


def transform(operand, matrix):
    return jnp.einsum("pcerxzy,ryqk->pceqxzk", operand, matrix, preferred_element_type=jnp.float32)


def combine_coils(maps_part, values):
    maps_real = maps_part[:, 0][None, :, None].astype(jnp.float32)
    maps_imaginary = maps_part[:, 1][None, :, None].astype(jnp.float32)
    real_sum = jnp.sum(maps_real * values[:, :, :, 0] + maps_imaginary * values[:, :, :, 1], axis=1)
    imaginary_sum = jnp.sum(
        maps_real * values[:, :, :, 1] - maps_imaginary * values[:, :, :, 0], axis=1
    )
    return jnp.stack([real_sum, imaginary_sum], axis=2)


def convolve(operand, weights):
    widened = jnp.pad(operand, ((0, 0), (0, 0), (0, 0), (0, 0), (1, 1)))
    return lax.conv_general_dilated(
        widened,
        weights,
        (1, 1, 1),
        "VALID",
        dimension_numbers=("DCNHW", "OIDHW", "DCNHW"),
        preferred_element_type=jnp.float32,
    )


def on_device(
    current_image,
    coil_maps,
    measured,
    sampling,
    first_weight,
    first_bias,
    second_weight,
    second_bias,
):
    depth = current_image.shape[4] * lax.axis_size("slab")
    forward_y = plain_table(current_image.shape[5], False)
    inverse_y = plain_table(current_image.shape[5], True)
    forward_z = plain_table(depth, False)
    inverse_z = plain_table(depth, True)
    sampled = sampling.astype(jnp.float32)[:, None, :, None, None]
    local_maps = lax.all_to_all(coil_maps, "slab", split_axis=0, concat_axis=3, tiled=True)
    row_spectra = transform(
        coil_products(local_maps, lax.all_gather(current_image, "slab", axis=4, tiled=True)),
        forward_y,
    ).astype(jnp.bfloat16)
    residual = (
        sampled
        * (
            jnp.einsum(
                "pcerxzk,rzqj->pceqxkj", row_spectra, forward_z, preferred_element_type=jnp.float32
            )
            - measured.astype(jnp.float32)
        )
    ).astype(jnp.bfloat16)
    depth_back = jnp.einsum(
        "pcerxkj,rjqz->pceqxzk", residual, inverse_z, preferred_element_type=jnp.float32
    ).astype(jnp.bfloat16)
    partial_sum = combine_coils(local_maps, transform(depth_back, inverse_y))
    gradient = lax.psum_scatter(
        partial_sum.astype(jnp.bfloat16), "slab", scatter_dimension=4, tiled=True
    ).astype(jnp.float32)
    updated = (current_image.astype(jnp.float32) - gradient).astype(jnp.bfloat16)
    stacked = updated.reshape((updated.shape[0], 2 * updated.shape[1]) + updated.shape[3:])
    bias_first = first_bias[None, :, None, None, None]
    bordered = with_halo(stacked, (("slab", 3), ("coil", 0)), 1)
    hidden = jax.nn.relu(convolve(bordered, first_weight) + bias_first).astype(jnp.bfloat16)
    bordered_hidden = with_halo(hidden, (("slab", 3), ("coil", 0)), 1)
    second = convolve(bordered_hidden, second_weight)
    refined = stacked.astype(jnp.float32) + second + second_bias[None, :, None, None, None]
    return refined.astype(jnp.bfloat16).reshape(updated.shape)


def fits(shape, devices):
    rows, ny = shape[4:]
    return rows % 16 == 0 and ny % 384 == 0 and 2 * ny == 3 * rows * devices


def solution(mesh):
    devices, phases = mesh.shape[SLAB], mesh.shape[COIL]

    def per_device(*args):
        coils, phase = args[2].shape[1], args[0].shape[0]
        if phases == 2 and coils == 2 and phase == 1 and devices % 4 == 0 and fits(args[0].shape, devices):
            return paired(*args)
        return on_device(*args)

    in_specs = (
        P("coil", None, None, None, "slab", None),
        P(None, None, None, "slab", None),
        P("coil", "slab", None, None, None, None, None),
        P("coil", None, None, None),
        P(),
        P(),
        P(),
        P(),
    )
    out_specs = P("coil", None, None, None, "slab", None)
    return jax.shard_map(
        per_device, mesh=mesh, in_specs=in_specs, out_specs=out_specs, check_vma=False
    )
```

```python
import functools
import math

import jax
import jax.numpy as jnp
import ml_dtypes
import numpy as np
from jax import lax
from jax.experimental import pallas as pl
from jax.experimental.pallas import tpu as pltpu
from jax.sharding import PartitionSpec as P

BF16 = jnp.bfloat16
F32 = jnp.float32
SLAB, COIL = "slab", "coil"


def dft_table(length, inverse):
    indices = np.arange(length, dtype=np.int64)
    wrapped = indices[:, None] * indices[None, :] % length
    angles = wrapped.astype(np.float32) * np.float32(2.0 * math.pi / length)
    factor = np.float32(1.0 / math.sqrt(length))
    cosine = np.cos(angles) * factor
    sine = np.sin(angles) * factor
    sign = np.float32(1.0 if inverse else -1.0)
    upper = np.stack([cosine, sign * sine], axis=1)
    lower = np.stack([-sign * sine, cosine], axis=1)
    return np.stack([upper, lower], axis=0).astype(ml_dtypes.bfloat16)


def split_tables(length, count, left, inverse):
    table = dft_table(length, inverse)
    part = length // count
    out = []
    for s in range(count):
        if inverse:
            piece = table[:, :part, :, s::count]
        else:
            piece = table[:, s::count, :, :part]
        if left:
            piece = piece.transpose(2, 3, 0, 1)
        out.append(piece.reshape(2 * part, 2 * part))
    return np.stack(out)


def order(length, count):
    taken = np.arange(length).reshape(-1, count).T.reshape(-1)
    return np.eye(length, dtype=np.float32)[:, taken]


class Ring:
    def __init__(self, devices):
        self.devices = devices
        self.chips = devices // 2
        self.half = self.chips // 2
        column = self.chips // 2
        self.order = [2 * i for i in range(column)] + [2 * i + 1 for i in reversed(range(column))]

    def perm(self):
        pairs = []
        for i in range(self.chips):
            for core, step in ((0, 1), (1, -1)):
                pairs.append((2 * self.order[i] + core, 2 * self.order[(i + step) % self.chips] + core))
        return pairs

    def siblings(self):
        return [(i, i ^ 1) for i in range(self.devices)]

    def steps(self):
        return [(step, True) for step in range(1, self.half)] + [(self.half, False)]

    def slabs(self):
        me = lax.axis_index(SLAB)
        chip, core = me // 2, me % 2
        column = self.chips // 2
        row = chip // 2
        place = jnp.where(chip % 2 == 0, row, self.chips - 1 - row)

        def slab(offset, parity):
            at = (place + offset + self.chips) % self.chips
            return 2 * jnp.where(at < column, 2 * at, 2 * (self.chips - 1 - at) + 1) + parity

        def handled(by, sign):
            way = sign * (1 - 2 * by)
            out = []
            for step, both in self.steps():
                out += [slab(way * step, by)] + ([slab(way * step, 1 - by)] if both else [])
            return out

        own = [slab(0, core), slab(0, 1 - core)]
        gathered = own + handled(core, -1) + handled(1 - core, -1)
        summed = own + handled(core, 1) + handled(1 - core, 1)
        return jnp.stack(gathered + summed).astype(jnp.int32)


def after(value, *earlier):
    return lax.optimization_barrier((value,) + earlier)[0]


class Gather:
    def __init__(self, ring, mine):
        self.ring = ring
        self.first = lax.ppermute(mine, SLAB, ring.perm())
        self.own = [mine, lax.ppermute(mine, SLAB, ring.siblings())]
        self.held = None
        self.kept, self.other = [], []

    def step(self, *earlier):
        both = self.ring.steps()[len(self.kept)][1]
        if self.held is None:
            self.held = jnp.concatenate([self.first, lax.ppermute(self.own[1], SLAB, self.ring.perm())], axis=0)
        else:
            held = self.held if both else self.held[:1]
            self.held = lax.ppermute(after(held, *earlier) if earlier else held, SLAB, self.ring.perm())
        self.kept.append(self.held)
        self.other.append(lax.ppermute(self.held, SLAB, self.ring.siblings()))

    def pieces(self):
        return self.own + self.kept + self.other


class Scatter:
    def __init__(self, ring, own, kept, sent):
        self.ring, self.own, self.kept = ring, own, kept
        self.other = lax.ppermute(sent, SLAB, ring.siblings())
        self.held = None
        self.left = list(ring.steps())
        self.end = kept.shape[0]

    def step(self):
        count = 2 if self.left.pop()[1] else 1
        self.end -= count
        total = self.kept[self.end : self.end + count].astype(F32) + self.other[self.end : self.end + count].astype(F32)
        if self.held is not None:
            got = self.held.astype(F32)
            if got.shape[0] < count:
                total = jnp.concatenate([total[:1] + got, total[1:]], axis=0)
            else:
                total = total + got
        self.held = lax.ppermute(total.astype(BF16), SLAB, self.ring.perm())
        return self.held

    def chip(self):
        return self.own.astype(F32) + self.held.astype(F32)


def nt_dot(a, b):
    return lax.dot_general(a, b, (((1,), (1,)), ((), ())), preferred_element_type=F32)


def nn_dot(a, b):
    return lax.dot_general(a, b, (((1,), (0,)), ((), ())), preferred_element_type=F32)


def gradient_kernel(images, coils, slabs, *refs):
    held_images, refs = refs[:images], refs[images:]
    maps, refs = refs[:coils], refs[coils:]
    measured, sampling, tables = refs[:3]
    out, products, backs = refs[3:6], refs[6], refs[7]
    ty_f, tz_f, tz_i, ty_i = [0, 1, 2], [3, 4], [5, 6], [7, 8, 9]
    rows, ny = held_images[0].shape[-2:]
    nz = sampling.shape[-1]
    count, half = nz // rows, rows // 2
    my, mz = ny // 3, nz // 2
    first = slabs[2 * count]
    root = math.sqrt(0.75)

    def pieces(arrays):
        return [(array, i) for array in arrays for i in range(array.shape[0])]

    def places(slab):
        at = pl.multiple_of(slab * half, half)
        return pl.ds(at, half), pl.ds(pl.multiple_of(at + mz, half), half)

    def thirds(b0, b1, b2, sign):
        add = [u + v for u, v in zip(b1, b2)]
        low = [u - 0.5 * v for u, v in zip(b0, add)]
        turn = [(sign * root) * (u - v) for u, v in zip(b1, b2)]
        return (
            (b0[0] + add[0], b0[1] + add[1]),
            (low[0] - turn[1], low[1] + turn[0]),
            (low[0] + turn[1], low[1] - turn[0]),
        )

    def product(c):
        for k, (held, i) in enumerate(pieces(held_images)):
            slab = slabs[k]
            real = held[i, 0].astype(F32)
            imag = held[i, 1].astype(F32)
            m_real = maps[c][slab, 0, 0].astype(F32)
            m_imag = maps[c][slab, 0, 1].astype(F32)
            p_real = m_real * real - m_imag * imag
            p_imag = m_real * imag + m_imag * real
            for parity, at in enumerate(places(slab)):
                lines = slice(parity * half, (parity + 1) * half)
                for j in range(3):
                    cells = slice(j * my, (j + 1) * my)
                    products[c, j, at, :my] = p_real[lines, cells]
                    products[c, j, at, my:] = p_imag[lines, cells]

    def to_frequency_y(c):
        return [nt_dot(tables[ty_f[j]], products[c, j].astype(BF16)) for j in range(3)]

    def spectra_of(parts):
        parts = thirds(*[(part[:my], part[my:]) for part in parts], -1.0)
        return [jnp.concatenate([part[q].astype(BF16) for part in parts], axis=0) for q in range(2)]

    def to_frequency_z(spectra):
        halves = []
        for j in range(2):
            cells = slice(j * mz, (j + 1) * mz)
            halves.append(nn_dot(jnp.concatenate([spectra[0][:, cells], spectra[1][:, cells]], axis=1), tables[tz_f[j]]))
        return halves

    def residual_of(c, halves):
        coil = first if c == 0 else 1 - first
        mask = sampling[0, 0].astype(F32)
        sums, differences = [], []
        for q in range(2):
            cells = slice(q * mz, (q + 1) * mz)
            seen = measured[0, coil, 0, q, 0].astype(F32)
            low = mask[:, :mz] * (halves[0][:, cells] + halves[1][:, cells] - seen[:, :mz])
            high = mask[:, mz:] * (halves[0][:, cells] - halves[1][:, cells] - seen[:, mz:])
            sums.append((low + high).astype(BF16))
            differences.append((low - high).astype(BF16))
        return jnp.concatenate(sums, axis=1), jnp.concatenate(differences, axis=1)

    def to_depth(folds):
        return [nt_dot(tables[tz_i[j]], folds[j]) for j in range(2)]

    def lines_of(depths):
        lines = [[], [], []]
        for j in range(2):
            cut = lambda q, i: depths[j][q * mz : (q + 1) * mz, i * my : (i + 1) * my]
            turned = thirds(*[(cut(0, i), cut(1, i)) for i in range(3)], 1.0)
            for i in range(3):
                lines[i].append(jnp.concatenate([turned[i][0].astype(BF16), turned[i][1].astype(BF16)], axis=1))
        return [jnp.concatenate(line, axis=0) for line in lines]

    def to_image(c, lines):
        for i in range(3):
            backs[c, i] = nn_dot(lines[i], tables[ty_i[i]])

    stages = [
        lambda c, _: product(c),
        lambda c, _: to_frequency_y(c),
        lambda c, value: spectra_of(value),
        lambda c, value: to_frequency_z(value),
        lambda c, value: residual_of(c, value),
        lambda c, value: to_depth(value),
        lambda c, value: lines_of(value),
        lambda c, value: to_image(c, value),
    ]
    held_values = [None] * coils
    for step in range(len(stages) + coils - 1):
        for c in range(coils):
            if 0 <= step - c < len(stages):
                held_values[c] = stages[step - c](c, held_values[c])
    for k, (held, i) in enumerate(pieces(out)):
        slab = slabs[count + k]
        for j in range(3):
            cells = slice(j * my, (j + 1) * my)
            real, imag = 0.0, 0.0
            for c in range(coils):
                m_real = maps[c][slab, 0, 0, :, cells].astype(F32)
                m_imag = maps[c][slab, 0, 1, :, cells].astype(F32)
                back = jnp.concatenate([backs[c, j, at, :] for at in places(slab)], axis=0)
                real += m_real * back[:, :my] + m_imag * back[:, my:]
                imag += m_real * back[:, my:] - m_imag * back[:, :my]
            held[i, 0, :, cells] = real.astype(BF16)
            held[i, 1, :, cells] = imag.astype(BF16)


def gradient(where, images, maps, measured, sampling, tables, x):
    _, channels, rows, ny = images[0].shape
    nz = sampling.shape[-1]
    n = len(maps)
    far = (nz // rows - 2) // 2
    whole = lambda a: pl.BlockSpec(a.shape, lambda e, s: (0,) * a.ndim, pipeline_mode=pl.Buffered(1))
    flops = channels * n * 2 * 4 * (nz * ny * ny + nz * nz * ny)
    return pl.pallas_call(
        functools.partial(gradient_kernel, len(images), n),
        grid_spec=pltpu.PrefetchScalarGridSpec(
            num_scalar_prefetch=1,
            grid=(channels // 2,),
            in_specs=[pl.BlockSpec((a.shape[0], 2, rows, ny), lambda e, s: (0, e, 0, 0)) for a in images]
            + [
                pl.BlockSpec((a.shape[0], 1, 2, rows, ny), functools.partial(lambda at, e, s: (0, at, 0, 0, 0), at),
                             pipeline_mode=pl.Buffered(1))
                for a, at in maps
            ]
            + [
                pl.BlockSpec((1, 2, 1, 2, 1, ny, nz), lambda e, s: (0, 0, e, 0, x, 0, 0)),
                pl.BlockSpec((1, 1, ny, nz), lambda e, s: (0, e, 0, 0)),
            ]
            + [whole(tables)],
            out_specs=[pl.BlockSpec((m, 2, rows, ny), lambda e, s: (0, e, 0, 0)) for m in (2, far, far)],
            scratch_shapes=[
                pltpu.VMEM((n, 3, nz, 2 * ny // 3), F32),
                pltpu.VMEM((n, 3, nz, 2 * ny // 3), F32),
            ],
        ),
        out_shape=[jax.ShapeDtypeStruct((m, channels, rows, ny), BF16) for m in (2, far, far)],
        compiler_params=pltpu.CompilerParams(vmem_limit_bytes=46 * 2**20),
        cost_estimate=pl.CostEstimate(flops=flops, bytes_accessed=8 * 2**20, transcendentals=0),
        name="gradient",
    )(where, *images, *[a for a, _ in maps], measured, sampling, tables)


def reordered(value, along_z, along_y):
    n, rows, ny = value.shape
    block = along_z.shape[0]
    flat = nn_dot(value.reshape(n * rows, ny), along_y).astype(BF16)
    out = []
    for start in range(0, n * rows, block):
        size = min(block, n * rows - start)
        out.append(nn_dot(along_z[:size, :size], flat[start : start + size]).astype(BF16))
    return jnp.concatenate(out, axis=0).reshape(n, rows, ny)


def orders(rows, ny, back):
    z, y = order(rows, 2), order(ny, 3)
    along_z = np.kron(np.eye(8, dtype=np.float32), z if back else z.T)
    return jnp.asarray(along_z, BF16), jnp.asarray(y.T if back else y, BF16)


def prepare_image_kernel(image, along_z, along_y, earlier, out):
    width, channels, rows, ny = out.shape
    picked = image[...].reshape((channels, width, rows, ny))
    for x in range(width):
        out[x] = reordered(picked[:, x], along_z[...], along_y[...])


def prepare_image(current_image, earlier):
    _, encodings, _, width, rows, ny = current_image.shape
    vmem = pl.BlockSpec(memory_space=pltpu.VMEM)
    return pl.pallas_call(
        prepare_image_kernel,
        in_specs=[vmem, vmem, vmem, pl.BlockSpec(memory_space=pl.ANY)],
        out_specs=vmem,
        out_shape=jax.ShapeDtypeStruct((width, 2 * encodings, rows, ny), BF16),
        compiler_params=pltpu.CompilerParams(vmem_limit_bytes=16 * 2**20),
        name="prepare_image",
    )(current_image, *orders(rows, ny, False), earlier)


def prepare_maps_kernel(which, maps, along_z, along_y, out):
    count, width, _, rows, ny = out.shape
    value = reordered(maps[:, 0].reshape((count * 2 * width, rows, ny)), along_z[...], along_y[...])
    for pair in range(count):
        for x in range(width):
            for part in range(2):
                out[pair, x, part] = value[(pair * 2 + part) * width + x]


def prepare_maps(which, coil_maps):
    coils, _, width, rows, ny = coil_maps.shape
    devices = coils // 2
    pairs = coil_maps.reshape((devices, 2) + coil_maps.shape[1:])
    matrices = orders(rows, ny, False)
    steps = 1
    return pl.pallas_call(
        prepare_maps_kernel,
        grid_spec=pltpu.PrefetchScalarGridSpec(
            num_scalar_prefetch=1,
            grid=(steps,),
            in_specs=[pl.BlockSpec((devices // steps, 1) + coil_maps.shape[1:], lambda i, t: (i, t[0], 0, 0, 0, 0))]
            + [pl.BlockSpec(m.shape, lambda i, t: (0, 0)) for m in matrices],
            out_specs=pl.BlockSpec((devices // steps, width, 2, rows, ny), lambda i, t: (i, 0, 0, 0, 0)),
        ),
        out_shape=jax.ShapeDtypeStruct((devices, width, 2, rows, ny), BF16),
        compiler_params=pltpu.CompilerParams(vmem_limit_bytes=58 * 2**20),
        name="prepare_maps",
    )(which, pairs, *matrices)


def update_kernel(image, chip, received, along_z, along_y, out):
    for x in range(image.shape[0]):
        value = image[x].astype(F32) - (chip[x] + received[x].astype(F32))
        out[x] = reordered(value.astype(BF16), along_z[...], along_y[...])


def update(image, chip, received):
    vmem = pl.BlockSpec(memory_space=pltpu.VMEM)
    return pl.pallas_call(
        update_kernel,
        in_specs=[vmem] * 5,
        out_specs=vmem,
        out_shape=jax.ShapeDtypeStruct(image.shape, BF16),
        compiler_params=pltpu.CompilerParams(vmem_limit_bytes=16 * 2**20),
        name="update",
    )(image, chip, received, *orders(*image.shape[-2:], True))


def shifted(value, step):
    rows = value.shape[:-1]
    edge = jnp.zeros(rows + (1,), value.dtype)
    if step > 0:
        return jnp.concatenate([value[..., 1:], edge], axis=-1)
    return jnp.concatenate([edge, value[..., :-1]], axis=-1)


def put_strided(ref, first, start, count, stride, value):
    for j in range(value.shape[1] // 128):
        ref[first + j, pl.ds(start, count, stride=stride), :] = value[:, j * 128 : (j + 1) * 128]


def get_lines(ref, chunks, start, count):
    return jnp.concatenate([ref[j, start : start + count, :] for j in chunks], axis=1)


def convolution_kernel(ends, *refs):
    sources, refs = (refs[:2], refs[2:4]), refs[4:]
    w_first, b_first, w_second, b_second, out, stacked, result = refs
    width, channels, rows, ny = sources[0][0].shape
    depth = rows + 4
    group = stacked.shape[1] // depth
    lanes = result.shape[1] // rows
    chunks = ny // 128
    nothing = jnp.zeros((depth, ny), F32)
    for x in range(width):
        for i in range(6 * channels, group):
            put_strided(stacked, x * chunks, i, depth, group, nothing)
        for t, (cells, edges) in enumerate(sources):
            for i in range(channels):
                edge = edges[x, i].astype(F32)
                value = jnp.concatenate([edge[:2], cells[x, i].astype(F32), edge[2:]], axis=0)
                for d in range(3):
                    line = value if d == 1 else shifted(value, d - 1)
                    put_strided(stacked, x * chunks, (d * 2 + t) * channels + i, depth, group, line)
    features = w_first.shape[0] // 2
    taps = w_second.shape[0] // 4
    partial = []
    for pair in range(rows // 2 + 1):
        window = get_lines(stacked, range(width * chunks), 2 * pair * group, 4 * group).astype(BF16)
        hidden = jnp.maximum(nn_dot(w_first[...], window) + b_first[...], 0.0)
        if pair == 0:
            hidden = jnp.concatenate([hidden[:features] * ends[0].astype(F32), hidden[features:]], axis=0)
        if pair == rows // 2:
            hidden = jnp.concatenate([hidden[:features], hidden[features:] * ends[1].astype(F32)], axis=0)
        partial.append(nn_dot(w_second[...], hidden.astype(BF16)))
        if pair > 0:
            for z in range(2):
                both = partial[0][(2 + z) * taps : (3 + z) * taps] + partial[1][z * taps : (z + 1) * taps]
                for x in range(width):
                    total = both[:, x * ny : (x + 1) * ny]
                    line = shifted(total[:lanes], -1) + total[lanes : 2 * lanes] + shifted(total[2 * lanes :], 1)
                    put_strided(result, x * chunks, 2 * pair - 2 + z, lanes, rows, line)
            partial = partial[1:]
    for x in range(width):
        for i in range(channels):
            value = sources[0][0][x, i].astype(F32)
            added = get_lines(result, range(x * chunks, (x + 1) * chunks), i * rows, rows)
            out[0, i // 2, i % 2, x] = (value + added + b_second[i]).astype(BF16)


def convolutions(ends, parts, w_first, b_first, w_second, b_second, shape):
    width, _, rows, ny = parts[0].shape
    group = w_first.shape[1] // 4
    lanes = w_second.shape[0] // 12
    smem = pl.BlockSpec(memory_space=pltpu.SMEM)
    vmem = pl.BlockSpec(memory_space=pltpu.VMEM)
    flops = width * (rows + 2) * ny * (w_first.size + w_second.size)
    return pl.pallas_call(
        convolution_kernel,
        in_specs=[smem] + [vmem] * (len(parts) + 3) + [smem],
        out_specs=vmem,
        out_shape=jax.ShapeDtypeStruct(shape, BF16),
        scratch_shapes=[
            pltpu.VMEM((width * ny // 128, (rows + 4) * group, 128), F32),
            pltpu.VMEM((width * ny // 128, lanes * rows, 128), F32),
        ],
        compiler_params=pltpu.CompilerParams(vmem_limit_bytes=24 * 2**20),
        cost_estimate=pl.CostEstimate(flops=flops, bytes_accessed=2**20, transcendentals=0),
        name="convolutions",
    )(ends, *parts, w_first, b_first, w_second, b_second)


def round_up(value, unit):
    return -(-value // unit) * unit


def convolution_weights(first_weight, first_bias, second_weight):
    q = lax.axis_index(COIL)
    ahead = 2 - 2 * q
    behind = 2 * q

    def tap(weight, index):
        return lax.dynamic_index_in_dim(weight, index, axis=2, keepdims=False)

    feat, channels = first_weight.shape[:2]
    same, of_other, of_own = (tap(first_weight, i) for i in (1, ahead, behind))
    first = jnp.stack([jnp.stack([same, of_other], 1), jnp.stack([of_own, same], 1)], 0)
    first = first.transpose(0, 1, 4, 5, 2, 3).reshape(2 * feat, 3, 6 * channels)
    group = round_up(6 * channels, 16)
    first = jnp.pad(first, ((0, 0), (0, 0), (0, group - 6 * channels))).reshape(2 * feat, 3 * group)
    first = jnp.concatenate([jnp.pad(first, ((0, 0), (0, group))), jnp.pad(first, ((0, 0), (group, 0)))], axis=0)
    bias = jnp.concatenate([first_bias] * 4)[:, None]
    second = jnp.stack([tap(second_weight, 1), tap(second_weight, ahead)], 1)
    second = second.transpose(3, 4, 0, 1, 2).reshape(3, 3, channels, 2 * feat)
    lanes = round_up(channels, 8)
    second = jnp.pad(second, ((0, 0), (0, 0), (0, lanes - channels), (0, 0))).reshape(3, 3 * lanes, 2 * feat)
    none = jnp.zeros_like(second[0])
    line = lambda u: jnp.concatenate([second[u + 2 - r] if 0 <= u + 2 - r <= 2 else none for r in range(4)], axis=0)
    return first, bias, jnp.concatenate([line(0), line(1)], axis=1)


def paired(current_image, coil_maps, measured, sampling, first_weight, first_bias, second_weight, second_bias):
    devices = lax.axis_size(SLAB)
    ring = Ring(devices)
    me, q = lax.axis_index(SLAB), lax.axis_index(COIL)
    _, encodings, _, width, rows, ny = current_image.shape
    nz = rows * devices
    channels = 2 * encodings
    tables = jnp.asarray(
        np.concatenate(
            [
                split_tables(ny, 3, True, False),
                split_tables(nz, 2, False, False),
                split_tables(nz, 2, True, True),
                split_tables(ny, 3, False, True),
            ]
        )
    )
    which = q[None].astype(jnp.int32)
    where = jnp.concatenate([ring.slabs(), which])
    swap = [(0, 1), (1, 0)]
    mask = sampling.astype(BF16)
    weights = convolution_weights(first_weight, first_bias, second_weight)
    ends = jnp.stack([me > 0, me < devices - 1]).astype(jnp.int32)

    pairs = prepare_maps(which, coil_maps)
    images = prepare_image(current_image, pairs)
    gathers = [Gather(ring, images[x : x + 1]) for x in range(width)]
    kept = lax.all_to_all(pairs, SLAB, split_axis=0, concat_axis=0, tiled=True)
    for step in range(len(ring.steps())):
        for gather in gathers:
            gather.step(*(weights + (mask,) if step == 1 else (kept,) if step == 2 else ()))
    swapped = lax.ppermute(kept, COIL, swap)
    scatters = []
    for x in range(width):
        scatters.append(Scatter(ring, *gradient(where, gathers[x].pieces(), [(kept, x), (swapped, x)], measured, mask, tables, x)))
    for _ in ring.steps():
        for scatter in scatters:
            scatter.step()
    chip = jnp.stack([scatter.chip() for scatter in scatters])
    updated = update(images, chip[:, 0], lax.ppermute(chip[:, 1].astype(BF16), SLAB, ring.siblings()))
    up = [(i, i + 1) for i in range(devices - 1)]
    down = [(i + 1, i) for i in range(devices - 1)]
    other = lax.ppermute(updated, COIL, swap)
    edges = jnp.concatenate(
        [lax.ppermute(updated[:, :, rows - 2 :], SLAB, up), lax.ppermute(updated[:, :, :2], SLAB, down)], axis=2
    )
    parts = (updated, edges, other, lax.ppermute(edges, COIL, swap))
    return convolutions(ends, parts, *weights, second_bias, current_image.shape)


def with_halo(cells, sides, width):
    for axis, dim in sides:
        count = lax.axis_size(axis)
        ends = count - 1
        head = lax.slice_in_dim(cells, 0, width, axis=dim)
        tail = lax.slice_in_dim(cells, cells.shape[dim] - width, cells.shape[dim], axis=dim)
        cells = jnp.concatenate(
            [
                lax.ppermute(tail, axis, [(i, (i + 1) % count) for i in range(ends)]),
                cells,
                lax.ppermute(head, axis, [((i + 1) % count, i) for i in range(ends)]),
            ],
            axis=dim,
        )
    return cells


def plain_table(length, inverse):
    indices = jnp.arange(length, dtype=jnp.int32)
    wrapped = indices[:, None] * indices[None, :] % length
    angles = wrapped.astype(jnp.float32) * (2.0 * math.pi / length)
    factor = 1.0 / math.sqrt(length)
    cosine = jnp.cos(angles) * factor
    sine_part = jnp.sin(angles) * factor
    phase_sign = 1.0 if inverse else -1.0
    upper_rows = jnp.stack([cosine, phase_sign * sine_part], axis=1)
    lower_rows = jnp.stack([-phase_sign * sine_part, cosine], axis=1)
    return jnp.stack([upper_rows, lower_rows], axis=0).astype(jnp.bfloat16)


def coil_products(maps_part, image_part):
    maps_real = maps_part[:, 0][None, :, None].astype(jnp.float32)
    maps_imaginary = maps_part[:, 1][None, :, None].astype(jnp.float32)
    image_real = image_part[:, :, 0][:, None].astype(jnp.float32)
    image_imaginary = image_part[:, :, 1][:, None].astype(jnp.float32)
    real_part = maps_real * image_real - maps_imaginary * image_imaginary
    imaginary_part = maps_real * image_imaginary + maps_imaginary * image_real
    return jnp.stack([real_part, imaginary_part], axis=3).astype(jnp.bfloat16)


def transform(operand, matrix):
    return jnp.einsum("pcerxzy,ryqk->pceqxzk", operand, matrix, preferred_element_type=jnp.float32)


def combine_coils(maps_part, values):
    maps_real = maps_part[:, 0][None, :, None].astype(jnp.float32)
    maps_imaginary = maps_part[:, 1][None, :, None].astype(jnp.float32)
    real_sum = jnp.sum(maps_real * values[:, :, :, 0] + maps_imaginary * values[:, :, :, 1], axis=1)
    imaginary_sum = jnp.sum(
        maps_real * values[:, :, :, 1] - maps_imaginary * values[:, :, :, 0], axis=1
    )
    return jnp.stack([real_sum, imaginary_sum], axis=2)


def convolve(operand, weights):
    widened = jnp.pad(operand, ((0, 0), (0, 0), (0, 0), (0, 0), (1, 1)))
    return lax.conv_general_dilated(
        widened,
        weights,
        (1, 1, 1),
        "VALID",
        dimension_numbers=("DCNHW", "OIDHW", "DCNHW"),
        preferred_element_type=jnp.float32,
    )


def on_device(
    current_image,
    coil_maps,
    measured,
    sampling,
    first_weight,
    first_bias,
    second_weight,
    second_bias,
):
    depth = current_image.shape[4] * lax.axis_size("slab")
    forward_y = plain_table(current_image.shape[5], False)
    inverse_y = plain_table(current_image.shape[5], True)
    forward_z = plain_table(depth, False)
    inverse_z = plain_table(depth, True)
    sampled = sampling.astype(jnp.float32)[:, None, :, None, None]
    local_maps = lax.all_to_all(coil_maps, "slab", split_axis=0, concat_axis=3, tiled=True)
    row_spectra = transform(
        coil_products(local_maps, lax.all_gather(current_image, "slab", axis=4, tiled=True)),
        forward_y,
    ).astype(jnp.bfloat16)
    residual = (
        sampled
        * (
            jnp.einsum(
                "pcerxzk,rzqj->pceqxkj", row_spectra, forward_z, preferred_element_type=jnp.float32
            )
            - measured.astype(jnp.float32)
        )
    ).astype(jnp.bfloat16)
    depth_back = jnp.einsum(
        "pcerxkj,rjqz->pceqxzk", residual, inverse_z, preferred_element_type=jnp.float32
    ).astype(jnp.bfloat16)
    partial_sum = combine_coils(local_maps, transform(depth_back, inverse_y))
    gradient = lax.psum_scatter(
        partial_sum.astype(jnp.bfloat16), "slab", scatter_dimension=4, tiled=True
    ).astype(jnp.float32)
    updated = (current_image.astype(jnp.float32) - gradient).astype(jnp.bfloat16)
    stacked = updated.reshape((updated.shape[0], 2 * updated.shape[1]) + updated.shape[3:])
    bias_first = first_bias[None, :, None, None, None]
    bordered = with_halo(stacked, (("slab", 3), ("coil", 0)), 1)
    hidden = jax.nn.relu(convolve(bordered, first_weight) + bias_first).astype(jnp.bfloat16)
    bordered_hidden = with_halo(hidden, (("slab", 3), ("coil", 0)), 1)
    second = convolve(bordered_hidden, second_weight)
    refined = stacked.astype(jnp.float32) + second + second_bias[None, :, None, None, None]
    return refined.astype(jnp.bfloat16).reshape(updated.shape)


def fits(shape, devices):
    rows, ny = shape[4:]
    return rows % 16 == 0 and ny % 384 == 0 and 2 * ny == 3 * rows * devices


def solution(mesh):
    devices, phases = mesh.shape[SLAB], mesh.shape[COIL]

    def per_device(*args):
        coils, phase = args[2].shape[1], args[0].shape[0]
        if phases == 2 and coils == 2 and phase == 1 and devices % 4 == 0 and fits(args[0].shape, devices):
            return paired(*args)
        return on_device(*args)

    in_specs = (
        P("coil", None, None, None, "slab", None),
        P(None, None, None, "slab", None),
        P("coil", "slab", None, None, None, None, None),
        P("coil", None, None, None),
        P(),
        P(),
        P(),
        P(),
    )
    out_specs = P("coil", None, None, None, "slab", None)
    return jax.shard_map(
        per_device, mesh=mesh, in_specs=in_specs, out_specs=out_specs, check_vma=False
    )
```

```python
import functools
import math

import jax
import jax.numpy as jnp
import ml_dtypes
import numpy as np
from jax import lax
from jax.experimental import pallas as pl
from jax.experimental.pallas import tpu as pltpu
from jax.sharding import PartitionSpec as P

BF16 = jnp.bfloat16
F32 = jnp.float32
SLAB, COIL = "slab", "coil"


def dft_table(length, inverse):
    indices = np.arange(length, dtype=np.int64)
    wrapped = indices[:, None] * indices[None, :] % length
    angles = wrapped.astype(np.float32) * np.float32(2.0 * math.pi / length)
    factor = np.float32(1.0 / math.sqrt(length))
    cosine = np.cos(angles) * factor
    sine = np.sin(angles) * factor
    sign = np.float32(1.0 if inverse else -1.0)
    upper = np.stack([cosine, sign * sine], axis=1)
    lower = np.stack([-sign * sine, cosine], axis=1)
    return np.stack([upper, lower], axis=0).astype(ml_dtypes.bfloat16)


def split_tables(length, count, left):
    table = dft_table(length, False)
    part = length // count
    out = []
    for s in range(count):
        piece = table[:, s::count, :, :part]
        if left:
            piece = piece.transpose(2, 3, 0, 1)
        out.append(piece.reshape(2 * part, 2 * part))
    return np.stack(out)


def order(length, count):
    taken = np.arange(length).reshape(-1, count).T.reshape(-1)
    return np.eye(length, dtype=np.float32)[:, taken]


class Ring:
    def __init__(self, devices):
        self.devices = devices
        self.chips = devices // 2
        self.half = self.chips // 2
        column = self.chips // 2
        self.order = [2 * i for i in range(column)] + [2 * i + 1 for i in reversed(range(column))]

    def perm(self):
        pairs = []
        for i in range(self.chips):
            for core, step in ((0, 1), (1, -1)):
                pairs.append((2 * self.order[i] + core, 2 * self.order[(i + step) % self.chips] + core))
        return pairs

    def siblings(self):
        return [(i, i ^ 1) for i in range(self.devices)]

    def steps(self):
        return [(step, True) for step in range(1, self.half)] + [(self.half, False)]

    def slabs(self):
        me = lax.axis_index(SLAB)
        chip, core = me // 2, me % 2
        column = self.chips // 2
        row = chip // 2
        place = jnp.where(chip % 2 == 0, row, self.chips - 1 - row)

        def slab(offset, parity):
            at = (place + offset + self.chips) % self.chips
            return 2 * jnp.where(at < column, 2 * at, 2 * (self.chips - 1 - at) + 1) + parity

        def handled(by, sign):
            way = sign * (1 - 2 * by)
            out = []
            for step, both in self.steps():
                out += [slab(way * step, by)] + ([slab(way * step, 1 - by)] if both else [])
            return out

        own = [slab(0, core), slab(0, 1 - core)]
        gathered = own + handled(core, -1) + handled(1 - core, -1)
        summed = own + handled(core, 1) + handled(1 - core, 1)
        return jnp.stack(gathered + summed).astype(jnp.int32)


def after(value, *earlier):
    return lax.optimization_barrier((value,) + earlier)[0]


class Gather:
    def __init__(self, ring, mine):
        self.ring = ring
        self.first = lax.ppermute(mine, SLAB, ring.perm())
        self.own = [mine, lax.ppermute(mine, SLAB, ring.siblings())]
        self.held = None
        self.kept, self.other = [], []

    def step(self, *earlier):
        both = self.ring.steps()[len(self.kept)][1]
        if self.held is None:
            self.held = jnp.concatenate([self.first, lax.ppermute(self.own[1], SLAB, self.ring.perm())], axis=0)
        else:
            held = self.held if both else self.held[:1]
            self.held = lax.ppermute(after(held, *earlier) if earlier else held, SLAB, self.ring.perm())
        self.kept.append(self.held)
        self.other.append(lax.ppermute(self.held, SLAB, self.ring.siblings()))

    def pieces(self):
        return self.own + self.kept + self.other


class Scatter:
    def __init__(self, ring, own, kept, sent):
        self.ring, self.own, self.kept = ring, own, kept
        self.other = lax.ppermute(sent, SLAB, ring.siblings())
        self.held = None
        self.left = list(ring.steps())
        self.end = kept.shape[0]

    def step(self):
        count = 2 if self.left.pop()[1] else 1
        self.end -= count
        total = self.kept[self.end : self.end + count].astype(F32) + self.other[self.end : self.end + count].astype(F32)
        if self.held is not None:
            got = self.held.astype(F32)
            if got.shape[0] < count:
                total = jnp.concatenate([total[:1] + got, total[1:]], axis=0)
            else:
                total = total + got
        self.held = lax.ppermute(total.astype(BF16), SLAB, self.ring.perm())
        return self.held

    def chip(self):
        return self.own.astype(F32) + self.held.astype(F32)


def nt_dot(a, b):
    return lax.dot_general(a, b, (((1,), (1,)), ((), ())), preferred_element_type=F32)


def nn_dot(a, b):
    return lax.dot_general(a, b, (((1,), (0,)), ((), ())), preferred_element_type=F32)


def gradient_kernel(images, coils, slabs, *refs):
    held_images, refs = refs[:images], refs[images:]
    maps, refs = refs[:coils], refs[coils:]
    measured, sampling, tables = refs[:3]
    out, products, backs = refs[3:6], refs[6], refs[7]
    in_y, in_z = [0, 1, 2], [3, 4]
    rows, ny = held_images[0].shape[-2:]
    nz = sampling.shape[-1]
    count, half = nz // rows, rows // 2
    my, mz = ny // 3, nz // 2
    first = slabs[2 * count]
    root = math.sqrt(0.75)

    def pieces(arrays):
        return [(array, i) for array in arrays for i in range(array.shape[0])]

    def places(slab):
        at = pl.multiple_of(slab * half, half)
        return pl.ds(at, half), pl.ds(pl.multiple_of(at + mz, half), half)

    def thirds(b0, b1, b2, sign):
        add = [u + v for u, v in zip(b1, b2)]
        low = [u - 0.5 * v for u, v in zip(b0, add)]
        turn = [(sign * root) * (u - v) for u, v in zip(b1, b2)]
        return (
            (b0[0] + add[0], b0[1] + add[1]),
            (low[0] - turn[1], low[1] + turn[0]),
            (low[0] + turn[1], low[1] - turn[0]),
        )

    def product(c):
        for k, (held, i) in enumerate(pieces(held_images)):
            slab = slabs[k]
            real = held[i, 0].astype(F32)
            imag = held[i, 1].astype(F32)
            m_real = maps[c][slab, 0, 0].astype(F32)
            m_imag = maps[c][slab, 0, 1].astype(F32)
            p_real = m_real * real - m_imag * imag
            p_imag = m_real * imag + m_imag * real
            for parity, at in enumerate(places(slab)):
                lines = slice(parity * half, (parity + 1) * half)
                for j in range(3):
                    cells = slice(j * my, (j + 1) * my)
                    products[c, j, at, :my] = p_real[lines, cells]
                    products[c, j, at, my:] = p_imag[lines, cells]

    def to_frequency_y(c):
        return [nt_dot(tables[in_y[j]], products[c, j].astype(BF16)) for j in range(3)]

    def spectra_of(parts):
        parts = thirds(*[(part[:my], part[my:]) for part in parts], -1.0)
        return [jnp.concatenate([part[q].astype(BF16) for part in parts], axis=0) for q in range(2)]

    def to_frequency_z(spectra):
        halves = []
        for j in range(2):
            cells = slice(j * mz, (j + 1) * mz)
            halves.append(nn_dot(jnp.concatenate([spectra[0][:, cells], spectra[1][:, cells]], axis=1), tables[in_z[j]]))
        return halves

    def residual_of(c, halves):
        coil = first if c == 0 else 1 - first
        mask = sampling[0, 0].astype(F32)
        sums, differences = [], []
        for q in range(2):
            cells = slice(q * mz, (q + 1) * mz)
            seen = measured[0, coil, 0, q, 0].astype(F32)
            low = mask[:, :mz] * (halves[0][:, cells] + halves[1][:, cells] - seen[:, :mz])
            high = mask[:, mz:] * (halves[0][:, cells] - halves[1][:, cells] - seen[:, mz:])
            sums.append((low + high).astype(BF16))
            differences.append((low - high).astype(BF16))
        return jnp.concatenate(sums, axis=1), jnp.concatenate(differences, axis=1)

    def to_depth(folds):
        return [nt_dot(tables[in_z[j]], folds[j]) for j in range(2)]

    def lines_of(depths):
        lines = [[], [], []]
        for j in range(2):
            cut = lambda q, i: depths[j][q * mz : (q + 1) * mz, i * my : (i + 1) * my]
            turned = thirds(*[(cut(0, i), cut(1, i)) for i in range(3)], 1.0)
            for i in range(3):
                lines[i].append(jnp.concatenate([turned[i][0].astype(BF16), turned[i][1].astype(BF16)], axis=1))
        return [jnp.concatenate(line, axis=0) for line in lines]

    def to_image(c, lines):
        for i in range(3):
            backs[c, i] = nn_dot(lines[i], tables[in_y[i]])

    stages = [
        lambda c, _: product(c),
        lambda c, _: to_frequency_y(c),
        lambda c, value: spectra_of(value),
        lambda c, value: to_frequency_z(value),
        lambda c, value: residual_of(c, value),
        lambda c, value: to_depth(value),
        lambda c, value: lines_of(value),
        lambda c, value: to_image(c, value),
    ]
    held_values = [None] * coils
    for step in range(len(stages) + coils - 1):
        for c in range(coils):
            if 0 <= step - c < len(stages):
                held_values[c] = stages[step - c](c, held_values[c])
    for k, (held, i) in enumerate(pieces(out)):
        slab = slabs[count + k]
        for j in range(3):
            cells = slice(j * my, (j + 1) * my)
            real, imag = 0.0, 0.0
            for c in range(coils):
                m_real = maps[c][slab, 0, 0, :, cells].astype(F32)
                m_imag = maps[c][slab, 0, 1, :, cells].astype(F32)
                back = jnp.concatenate([backs[c, j, at, :] for at in places(slab)], axis=0)
                real += m_real * back[:, :my] + m_imag * back[:, my:]
                imag += m_real * back[:, my:] - m_imag * back[:, :my]
            held[i, 0, :, cells] = real.astype(BF16)
            held[i, 1, :, cells] = imag.astype(BF16)


def gradient(where, images, maps, measured, sampling, tables, x):
    _, channels, rows, ny = images[0].shape
    nz = sampling.shape[-1]
    n = len(maps)
    far = (nz // rows - 2) // 2
    whole = lambda a: pl.BlockSpec(a.shape, lambda e, s: (0,) * a.ndim, pipeline_mode=pl.Buffered(1))
    flops = channels * n * 2 * 4 * (nz * ny * ny + nz * nz * ny)
    return pl.pallas_call(
        functools.partial(gradient_kernel, len(images), n),
        grid_spec=pltpu.PrefetchScalarGridSpec(
            num_scalar_prefetch=1,
            grid=(channels // 2,),
            in_specs=[pl.BlockSpec((a.shape[0], 2, rows, ny), lambda e, s: (0, e, 0, 0)) for a in images]
            + [
                pl.BlockSpec((a.shape[0], 1, 2, rows, ny), functools.partial(lambda at, e, s: (0, at, 0, 0, 0), at),
                             pipeline_mode=pl.Buffered(1))
                for a, at in maps
            ]
            + [
                pl.BlockSpec((1, 2, 1, 2, 1, ny, nz), lambda e, s: (0, 0, e, 0, x, 0, 0)),
                pl.BlockSpec((1, 1, ny, nz), lambda e, s: (0, e, 0, 0)),
            ]
            + [whole(tables)],
            out_specs=[pl.BlockSpec((m, 2, rows, ny), lambda e, s: (0, e, 0, 0)) for m in (2, far, far)],
            scratch_shapes=[
                pltpu.VMEM((n, 3, nz, 2 * ny // 3), F32),
                pltpu.VMEM((n, 3, nz, 2 * ny // 3), F32),
            ],
        ),
        out_shape=[jax.ShapeDtypeStruct((m, channels, rows, ny), BF16) for m in (2, far, far)],
        compiler_params=pltpu.CompilerParams(vmem_limit_bytes=52 * 2**20),
        cost_estimate=pl.CostEstimate(flops=flops, bytes_accessed=8 * 2**20, transcendentals=0),
        name="gradient",
    )(where, *images, *[a for a, _ in maps], measured, sampling, tables)


def reordered(value, along_z, along_y):
    n, rows, ny = value.shape
    block = along_z.shape[0]
    flat = nn_dot(value.reshape(n * rows, ny), along_y).astype(BF16)
    out = []
    for start in range(0, n * rows, block):
        size = min(block, n * rows - start)
        out.append(nn_dot(along_z[:size, :size], flat[start : start + size]).astype(BF16))
    return jnp.concatenate(out, axis=0).reshape(n, rows, ny)


def orders(rows, ny, back):
    z, y = order(rows, 2), order(ny, 3)
    along_z = np.kron(np.eye(8, dtype=np.float32), z if back else z.T)
    return jnp.asarray(along_z, BF16), jnp.asarray(y.T if back else y, BF16)


def prepare_image_kernel(image, along_z, along_y, earlier, out):
    width, channels, rows, ny = out.shape
    picked = image[...].reshape((channels, width, rows, ny))
    for x in range(width):
        out[x] = reordered(picked[:, x], along_z[...], along_y[...])


def prepare_image(current_image, earlier):
    _, encodings, _, width, rows, ny = current_image.shape
    vmem = pl.BlockSpec(memory_space=pltpu.VMEM)
    return pl.pallas_call(
        prepare_image_kernel,
        in_specs=[vmem, vmem, vmem, pl.BlockSpec(memory_space=pl.ANY)],
        out_specs=vmem,
        out_shape=jax.ShapeDtypeStruct((width, 2 * encodings, rows, ny), BF16),
        compiler_params=pltpu.CompilerParams(vmem_limit_bytes=16 * 2**20),
        name="prepare_image",
    )(current_image, *orders(rows, ny, False), earlier)


def prepare_maps_kernel(which, maps, along_z, along_y, out):
    count, width, _, rows, ny = out.shape
    value = reordered(maps[:, 0].reshape((count * 2 * width, rows, ny)), along_z[...], along_y[...])
    for pair in range(count):
        for x in range(width):
            for part in range(2):
                out[pair, x, part] = value[(pair * 2 + part) * width + x]


def prepare_maps(which, coil_maps):
    coils, _, width, rows, ny = coil_maps.shape
    devices = coils // 2
    pairs = coil_maps.reshape((devices, 2) + coil_maps.shape[1:])
    matrices = orders(rows, ny, False)
    steps = 1
    return pl.pallas_call(
        prepare_maps_kernel,
        grid_spec=pltpu.PrefetchScalarGridSpec(
            num_scalar_prefetch=1,
            grid=(steps,),
            in_specs=[pl.BlockSpec((devices // steps, 1) + coil_maps.shape[1:], lambda i, t: (i, t[0], 0, 0, 0, 0))]
            + [pl.BlockSpec(m.shape, lambda i, t: (0, 0)) for m in matrices],
            out_specs=pl.BlockSpec((devices // steps, width, 2, rows, ny), lambda i, t: (i, 0, 0, 0, 0)),
        ),
        out_shape=jax.ShapeDtypeStruct((devices, width, 2, rows, ny), BF16),
        compiler_params=pltpu.CompilerParams(vmem_limit_bytes=58 * 2**20),
        name="prepare_maps",
    )(which, pairs, *matrices)


def update_kernel(image, chip, received, along_z, along_y, out):
    for x in range(image.shape[0]):
        value = image[x].astype(F32) - (chip[x] + received[x].astype(F32))
        out[x] = reordered(value.astype(BF16), along_z[...], along_y[...])


def update(image, chip, received):
    vmem = pl.BlockSpec(memory_space=pltpu.VMEM)
    return pl.pallas_call(
        update_kernel,
        in_specs=[vmem] * 5,
        out_specs=vmem,
        out_shape=jax.ShapeDtypeStruct(image.shape, BF16),
        compiler_params=pltpu.CompilerParams(vmem_limit_bytes=16 * 2**20),
        name="update",
    )(image, chip, received, *orders(*image.shape[-2:], True))


def shifted(value, step):
    rows = value.shape[:-1]
    edge = jnp.zeros(rows + (1,), value.dtype)
    if step > 0:
        return jnp.concatenate([value[..., 1:], edge], axis=-1)
    return jnp.concatenate([edge, value[..., :-1]], axis=-1)


def put_strided(ref, first, start, count, stride, value):
    for j in range(value.shape[1] // 128):
        ref[first + j, pl.ds(start, count, stride=stride), :] = value[:, j * 128 : (j + 1) * 128]


def get_lines(ref, chunks, start, count):
    return jnp.concatenate([ref[j, start : start + count, :] for j in chunks], axis=1)


def convolution_kernel(ends, *refs):
    sources, refs = (refs[:2], refs[2:4]), refs[4:]
    w_first, b_first, w_second, b_second, out, stacked, result = refs
    width, channels, rows, ny = sources[0][0].shape
    depth = rows + 4
    group = stacked.shape[1] // depth
    lanes = result.shape[1] // rows
    chunks = ny // 128
    nothing = jnp.zeros((depth, ny), F32)
    for x in range(width):
        for i in range(6 * channels, group):
            put_strided(stacked, x * chunks, i, depth, group, nothing)
        for t, (cells, edges) in enumerate(sources):
            for i in range(channels):
                edge = edges[x, i].astype(F32)
                value = jnp.concatenate([edge[:2], cells[x, i].astype(F32), edge[2:]], axis=0)
                for d in range(3):
                    line = value if d == 1 else shifted(value, d - 1)
                    put_strided(stacked, x * chunks, (d * 2 + t) * channels + i, depth, group, line)
    features = w_first.shape[0] // 2
    taps = w_second.shape[0] // 4
    partial = []
    for pair in range(rows // 2 + 1):
        window = get_lines(stacked, range(width * chunks), 2 * pair * group, 4 * group).astype(BF16)
        hidden = jnp.maximum(nn_dot(w_first[...], window) + b_first[...], 0.0)
        if pair == 0:
            hidden = jnp.concatenate([hidden[:features] * ends[0].astype(F32), hidden[features:]], axis=0)
        if pair == rows // 2:
            hidden = jnp.concatenate([hidden[:features], hidden[features:] * ends[1].astype(F32)], axis=0)
        partial.append(nn_dot(w_second[...], hidden.astype(BF16)))
        if pair > 0:
            for z in range(2):
                both = partial[0][(2 + z) * taps : (3 + z) * taps] + partial[1][z * taps : (z + 1) * taps]
                for x in range(width):
                    total = both[:, x * ny : (x + 1) * ny]
                    line = shifted(total[:lanes], -1) + total[lanes : 2 * lanes] + shifted(total[2 * lanes :], 1)
                    put_strided(result, x * chunks, 2 * pair - 2 + z, lanes, rows, line)
            partial = partial[1:]
    for x in range(width):
        for i in range(channels):
            value = sources[0][0][x, i].astype(F32)
            added = get_lines(result, range(x * chunks, (x + 1) * chunks), i * rows, rows)
            out[0, i // 2, i % 2, x] = (value + added + b_second[i]).astype(BF16)


def convolutions(ends, parts, w_first, b_first, w_second, b_second, shape):
    width, _, rows, ny = parts[0].shape
    group = w_first.shape[1] // 4
    lanes = w_second.shape[0] // 12
    smem = pl.BlockSpec(memory_space=pltpu.SMEM)
    vmem = pl.BlockSpec(memory_space=pltpu.VMEM)
    flops = width * (rows + 2) * ny * (w_first.size + w_second.size)
    return pl.pallas_call(
        convolution_kernel,
        in_specs=[smem] + [vmem] * (len(parts) + 3) + [smem],
        out_specs=vmem,
        out_shape=jax.ShapeDtypeStruct(shape, BF16),
        scratch_shapes=[
            pltpu.VMEM((width * ny // 128, (rows + 4) * group, 128), F32),
            pltpu.VMEM((width * ny // 128, lanes * rows, 128), F32),
        ],
        compiler_params=pltpu.CompilerParams(vmem_limit_bytes=24 * 2**20),
        cost_estimate=pl.CostEstimate(flops=flops, bytes_accessed=2**20, transcendentals=0),
        name="convolutions",
    )(ends, *parts, w_first, b_first, w_second, b_second)


def round_up(value, unit):
    return -(-value // unit) * unit


def convolution_weights(first_weight, first_bias, second_weight):
    q = lax.axis_index(COIL)
    ahead = 2 - 2 * q
    behind = 2 * q

    def tap(weight, index):
        return lax.dynamic_index_in_dim(weight, index, axis=2, keepdims=False)

    feat, channels = first_weight.shape[:2]
    same, of_other, of_own = (tap(first_weight, i) for i in (1, ahead, behind))
    first = jnp.stack([jnp.stack([same, of_other], 1), jnp.stack([of_own, same], 1)], 0)
    first = first.transpose(0, 1, 4, 5, 2, 3).reshape(2 * feat, 3, 6 * channels)
    group = round_up(6 * channels, 16)
    first = jnp.pad(first, ((0, 0), (0, 0), (0, group - 6 * channels))).reshape(2 * feat, 3 * group)
    first = jnp.concatenate([jnp.pad(first, ((0, 0), (0, group))), jnp.pad(first, ((0, 0), (group, 0)))], axis=0)
    bias = jnp.concatenate([first_bias] * 4)[:, None]
    second = jnp.stack([tap(second_weight, 1), tap(second_weight, ahead)], 1)
    second = second.transpose(3, 4, 0, 1, 2).reshape(3, 3, channels, 2 * feat)
    lanes = round_up(channels, 8)
    second = jnp.pad(second, ((0, 0), (0, 0), (0, lanes - channels), (0, 0))).reshape(3, 3 * lanes, 2 * feat)
    none = jnp.zeros_like(second[0])
    line = lambda u: jnp.concatenate([second[u + 2 - r] if 0 <= u + 2 - r <= 2 else none for r in range(4)], axis=0)
    return first, bias, jnp.concatenate([line(0), line(1)], axis=1)


def paired(current_image, coil_maps, measured, sampling, first_weight, first_bias, second_weight, second_bias):
    devices = lax.axis_size(SLAB)
    ring = Ring(devices)
    me, q = lax.axis_index(SLAB), lax.axis_index(COIL)
    _, encodings, _, width, rows, ny = current_image.shape
    nz = rows * devices
    channels = 2 * encodings
    tables = jnp.asarray(np.concatenate([split_tables(ny, 3, True), split_tables(nz, 2, False)]))
    which = q[None].astype(jnp.int32)
    where = jnp.concatenate([ring.slabs(), which])
    swap = [(0, 1), (1, 0)]
    mask = sampling.astype(BF16)
    weights = convolution_weights(first_weight, first_bias, second_weight)
    ends = jnp.stack([me > 0, me < devices - 1]).astype(jnp.int32)

    pairs = prepare_maps(which, coil_maps)
    images = prepare_image(current_image, pairs)
    gathers = [Gather(ring, images[x : x + 1]) for x in range(width)]
    kept = lax.all_to_all(pairs, SLAB, split_axis=0, concat_axis=0, tiled=True)
    for step in range(len(ring.steps())):
        for gather in gathers:
            gather.step(*(weights + (mask,) if step == 1 else (kept,) if step == 2 else ()))
    swapped = lax.ppermute(kept, COIL, swap)
    scatters = []
    for x in range(width):
        scatters.append(Scatter(ring, *gradient(where, gathers[x].pieces(), [(kept, x), (swapped, x)], measured, mask, tables, x)))
    for _ in ring.steps():
        for scatter in scatters:
            scatter.step()
    chip = jnp.stack([scatter.chip() for scatter in scatters])
    updated = update(images, chip[:, 0], lax.ppermute(chip[:, 1].astype(BF16), SLAB, ring.siblings()))
    up = [(i, i + 1) for i in range(devices - 1)]
    down = [(i + 1, i) for i in range(devices - 1)]
    other = lax.ppermute(updated, COIL, swap)
    edges = jnp.concatenate(
        [lax.ppermute(updated[:, :, rows - 2 :], SLAB, up), lax.ppermute(updated[:, :, :2], SLAB, down)], axis=2
    )
    parts = (updated, edges, other, lax.ppermute(edges, COIL, swap))
    return convolutions(ends, parts, *weights, second_bias, current_image.shape)


def with_halo(cells, sides, width):
    for axis, dim in sides:
        count = lax.axis_size(axis)
        ends = count - 1
        head = lax.slice_in_dim(cells, 0, width, axis=dim)
        tail = lax.slice_in_dim(cells, cells.shape[dim] - width, cells.shape[dim], axis=dim)
        cells = jnp.concatenate(
            [
                lax.ppermute(tail, axis, [(i, (i + 1) % count) for i in range(ends)]),
                cells,
                lax.ppermute(head, axis, [((i + 1) % count, i) for i in range(ends)]),
            ],
            axis=dim,
        )
    return cells


def plain_table(length, inverse):
    indices = jnp.arange(length, dtype=jnp.int32)
    wrapped = indices[:, None] * indices[None, :] % length
    angles = wrapped.astype(jnp.float32) * (2.0 * math.pi / length)
    factor = 1.0 / math.sqrt(length)
    cosine = jnp.cos(angles) * factor
    sine_part = jnp.sin(angles) * factor
    phase_sign = 1.0 if inverse else -1.0
    upper_rows = jnp.stack([cosine, phase_sign * sine_part], axis=1)
    lower_rows = jnp.stack([-phase_sign * sine_part, cosine], axis=1)
    return jnp.stack([upper_rows, lower_rows], axis=0).astype(jnp.bfloat16)


def coil_products(maps_part, image_part):
    maps_real = maps_part[:, 0][None, :, None].astype(jnp.float32)
    maps_imaginary = maps_part[:, 1][None, :, None].astype(jnp.float32)
    image_real = image_part[:, :, 0][:, None].astype(jnp.float32)
    image_imaginary = image_part[:, :, 1][:, None].astype(jnp.float32)
    real_part = maps_real * image_real - maps_imaginary * image_imaginary
    imaginary_part = maps_real * image_imaginary + maps_imaginary * image_real
    return jnp.stack([real_part, imaginary_part], axis=3).astype(jnp.bfloat16)


def transform(operand, matrix):
    return jnp.einsum("pcerxzy,ryqk->pceqxzk", operand, matrix, preferred_element_type=jnp.float32)


def combine_coils(maps_part, values):
    maps_real = maps_part[:, 0][None, :, None].astype(jnp.float32)
    maps_imaginary = maps_part[:, 1][None, :, None].astype(jnp.float32)
    real_sum = jnp.sum(maps_real * values[:, :, :, 0] + maps_imaginary * values[:, :, :, 1], axis=1)
    imaginary_sum = jnp.sum(
        maps_real * values[:, :, :, 1] - maps_imaginary * values[:, :, :, 0], axis=1
    )
    return jnp.stack([real_sum, imaginary_sum], axis=2)


def convolve(operand, weights):
    widened = jnp.pad(operand, ((0, 0), (0, 0), (0, 0), (0, 0), (1, 1)))
    return lax.conv_general_dilated(
        widened,
        weights,
        (1, 1, 1),
        "VALID",
        dimension_numbers=("DCNHW", "OIDHW", "DCNHW"),
        preferred_element_type=jnp.float32,
    )


def on_device(
    current_image,
    coil_maps,
    measured,
    sampling,
    first_weight,
    first_bias,
    second_weight,
    second_bias,
):
    depth = current_image.shape[4] * lax.axis_size("slab")
    forward_y = plain_table(current_image.shape[5], False)
    inverse_y = plain_table(current_image.shape[5], True)
    forward_z = plain_table(depth, False)
    inverse_z = plain_table(depth, True)
    sampled = sampling.astype(jnp.float32)[:, None, :, None, None]
    local_maps = lax.all_to_all(coil_maps, "slab", split_axis=0, concat_axis=3, tiled=True)
    row_spectra = transform(
        coil_products(local_maps, lax.all_gather(current_image, "slab", axis=4, tiled=True)),
        forward_y,
    ).astype(jnp.bfloat16)
    residual = (
        sampled
        * (
            jnp.einsum(
                "pcerxzk,rzqj->pceqxkj", row_spectra, forward_z, preferred_element_type=jnp.float32
            )
            - measured.astype(jnp.float32)
        )
    ).astype(jnp.bfloat16)
    depth_back = jnp.einsum(
        "pcerxkj,rjqz->pceqxzk", residual, inverse_z, preferred_element_type=jnp.float32
    ).astype(jnp.bfloat16)
    partial_sum = combine_coils(local_maps, transform(depth_back, inverse_y))
    gradient = lax.psum_scatter(
        partial_sum.astype(jnp.bfloat16), "slab", scatter_dimension=4, tiled=True
    ).astype(jnp.float32)
    updated = (current_image.astype(jnp.float32) - gradient).astype(jnp.bfloat16)
    stacked = updated.reshape((updated.shape[0], 2 * updated.shape[1]) + updated.shape[3:])
    bias_first = first_bias[None, :, None, None, None]
    bordered = with_halo(stacked, (("slab", 3), ("coil", 0)), 1)
    hidden = jax.nn.relu(convolve(bordered, first_weight) + bias_first).astype(jnp.bfloat16)
    bordered_hidden = with_halo(hidden, (("slab", 3), ("coil", 0)), 1)
    second = convolve(bordered_hidden, second_weight)
    refined = stacked.astype(jnp.float32) + second + second_bias[None, :, None, None, None]
    return refined.astype(jnp.bfloat16).reshape(updated.shape)


def fits(shape, devices):
    rows, ny = shape[4:]
    return rows % 16 == 0 and ny % 384 == 0 and 2 * ny == 3 * rows * devices


def solution(mesh):
    devices, phases = mesh.shape[SLAB], mesh.shape[COIL]

    def per_device(*args):
        coils, phase = args[2].shape[1], args[0].shape[0]
        if phases == 2 and coils == 2 and phase == 1 and devices % 4 == 0 and fits(args[0].shape, devices):
            return paired(*args)
        return on_device(*args)

    in_specs = (
        P("coil", None, None, None, "slab", None),
        P(None, None, None, "slab", None),
        P("coil", "slab", None, None, None, None, None),
        P("coil", None, None, None),
        P(),
        P(),
        P(),
        P(),
    )
    out_specs = P("coil", None, None, None, "slab", None)
    return jax.shard_map(
        per_device, mesh=mesh, in_specs=in_specs, out_specs=out_specs, check_vma=False
    )
```

```python
import functools
import math

import jax
import jax.numpy as jnp
import ml_dtypes
import numpy as np
from jax import lax
from jax.experimental import pallas as pl
from jax.experimental.pallas import tpu as pltpu
from jax.sharding import PartitionSpec as P

BF16 = jnp.bfloat16
F32 = jnp.float32
SLAB, COIL = "slab", "coil"


def dft_table(length, inverse):
    indices = np.arange(length, dtype=np.int64)
    wrapped = indices[:, None] * indices[None, :] % length
    angles = wrapped.astype(np.float32) * np.float32(2.0 * math.pi / length)
    factor = np.float32(1.0 / math.sqrt(length))
    cosine = np.cos(angles) * factor
    sine = np.sin(angles) * factor
    sign = np.float32(1.0 if inverse else -1.0)
    upper = np.stack([cosine, sign * sine], axis=1)
    lower = np.stack([-sign * sine, cosine], axis=1)
    return np.stack([upper, lower], axis=0).astype(ml_dtypes.bfloat16)


def split_tables(length, count, left):
    table = dft_table(length, False)
    part = length // count
    out = []
    for s in range(count):
        piece = table[:, s::count, :, :part]
        if left:
            piece = piece.transpose(2, 3, 0, 1)
        out.append(piece.reshape(2 * part, 2 * part))
    return np.stack(out)


def order(length, count):
    taken = np.arange(length).reshape(-1, count).T.reshape(-1)
    return np.eye(length, dtype=np.float32)[:, taken]


class Ring:
    def __init__(self, devices):
        self.devices = devices
        self.chips = devices // 2
        self.half = self.chips // 2
        column = self.chips // 2
        self.order = [2 * i for i in range(column)] + [2 * i + 1 for i in reversed(range(column))]

    def perm(self):
        pairs = []
        for i in range(self.chips):
            for core, step in ((0, 1), (1, -1)):
                pairs.append((2 * self.order[i] + core, 2 * self.order[(i + step) % self.chips] + core))
        return pairs

    def siblings(self):
        return [(i, i ^ 1) for i in range(self.devices)]

    def steps(self):
        return [(step, True) for step in range(1, self.half)] + [(self.half, False)]

    def slabs(self):
        me = lax.axis_index(SLAB)
        chip, core = me // 2, me % 2
        column = self.chips // 2
        row = chip // 2
        place = jnp.where(chip % 2 == 0, row, self.chips - 1 - row)

        def slab(offset, parity):
            at = (place + offset + self.chips) % self.chips
            return 2 * jnp.where(at < column, 2 * at, 2 * (self.chips - 1 - at) + 1) + parity

        def handled(by, sign):
            way = sign * (1 - 2 * by)
            out = []
            for step, both in self.steps():
                out += [slab(way * step, by)] + ([slab(way * step, 1 - by)] if both else [])
            return out

        own = [slab(0, core), slab(0, 1 - core)]
        gathered = own + handled(core, -1) + handled(1 - core, -1)
        summed = own + handled(core, 1) + handled(1 - core, 1)
        return jnp.stack(gathered + summed).astype(jnp.int32)


def after(value, *earlier):
    return lax.optimization_barrier((value,) + earlier)[0]


class Gather:
    def __init__(self, ring, mine):
        self.ring = ring
        self.first = lax.ppermute(mine, SLAB, ring.perm())
        self.own = [mine, lax.ppermute(mine, SLAB, ring.siblings())]
        self.held = None
        self.kept, self.other = [], []

    def step(self, *earlier):
        both = self.ring.steps()[len(self.kept)][1]
        if self.held is None:
            self.held = jnp.concatenate([self.first, lax.ppermute(self.own[1], SLAB, self.ring.perm())], axis=0)
        else:
            held = self.held if both else self.held[:1]
            self.held = lax.ppermute(after(held, *earlier) if earlier else held, SLAB, self.ring.perm())
        self.kept.append(self.held)
        self.other.append(lax.ppermute(self.held, SLAB, self.ring.siblings()))

    def pieces(self):
        return self.own + self.kept + self.other


class Scatter:
    def __init__(self, ring, own, kept, sent):
        self.ring, self.own, self.kept = ring, own, kept
        self.other = lax.ppermute(sent, SLAB, ring.siblings())
        self.held = None
        self.left = list(ring.steps())
        self.end = kept.shape[0]

    def step(self):
        count = 2 if self.left.pop()[1] else 1
        self.end -= count
        total = self.kept[self.end : self.end + count].astype(F32) + self.other[self.end : self.end + count].astype(F32)
        if self.held is not None:
            got = self.held.astype(F32)
            if got.shape[0] < count:
                total = jnp.concatenate([total[:1] + got, total[1:]], axis=0)
            else:
                total = total + got
        self.held = lax.ppermute(total.astype(BF16), SLAB, self.ring.perm())
        return self.held

    def chip(self):
        return self.own.astype(F32) + self.held.astype(F32)


def nt_dot(a, b):
    return lax.dot_general(a, b, (((1,), (1,)), ((), ())), preferred_element_type=F32)


def nn_dot(a, b):
    return lax.dot_general(a, b, (((1,), (0,)), ((), ())), preferred_element_type=F32)


def gradient_kernel(images, coils, slabs, *refs):
    held_images, refs = refs[:images], refs[images:]
    maps, refs = refs[:coils], refs[coils:]
    measured, sampling, tables = refs[:3]
    out, products, backs = refs[3:6], refs[6], refs[7]
    in_y, in_z = [0, 1, 2], [3, 4]
    rows, ny = held_images[0].shape[-2:]
    nz = sampling.shape[-1]
    count, half = nz // rows, rows // 2
    my, mz = ny // 3, nz // 2
    first = slabs[2 * count]
    root = math.sqrt(0.75)

    def pieces(arrays):
        return [(array, i) for array in arrays for i in range(array.shape[0])]

    def places(slab):
        at = pl.multiple_of(slab * half, half)
        return pl.ds(at, half), pl.ds(pl.multiple_of(at + mz, half), half)

    def thirds(b0, b1, b2, sign):
        add = [u + v for u, v in zip(b1, b2)]
        low = [u - 0.5 * v for u, v in zip(b0, add)]
        turn = [(sign * root) * (u - v) for u, v in zip(b1, b2)]
        return (
            (b0[0] + add[0], b0[1] + add[1]),
            (low[0] - turn[1], low[1] + turn[0]),
            (low[0] + turn[1], low[1] - turn[0]),
        )

    def product(c):
        for k, (held, i) in enumerate(pieces(held_images)):
            slab = slabs[k]
            real = held[i, 0].astype(F32)
            imag = held[i, 1].astype(F32)
            m_real = maps[c][slab, 0, 0].astype(F32)
            m_imag = maps[c][slab, 0, 1].astype(F32)
            p_real = m_real * real - m_imag * imag
            p_imag = m_real * imag + m_imag * real
            for parity, at in enumerate(places(slab)):
                lines = slice(parity * half, (parity + 1) * half)
                for j in range(3):
                    cells = slice(j * my, (j + 1) * my)
                    products[c, j, at, :my] = p_real[lines, cells]
                    products[c, j, at, my:] = p_imag[lines, cells]

    def to_frequency_y(c):
        return [nt_dot(tables[in_y[j]], products[c, j].astype(BF16)) for j in range(3)]

    def spectra_of(parts):
        parts = thirds(*[(part[:my], part[my:]) for part in parts], -1.0)
        return [jnp.concatenate([part[q].astype(BF16) for part in parts], axis=0) for q in range(2)]

    def to_frequency_z(spectra):
        halves = []
        for j in range(2):
            cells = slice(j * mz, (j + 1) * mz)
            halves.append(nn_dot(jnp.concatenate([spectra[0][:, cells], spectra[1][:, cells]], axis=1), tables[in_z[j]]))
        return halves

    def residual_of(c, halves):
        coil = first if c == 0 else 1 - first
        mask = sampling[0, 0].astype(F32)
        sums, differences = [], []
        for q in range(2):
            cells = slice(q * mz, (q + 1) * mz)
            seen = measured[0, coil, 0, q, 0].astype(F32)
            low = mask[:, :mz] * (halves[0][:, cells] + halves[1][:, cells] - seen[:, :mz])
            high = mask[:, mz:] * (halves[0][:, cells] - halves[1][:, cells] - seen[:, mz:])
            sums.append((low + high).astype(BF16))
            differences.append((low - high).astype(BF16))
        return jnp.concatenate(sums, axis=1), jnp.concatenate(differences, axis=1)

    def to_depth(folds):
        return [nt_dot(tables[in_z[j]], folds[j]) for j in range(2)]

    def lines_of(depths):
        lines = [[], [], []]
        for j in range(2):
            cut = lambda q, i: depths[j][q * mz : (q + 1) * mz, i * my : (i + 1) * my]
            turned = thirds(*[(cut(0, i), cut(1, i)) for i in range(3)], 1.0)
            for i in range(3):
                lines[i].append(jnp.concatenate([turned[i][0].astype(BF16), turned[i][1].astype(BF16)], axis=1))
        return [jnp.concatenate(line, axis=0) for line in lines]

    def to_image(c, lines):
        for i in range(3):
            backs[c, i] = nn_dot(lines[i], tables[in_y[i]])

    stages = [
        lambda c, _: product(c),
        lambda c, _: to_frequency_y(c),
        lambda c, value: spectra_of(value),
        lambda c, value: to_frequency_z(value),
        lambda c, value: residual_of(c, value),
        lambda c, value: to_depth(value),
        lambda c, value: lines_of(value),
        lambda c, value: to_image(c, value),
    ]
    held_values = [None] * coils
    for step in range(len(stages) + coils - 1):
        for c in range(coils):
            if 0 <= step - c < len(stages):
                held_values[c] = stages[step - c](c, held_values[c])
    for k, (held, i) in enumerate(pieces(out)):
        slab = slabs[count + k]
        for j in range(3):
            cells = slice(j * my, (j + 1) * my)
            real, imag = 0.0, 0.0
            for c in range(coils):
                m_real = maps[c][slab, 0, 0, :, cells].astype(F32)
                m_imag = maps[c][slab, 0, 1, :, cells].astype(F32)
                back = jnp.concatenate([backs[c, j, at, :] for at in places(slab)], axis=0)
                real += m_real * back[:, :my] + m_imag * back[:, my:]
                imag += m_real * back[:, my:] - m_imag * back[:, :my]
            held[i, 0, :, cells] = real.astype(BF16)
            held[i, 1, :, cells] = imag.astype(BF16)


def gradient(where, images, maps, measured, sampling, tables, x):
    _, channels, rows, ny = images[0].shape
    nz = sampling.shape[-1]
    n = len(maps)
    far = (nz // rows - 2) // 2
    whole = lambda a: pl.BlockSpec(a.shape, lambda e, s: (0,) * a.ndim, pipeline_mode=pl.Buffered(1))
    flops = channels * n * 2 * 4 * (nz * ny * ny + nz * nz * ny)
    return pl.pallas_call(
        functools.partial(gradient_kernel, len(images), n),
        grid_spec=pltpu.PrefetchScalarGridSpec(
            num_scalar_prefetch=1,
            grid=(channels // 2,),
            in_specs=[pl.BlockSpec((a.shape[0], 2, rows, ny), lambda e, s: (0, e, 0, 0)) for a in images]
            + [
                pl.BlockSpec((a.shape[0], 1, 2, rows, ny), functools.partial(lambda at, e, s: (0, at, 0, 0, 0), at),
                             pipeline_mode=pl.Buffered(1))
                for a, at in maps
            ]
            + [
                pl.BlockSpec((1, 2, 1, 2, 1, ny, nz), lambda e, s: (0, 0, e, 0, x, 0, 0)),
                pl.BlockSpec((1, 1, ny, nz), lambda e, s: (0, e, 0, 0)),
            ]
            + [whole(tables)],
            out_specs=[pl.BlockSpec((m, 2, rows, ny), lambda e, s: (0, e, 0, 0)) for m in (2, far, far)],
            scratch_shapes=[
                pltpu.VMEM((n, 3, nz, 2 * ny // 3), F32),
                pltpu.VMEM((n, 3, nz, 2 * ny // 3), F32),
            ],
        ),
        out_shape=[jax.ShapeDtypeStruct((m, channels, rows, ny), BF16) for m in (2, far, far)],
        compiler_params=pltpu.CompilerParams(vmem_limit_bytes=49 * 2**20),
        cost_estimate=pl.CostEstimate(flops=flops, bytes_accessed=8 * 2**20, transcendentals=0),
        name="gradient",
    )(where, *images, *[a for a, _ in maps], measured, sampling, tables)


def reordered(value, along_z, along_y):
    n, rows, ny = value.shape
    block = along_z.shape[0]
    flat = nn_dot(value.reshape(n * rows, ny), along_y).astype(BF16)
    out = []
    for start in range(0, n * rows, block):
        size = min(block, n * rows - start)
        out.append(nn_dot(along_z[:size, :size], flat[start : start + size]).astype(BF16))
    return jnp.concatenate(out, axis=0).reshape(n, rows, ny)


def orders(rows, ny, back):
    z, y = order(rows, 2), order(ny, 3)
    along_z = np.kron(np.eye(8, dtype=np.float32), z if back else z.T)
    return jnp.asarray(along_z, BF16), jnp.asarray(y.T if back else y, BF16)


def prepare_image_kernel(image, along_z, along_y, earlier, out):
    width, channels, rows, ny = out.shape
    picked = image[...].reshape((channels, width, rows, ny))
    for x in range(width):
        out[x] = reordered(picked[:, x], along_z[...], along_y[...])


def prepare_image(current_image, earlier):
    _, encodings, _, width, rows, ny = current_image.shape
    vmem = pl.BlockSpec(memory_space=pltpu.VMEM)
    return pl.pallas_call(
        prepare_image_kernel,
        in_specs=[vmem, vmem, vmem, pl.BlockSpec(memory_space=pl.ANY)],
        out_specs=vmem,
        out_shape=jax.ShapeDtypeStruct((width, 2 * encodings, rows, ny), BF16),
        compiler_params=pltpu.CompilerParams(vmem_limit_bytes=16 * 2**20),
        name="prepare_image",
    )(current_image, *orders(rows, ny, False), earlier)


def prepare_maps_kernel(which, maps, along_z, along_y, out):
    count, width, _, rows, ny = out.shape
    value = reordered(maps[:, 0].reshape((count * 2 * width, rows, ny)), along_z[...], along_y[...])
    for pair in range(count):
        for x in range(width):
            for part in range(2):
                out[pair, x, part] = value[(pair * 2 + part) * width + x]


def prepare_maps(which, coil_maps):
    coils, _, width, rows, ny = coil_maps.shape
    devices = coils // 2
    pairs = coil_maps.reshape((devices, 2) + coil_maps.shape[1:])
    matrices = orders(rows, ny, False)
    steps = 1
    return pl.pallas_call(
        prepare_maps_kernel,
        grid_spec=pltpu.PrefetchScalarGridSpec(
            num_scalar_prefetch=1,
            grid=(steps,),
            in_specs=[pl.BlockSpec((devices // steps, 1) + coil_maps.shape[1:], lambda i, t: (i, t[0], 0, 0, 0, 0))]
            + [pl.BlockSpec(m.shape, lambda i, t: (0, 0)) for m in matrices],
            out_specs=pl.BlockSpec((devices // steps, width, 2, rows, ny), lambda i, t: (i, 0, 0, 0, 0)),
        ),
        out_shape=jax.ShapeDtypeStruct((devices, width, 2, rows, ny), BF16),
        compiler_params=pltpu.CompilerParams(vmem_limit_bytes=58 * 2**20),
        name="prepare_maps",
    )(which, pairs, *matrices)


def update_kernel(image, chip, received, along_z, along_y, out):
    for x in range(image.shape[0]):
        value = image[x].astype(F32) - (chip[x] + received[x].astype(F32))
        out[x] = reordered(value.astype(BF16), along_z[...], along_y[...])


def update(image, chip, received):
    vmem = pl.BlockSpec(memory_space=pltpu.VMEM)
    return pl.pallas_call(
        update_kernel,
        in_specs=[vmem] * 5,
        out_specs=vmem,
        out_shape=jax.ShapeDtypeStruct(image.shape, BF16),
        compiler_params=pltpu.CompilerParams(vmem_limit_bytes=16 * 2**20),
        name="update",
    )(image, chip, received, *orders(*image.shape[-2:], True))


def shifted(value, step):
    rows = value.shape[:-1]
    edge = jnp.zeros(rows + (1,), value.dtype)
    if step > 0:
        return jnp.concatenate([value[..., 1:], edge], axis=-1)
    return jnp.concatenate([edge, value[..., :-1]], axis=-1)


def put_strided(ref, first, start, count, stride, value):
    for j in range(value.shape[1] // 128):
        ref[first + j, pl.ds(start, count, stride=stride), :] = value[:, j * 128 : (j + 1) * 128]


def get_lines(ref, chunks, start, count):
    return jnp.concatenate([ref[j, start : start + count, :] for j in chunks], axis=1)


def convolution_kernel(ends, *refs):
    sources, refs = (refs[:2], refs[2:4]), refs[4:]
    w_first, b_first, w_second, b_second, out, stacked, result = refs
    width, channels, rows, ny = sources[0][0].shape
    depth = rows + 4
    group = stacked.shape[1] // depth
    lanes = result.shape[1] // rows
    chunks = ny // 128
    nothing = jnp.zeros((depth, ny), F32)
    for x in range(width):
        for i in range(6 * channels, group):
            put_strided(stacked, x * chunks, i, depth, group, nothing)
        for t, (cells, edges) in enumerate(sources):
            for i in range(channels):
                edge = edges[x, i].astype(F32)
                value = jnp.concatenate([edge[:2], cells[x, i].astype(F32), edge[2:]], axis=0)
                for d in range(3):
                    line = value if d == 1 else shifted(value, d - 1)
                    put_strided(stacked, x * chunks, (d * 2 + t) * channels + i, depth, group, line)
    features = w_first.shape[0] // 2
    taps = w_second.shape[0] // 4
    partial = []
    for pair in range(rows // 2 + 1):
        window = get_lines(stacked, range(width * chunks), 2 * pair * group, 4 * group).astype(BF16)
        hidden = jnp.maximum(nn_dot(w_first[...], window) + b_first[...], 0.0)
        if pair == 0:
            hidden = jnp.concatenate([hidden[:features] * ends[0].astype(F32), hidden[features:]], axis=0)
        if pair == rows // 2:
            hidden = jnp.concatenate([hidden[:features], hidden[features:] * ends[1].astype(F32)], axis=0)
        partial.append(nn_dot(w_second[...], hidden.astype(BF16)))
        if pair > 0:
            for z in range(2):
                both = partial[0][(2 + z) * taps : (3 + z) * taps] + partial[1][z * taps : (z + 1) * taps]
                for x in range(width):
                    total = both[:, x * ny : (x + 1) * ny]
                    line = shifted(total[:lanes], -1) + total[lanes : 2 * lanes] + shifted(total[2 * lanes :], 1)
                    put_strided(result, x * chunks, 2 * pair - 2 + z, lanes, rows, line)
            partial = partial[1:]
    for x in range(width):
        for i in range(channels):
            value = sources[0][0][x, i].astype(F32)
            added = get_lines(result, range(x * chunks, (x + 1) * chunks), i * rows, rows)
            out[0, i // 2, i % 2, x] = (value + added + b_second[i]).astype(BF16)


def convolutions(ends, parts, w_first, b_first, w_second, b_second, shape):
    width, _, rows, ny = parts[0].shape
    group = w_first.shape[1] // 4
    lanes = w_second.shape[0] // 12
    smem = pl.BlockSpec(memory_space=pltpu.SMEM)
    vmem = pl.BlockSpec(memory_space=pltpu.VMEM)
    flops = width * (rows + 2) * ny * (w_first.size + w_second.size)
    return pl.pallas_call(
        convolution_kernel,
        in_specs=[smem] + [vmem] * (len(parts) + 3) + [smem],
        out_specs=vmem,
        out_shape=jax.ShapeDtypeStruct(shape, BF16),
        scratch_shapes=[
            pltpu.VMEM((width * ny // 128, (rows + 4) * group, 128), F32),
            pltpu.VMEM((width * ny // 128, lanes * rows, 128), F32),
        ],
        compiler_params=pltpu.CompilerParams(vmem_limit_bytes=24 * 2**20),
        cost_estimate=pl.CostEstimate(flops=flops, bytes_accessed=2**20, transcendentals=0),
        name="convolutions",
    )(ends, *parts, w_first, b_first, w_second, b_second)


def round_up(value, unit):
    return -(-value // unit) * unit


def convolution_weights(first_weight, first_bias, second_weight):
    q = lax.axis_index(COIL)
    ahead = 2 - 2 * q
    behind = 2 * q

    def tap(weight, index):
        return lax.dynamic_index_in_dim(weight, index, axis=2, keepdims=False)

    feat, channels = first_weight.shape[:2]
    same, of_other, of_own = (tap(first_weight, i) for i in (1, ahead, behind))
    first = jnp.stack([jnp.stack([same, of_other], 1), jnp.stack([of_own, same], 1)], 0)
    first = first.transpose(0, 1, 4, 5, 2, 3).reshape(2 * feat, 3, 6 * channels)
    group = round_up(6 * channels, 16)
    first = jnp.pad(first, ((0, 0), (0, 0), (0, group - 6 * channels))).reshape(2 * feat, 3 * group)
    first = jnp.concatenate([jnp.pad(first, ((0, 0), (0, group))), jnp.pad(first, ((0, 0), (group, 0)))], axis=0)
    bias = jnp.concatenate([first_bias] * 4)[:, None]
    second = jnp.stack([tap(second_weight, 1), tap(second_weight, ahead)], 1)
    second = second.transpose(3, 4, 0, 1, 2).reshape(3, 3, channels, 2 * feat)
    lanes = round_up(channels, 8)
    second = jnp.pad(second, ((0, 0), (0, 0), (0, lanes - channels), (0, 0))).reshape(3, 3 * lanes, 2 * feat)
    none = jnp.zeros_like(second[0])
    line = lambda u: jnp.concatenate([second[u + 2 - r] if 0 <= u + 2 - r <= 2 else none for r in range(4)], axis=0)
    return first, bias, jnp.concatenate([line(0), line(1)], axis=1)


def paired(current_image, coil_maps, measured, sampling, first_weight, first_bias, second_weight, second_bias):
    devices = lax.axis_size(SLAB)
    ring = Ring(devices)
    me, q = lax.axis_index(SLAB), lax.axis_index(COIL)
    _, encodings, _, width, rows, ny = current_image.shape
    nz = rows * devices
    channels = 2 * encodings
    tables = jnp.asarray(np.concatenate([split_tables(ny, 3, True), split_tables(nz, 2, False)]))
    which = q[None].astype(jnp.int32)
    where = jnp.concatenate([ring.slabs(), which])
    swap = [(0, 1), (1, 0)]
    mask = sampling.astype(BF16)
    weights = convolution_weights(first_weight, first_bias, second_weight)
    ends = jnp.stack([me > 0, me < devices - 1]).astype(jnp.int32)

    pairs = prepare_maps(which, coil_maps)
    images = prepare_image(current_image, pairs)
    gathers = [Gather(ring, images[x : x + 1]) for x in range(width)]
    kept = lax.all_to_all(pairs, SLAB, split_axis=0, concat_axis=0, tiled=True)
    for step in range(len(ring.steps())):
        for gather in gathers:
            gather.step(*(weights + (mask,) if step == 1 else (kept,) if step == 2 else ()))
    swapped = lax.ppermute(kept, COIL, swap)
    scatters = []
    for x in range(width):
        scatters.append(Scatter(ring, *gradient(where, gathers[x].pieces(), [(kept, x), (swapped, x)], measured, mask, tables, x)))
    for _ in ring.steps():
        for scatter in scatters:
            scatter.step()
    chip = jnp.stack([scatter.chip() for scatter in scatters])
    updated = update(images, chip[:, 0], lax.ppermute(chip[:, 1].astype(BF16), SLAB, ring.siblings()))
    up = [(i, i + 1) for i in range(devices - 1)]
    down = [(i + 1, i) for i in range(devices - 1)]
    other = lax.ppermute(updated, COIL, swap)
    edges = jnp.concatenate(
        [lax.ppermute(updated[:, :, rows - 2 :], SLAB, up), lax.ppermute(updated[:, :, :2], SLAB, down)], axis=2
    )
    parts = (updated, edges, other, lax.ppermute(edges, COIL, swap))
    return convolutions(ends, parts, *weights, second_bias, current_image.shape)


def with_halo(cells, sides, width):
    for axis, dim in sides:
        count = lax.axis_size(axis)
        ends = count - 1
        head = lax.slice_in_dim(cells, 0, width, axis=dim)
        tail = lax.slice_in_dim(cells, cells.shape[dim] - width, cells.shape[dim], axis=dim)
        cells = jnp.concatenate(
            [
                lax.ppermute(tail, axis, [(i, (i + 1) % count) for i in range(ends)]),
                cells,
                lax.ppermute(head, axis, [((i + 1) % count, i) for i in range(ends)]),
            ],
            axis=dim,
        )
    return cells


def plain_table(length, inverse):
    indices = jnp.arange(length, dtype=jnp.int32)
    wrapped = indices[:, None] * indices[None, :] % length
    angles = wrapped.astype(jnp.float32) * (2.0 * math.pi / length)
    factor = 1.0 / math.sqrt(length)
    cosine = jnp.cos(angles) * factor
    sine_part = jnp.sin(angles) * factor
    phase_sign = 1.0 if inverse else -1.0
    upper_rows = jnp.stack([cosine, phase_sign * sine_part], axis=1)
    lower_rows = jnp.stack([-phase_sign * sine_part, cosine], axis=1)
    return jnp.stack([upper_rows, lower_rows], axis=0).astype(jnp.bfloat16)


def coil_products(maps_part, image_part):
    maps_real = maps_part[:, 0][None, :, None].astype(jnp.float32)
    maps_imaginary = maps_part[:, 1][None, :, None].astype(jnp.float32)
    image_real = image_part[:, :, 0][:, None].astype(jnp.float32)
    image_imaginary = image_part[:, :, 1][:, None].astype(jnp.float32)
    real_part = maps_real * image_real - maps_imaginary * image_imaginary
    imaginary_part = maps_real * image_imaginary + maps_imaginary * image_real
    return jnp.stack([real_part, imaginary_part], axis=3).astype(jnp.bfloat16)


def transform(operand, matrix):
    return jnp.einsum("pcerxzy,ryqk->pceqxzk", operand, matrix, preferred_element_type=jnp.float32)


def combine_coils(maps_part, values):
    maps_real = maps_part[:, 0][None, :, None].astype(jnp.float32)
    maps_imaginary = maps_part[:, 1][None, :, None].astype(jnp.float32)
    real_sum = jnp.sum(maps_real * values[:, :, :, 0] + maps_imaginary * values[:, :, :, 1], axis=1)
    imaginary_sum = jnp.sum(
        maps_real * values[:, :, :, 1] - maps_imaginary * values[:, :, :, 0], axis=1
    )
    return jnp.stack([real_sum, imaginary_sum], axis=2)


def convolve(operand, weights):
    widened = jnp.pad(operand, ((0, 0), (0, 0), (0, 0), (0, 0), (1, 1)))
    return lax.conv_general_dilated(
        widened,
        weights,
        (1, 1, 1),
        "VALID",
        dimension_numbers=("DCNHW", "OIDHW", "DCNHW"),
        preferred_element_type=jnp.float32,
    )


def on_device(
    current_image,
    coil_maps,
    measured,
    sampling,
    first_weight,
    first_bias,
    second_weight,
    second_bias,
):
    depth = current_image.shape[4] * lax.axis_size("slab")
    forward_y = plain_table(current_image.shape[5], False)
    inverse_y = plain_table(current_image.shape[5], True)
    forward_z = plain_table(depth, False)
    inverse_z = plain_table(depth, True)
    sampled = sampling.astype(jnp.float32)[:, None, :, None, None]
    local_maps = lax.all_to_all(coil_maps, "slab", split_axis=0, concat_axis=3, tiled=True)
    row_spectra = transform(
        coil_products(local_maps, lax.all_gather(current_image, "slab", axis=4, tiled=True)),
        forward_y,
    ).astype(jnp.bfloat16)
    residual = (
        sampled
        * (
            jnp.einsum(
                "pcerxzk,rzqj->pceqxkj", row_spectra, forward_z, preferred_element_type=jnp.float32
            )
            - measured.astype(jnp.float32)
        )
    ).astype(jnp.bfloat16)
    depth_back = jnp.einsum(
        "pcerxkj,rjqz->pceqxzk", residual, inverse_z, preferred_element_type=jnp.float32
    ).astype(jnp.bfloat16)
    partial_sum = combine_coils(local_maps, transform(depth_back, inverse_y))
    gradient = lax.psum_scatter(
        partial_sum.astype(jnp.bfloat16), "slab", scatter_dimension=4, tiled=True
    ).astype(jnp.float32)
    updated = (current_image.astype(jnp.float32) - gradient).astype(jnp.bfloat16)
    stacked = updated.reshape((updated.shape[0], 2 * updated.shape[1]) + updated.shape[3:])
    bias_first = first_bias[None, :, None, None, None]
    bordered = with_halo(stacked, (("slab", 3), ("coil", 0)), 1)
    hidden = jax.nn.relu(convolve(bordered, first_weight) + bias_first).astype(jnp.bfloat16)
    bordered_hidden = with_halo(hidden, (("slab", 3), ("coil", 0)), 1)
    second = convolve(bordered_hidden, second_weight)
    refined = stacked.astype(jnp.float32) + second + second_bias[None, :, None, None, None]
    return refined.astype(jnp.bfloat16).reshape(updated.shape)


def fits(shape, devices):
    rows, ny = shape[4:]
    return rows % 16 == 0 and ny % 384 == 0 and 2 * ny == 3 * rows * devices


def solution(mesh):
    devices, phases = mesh.shape[SLAB], mesh.shape[COIL]

    def per_device(*args):
        coils, phase = args[2].shape[1], args[0].shape[0]
        if phases == 2 and coils == 2 and phase == 1 and devices % 4 == 0 and fits(args[0].shape, devices):
            return paired(*args)
        return on_device(*args)

    in_specs = (
        P("coil", None, None, None, "slab", None),
        P(None, None, None, "slab", None),
        P("coil", "slab", None, None, None, None, None),
        P("coil", None, None, None),
        P(),
        P(),
        P(),
        P(),
    )
    out_specs = P("coil", None, None, None, "slab", None)
    return jax.shard_map(
        per_device, mesh=mesh, in_specs=in_specs, out_specs=out_specs, check_vma=False
    )
```
